32 devices in a mesh: grp: 4 (over y, core), req: 8 (over z, x).
Axes of the slice: x: 2, y: 2, z: 4, core: 2. Of those that a mesh axis runs over, the one named last changes fastest.
Arguments:
- tokens: bfloat16 [4096, 1024], P(('grp', 'req')), may hold values from -6 to 6
- attn_gain: float32 [1024], replicated, may hold values from 0.1 to 1.9
- w_query: bfloat16 [1024, 1024], replicated, may hold values from -0.0234375 to 0.0234375
- w_key: bfloat16 [1024, 1024], replicated, may hold values from -0.1875 to 0.1875
- w_value: bfloat16 [1024, 1024], replicated, may hold values from -0.1875 to 0.1875
- w_attn_out: bfloat16 [1024, 1024], replicated, may hold values from -0.1875 to 0.1875
- rel_bias: float32 [32, 16], replicated, may hold values from -4 to 4
- prefix_cache: bfloat16 [8, 512, 2048], P('grp', 'req'), may hold values from -6 to 6
- lengths: int32 [4, 16], P('grp'), may hold values from 1 to 128, 1024 in all within a row
- prefix_map: int32 [4, 16], P('grp'), may hold values from 0 to 1
- mlp_gain: float32 [1024], replicated, may hold values from 0.1 to 1.9
- w_in: bfloat16 [4096, 1024], P('grp'), may hold values from -0.1875 to 0.1875
- w_out: bfloat16 [4096, 1024], P('grp'), may hold values from -0.09375 to 0.09375
Outputs:
- layer_out: bfloat16 [4096, 1024], P(('grp', 'req'))
The draws below stay inside these ranges and needn't reach their ends.
Inputs may be any that keep to these rules, and one draw needn't show every extreme that they name: In each group the lengths sum to 1024 and the longest is exactly 128.
All inputs are finite; a program needn't handle non-finite values.
Results may differ from the reference program's by a relative error of at most 0.017.
Values may be sent and summed in bfloat16 or wider, within the bound.
A program may use at most 128 MiB of HBM per device.

```python
import math
import jax
import jax.numpy as jnp
import numpy as np
from jax import lax

D = 1024
H = 16
DK = 64
FF = 4096
BUCKETS = 32
PLEN = 512
PREF_GRP = 2
TOK_DEV = 128
TOK_GRP = 1024
TOKENS = 4096
REQ_GRP = 16
PREFIXES = 8
N_GRP = 4
N_REQ = 8


def shared_pattern(key):
    base = jax.random.fold_in(key, 7301)
    signs = (2 * jax.random.randint(jax.random.fold_in(base, 1), (D,), 0, 2) - 1).astype(jnp.float32)
    features = jax.random.permutation(jax.random.fold_in(base, 2), D)[:2].astype(jnp.int32)
    return (signs, features)


def draw_w_query(key, part):
    signs, features = shared_pattern(key)
    spread = 1.0 / math.sqrt(D * DK)
    limit = 6.0 * spread
    own = jax.random.fold_in(key, 11)
    drawn = jax.random.normal(own, (D, D), jnp.float32) * spread
    drawn = jnp.clip(drawn, -limit, limit)
    row_ids = jnp.arange(D, dtype=jnp.int32)
    marked = jnp.any(row_ids[:, None] == features[None, :], axis=1)
    return jnp.where(marked[:, None], limit * signs[None, :], drawn).astype(jnp.bfloat16)


def draw_tokens(key, part):
    signs, features = shared_pattern(key)
    own = jax.random.fold_in(key, 23)
    drawn = jnp.clip(jax.random.normal(own, (TOKENS, D), jnp.float32), -6.0, 6.0)
    quiet = jnp.clip(jax.random.normal(jax.random.fold_in(key, 31), (TOKENS, D), jnp.float32), -4.0, 4.0)
    columns = jnp.arange(D, dtype=jnp.int32)
    feature_col = (columns == features[0]) | (columns == features[1])
    drawn = jnp.where(feature_col[None, :], 0.1 * drawn, drawn)
    blocks = TOKENS // TOK_DEV
    spot = jax.random.randint(jax.random.fold_in(key, 29), (blocks,), 0, TOK_DEV)
    row_ids = jnp.arange(TOKENS, dtype=jnp.int32)
    block_of = row_ids // TOK_DEV
    is_spike = row_ids - block_of * TOK_DEV == spot[block_of]
    noise_level = jnp.array([0.05, 0.2, 0.35], jnp.float32)[block_of % 3]
    spike_rows = jnp.where(feature_col[None, :], 6.0, quiet * noise_level[:, None])
    return jnp.where(is_spike[:, None], spike_rows, drawn).astype(jnp.bfloat16)


def draw_prefix_cache(key, part):
    signs, features = shared_pattern(key)
    own = jax.random.fold_in(key, 41)
    drawn = jnp.clip(jax.random.normal(own, (PREFIXES, PLEN, 2 * D), jnp.float32), -6.0, 6.0)
    reach = max(PLEN - 128, PLEN // 2)
    first = jax.random.randint(jax.random.fold_in(key, 43), (PREFIXES,), 0, reach)
    second = (first + 1 + jax.random.randint(jax.random.fold_in(key, 47), (PREFIXES,), 0, reach - 1)) % reach
    positions = jnp.arange(PLEN, dtype=jnp.int32)
    columns = jnp.arange(2 * D, dtype=jnp.int32)
    key_col = columns < D
    dip = (columns % DK == 0) & key_col
    sign_full = jnp.concatenate([signs, jnp.zeros((D,), jnp.float32)])
    first_vals = 6.0 * sign_full
    second_vals = jnp.where(dip, 4.25, 6.0) * sign_full
    at_first = (positions[None, :] == first[:, None])[:, :, None] & key_col[None, None, :]
    at_second = (positions[None, :] == second[:, None])[:, :, None] & key_col[None, None, :]
    out = jnp.where(at_first, first_vals[None, None, :], drawn)
    return jnp.where(at_second, second_vals[None, None, :], out).astype(jnp.bfloat16)


def touch_ends(values, own_key, smallest, largest):
    dims = values.shape
    index_at = [jax.random.randint(jax.random.fold_in(own_key, axis), (), 0, dims[axis]) for axis in range(len(dims))]
    values = values.at[tuple(index_at)].set(smallest)
    longest = dims.index(max(dims))
    index_at[longest] = (index_at[longest] + 1) % dims[longest]
    return values.at[tuple(index_at)].set(largest)


def block_scale(rng, dims, split, low, high):
    level = 1.0
    for axis_at, blocks in split:
        draws = jax.random.uniform(jax.random.fold_in(jax.random.fold_in(rng, 6), axis_at), (blocks,), jnp.float32, low / len(split), high / len(split))
        level = level * jnp.repeat(jnp.exp(draws), dims[axis_at] // blocks).reshape((-1,) + (1,) * (len(dims) - 1 - axis_at))
    return level


def length_profile(number_of, total, bound, skew):
    weights = [(1 << 20) // math.isqrt(standing ** skew) + 1 for standing in range(2, number_of + 1)]
    spare, counts = total - bound - (number_of - 1), [1] * (number_of - 1)
    while spare > 0:
        movable = [i for i in range(number_of - 1) if counts[i] < bound]
        pool, remaining = sum([weights[i] for i in movable]), spare
        for i in movable:
            extra = min(bound - counts[i], max(1, remaining * weights[i] // pool), spare)
            counts[i] = counts[i] + extra
            spare = spare - extra
    return np.array([bound] + counts)


def uneven(stream_key, number_of, total, most, slope):
    if number_of == 2:
        one = jax.random.randint(stream_key, (), max(1, total - most), min(most, total - 1) + 1)
        return jnp.stack([one, total - one])
    sizes = jnp.asarray(length_profile(number_of, total, most, slope), jnp.int32)
    twos = (number_of - 1) // 2
    giver, taker = sizes[1:1 + 2 * twos:2], sizes[2:2 + 2 * twos:2]
    room = jnp.minimum(giver - 1, most - taker)
    shifted = jax.random.randint(jax.random.fold_in(stream_key, 1), (twos,), 0, 1 << 20) % (room + 1)
    sizes = sizes.at[1:1 + 2 * twos:2].set(giver - shifted).at[2:2 + 2 * twos:2].set(taker + shifted)
    return sizes[jax.random.permutation(jax.random.fold_in(stream_key, 2), number_of)]


def centred(key, shape, scale, most, shards=(), kind=jnp.bfloat16):
    entries = jax.random.normal(key, shape, jnp.float32) * scale
    if len(shards) > 0:
        entries = block_scale(key, shape, shards, -0.22, 0.18) * entries
    return jnp.clip(entries, min=-most, max=most).astype(kind)


def setup_inputs(seed: int = 0) -> dict:
    splits = jax.random.split(jax.random.key(seed), 14)
    return {
        "tokens": draw_tokens(jax.random.fold_in(splits[13], 71), 0),
        "attn_gain": jnp.clip(1.0 + 0.18 * jax.random.normal(splits[1], (D,), jnp.float32), 0.1, 1.9),
        "w_query": draw_w_query(jax.random.fold_in(splits[13], 71), 0),
        "w_key": centred(splits[3], (D, D), D ** -0.5, 0.1875),
        "w_value": centred(splits[4], (D, D), D ** -0.5, 0.1875),
        "w_attn_out": centred(splits[5], (D, D), D ** -0.5, 0.1875),
        "rel_bias": centred(splits[6], (BUCKETS, H), 1.0, 4.0, (), jnp.float32),
        "prefix_cache": draw_prefix_cache(jax.random.fold_in(splits[13], 71), 0),
        "lengths": jax.vmap(lambda own: uneven(own, REQ_GRP, TOK_GRP, TOK_DEV, 2))(jax.random.split(splits[8], N_GRP)).reshape((N_GRP, REQ_GRP)).astype(jnp.int32),
        "prefix_map": touch_ends(jax.random.randint(splits[9], (N_GRP, REQ_GRP), 0, PREF_GRP), jax.random.fold_in(splits[9], 1), 0, PREF_GRP - 1).astype(jnp.int32),
        "mlp_gain": jnp.clip(1.0 + 0.18 * jax.random.normal(splits[10], (D,), jnp.float32), 0.1, 1.9),
        "w_in": centred(splits[11], (FF, D), D ** -0.5, 0.1875, ((0, 4),)),
        "w_out": centred(splits[12], (FF, D), FF ** -0.5, 0.09375, ((0, 4),)),
    }


epsilon = 1e-06
far_marks = (12, 16, 23, 32, 46, 64, 91)
masked_score = -1e+30

def bucket_of(relative):
    distance = jnp.abs(relative)
    far_bucket = 8 + sum([(distance >= threshold).astype(jnp.int32) for threshold in far_marks])
    bucket = jnp.where(distance < 8, distance, far_bucket)
    return (bucket + jnp.where(relative > 0, 16, 0)).astype(jnp.int32)

def norm_rows(values_in, gain):
    widened = values_in.astype(jnp.float32)
    scale = lax.rsqrt(lax.optimization_barrier(jnp.mean(widened * widened, axis=-1, keepdims=True)) + epsilon)
    return (widened * scale * gain).astype(jnp.bfloat16)

def layout(lengths_row, prefix_row, row_ids):
    req_ends = jnp.cumsum(lengths_row).astype(jnp.int32)
    req_starts = (req_ends - lengths_row).astype(jnp.int32)
    member = ((row_ids[:, None] >= req_starts[None, :]) & (row_ids[:, None] < req_ends[None, :])).astype(jnp.int32)
    numbers = jnp.arange(lengths_row.shape[0], dtype=jnp.int32)
    req_index = (lax.optimization_barrier(jnp.sum(member * numbers[None, :], axis=1)) + lax.optimization_barrier(jnp.sum(member, axis=1)) - 1).astype(jnp.int32)
    offset = (row_ids - lax.optimization_barrier(jnp.sum(member * req_starts[None, :], axis=1))).astype(jnp.int32)
    chosen = lax.optimization_barrier(jnp.sum(member * prefix_row[None, :], axis=1)).astype(jnp.int32)
    return (req_index, offset, chosen)

def reference(tokens, attn_gain, w_query, w_key, w_value, w_attn_out, rel_bias, prefix_cache, lengths, prefix_map, mlp_gain, w_in, w_out):
    bias_table = rel_bias.T
    results = []
    for group_idx in range(N_GRP):
        group_rows = tokens[group_idx * TOK_GRP:(group_idx + 1) * TOK_GRP]
        normed = norm_rows(group_rows, attn_gain)
        query = jnp.dot(normed, w_query, preferred_element_type=jnp.float32).astype(jnp.bfloat16)
        key_proj = jnp.dot(normed, w_key, preferred_element_type=jnp.float32).astype(jnp.bfloat16)
        value_proj = jnp.dot(normed, w_value, preferred_element_type=jnp.float32).astype(jnp.bfloat16)
        pad_rows = jnp.zeros((TOK_DEV, D), jnp.bfloat16)
        key_padded = jnp.concatenate([pad_rows, key_proj, pad_rows], axis=0)
        value_padded = jnp.concatenate([pad_rows, value_proj, pad_rows], axis=0)
        cache = prefix_cache[group_idx * PREF_GRP:(group_idx + 1) * PREF_GRP].astype(jnp.float32)
        cache_keys = cache[:, :, :D].reshape(PREF_GRP * PLEN, H, DK)
        cache_values = cache[:, :, D:].reshape(PREF_GRP * PLEN, H, DK)
        group_lengths = lengths[group_idx]
        group_map = prefix_map[group_idx]

        def attend(block_idx):
            row_first = block_idx * TOK_DEV
            query_ids = row_first + jnp.arange(TOK_DEV, dtype=jnp.int32)
            window_ids = row_first - TOK_DEV + jnp.arange(3 * TOK_DEV, dtype=jnp.int32)
            query_req, query_offset, query_prefix = layout(group_lengths, group_map, query_ids)
            window_req = layout(group_lengths, group_map, window_ids)[0]
            query_block = lax.dynamic_slice_in_dim(query, row_first, TOK_DEV, 0).astype(jnp.float32).reshape(TOK_DEV, H, DK)
            key_window = lax.dynamic_slice_in_dim(key_padded, row_first, 3 * TOK_DEV, 0).astype(jnp.float32).reshape(3 * TOK_DEV, H, DK)
            value_window = lax.dynamic_slice_in_dim(value_padded, row_first, 3 * TOK_DEV, 0).astype(jnp.float32).reshape(3 * TOK_DEV, H, DK)
            positions = jnp.arange(PLEN, dtype=jnp.int32)
            prefix_terms = jnp.take(bias_table, bucket_of(positions[None, :] - PLEN - query_offset[:, None]), axis=1)
            prefix_terms = jnp.tile(prefix_terms, (1, 1, PREF_GRP))
            prefix_allowed = jnp.repeat(query_prefix[:, None] == jnp.arange(PREF_GRP, dtype=jnp.int32)[None, :], PLEN, axis=1)
            suffix_terms = jnp.take(bias_table, bucket_of(window_ids[None, :] - query_ids[:, None]), axis=1)
            suffix_allowed = window_req[None, :] == query_req[:, None]
            scores = jnp.concatenate([jnp.einsum('qhd,khd->hqk', query_block, cache_keys) + prefix_terms, jnp.einsum('qhd,khd->hqk', query_block, key_window) + suffix_terms], axis=2)
            allowed = jnp.concatenate([prefix_allowed, suffix_allowed], axis=1)
            scores = jnp.where(allowed[None], scores, masked_score)
            row_max = lax.optimization_barrier(jnp.max(scores, axis=2, keepdims=True))
            exp_terms = jnp.exp(scores - row_max)
            row_sum = lax.optimization_barrier(jnp.sum(exp_terms, axis=2))
            weights = lax.optimization_barrier(exp_terms.astype(jnp.bfloat16)).astype(jnp.float32)
            all_values = jnp.concatenate([cache_values, value_window], axis=0)
            weighted = jnp.einsum('hqk,khd->hqd', weights, all_values)
            attended = (weighted / row_sum[:, :, None]).transpose(1, 0, 2).reshape(TOK_DEV, D)
            return attended.astype(jnp.bfloat16)
        attended = lax.map(attend, jnp.arange(N_REQ, dtype=jnp.int32)).reshape(TOK_GRP, D)
        hidden_one = (group_rows.astype(jnp.float32) + jnp.dot(attended, w_attn_out, preferred_element_type=jnp.float32)).astype(jnp.bfloat16)
        normed_two = norm_rows(hidden_one, mlp_gain)
        units = jnp.maximum(jnp.dot(normed_two, w_in.T, preferred_element_type=jnp.float32), 0.0).astype(jnp.bfloat16)
        layer_out = (hidden_one.astype(jnp.float32) + jnp.dot(units, w_out, preferred_element_type=jnp.float32)).astype(jnp.bfloat16)
        results.append(layer_out)
    return jnp.concatenate(results, axis=0)
```

```python
import functools

import jax
import jax.numpy as jnp
from jax import lax
from jax.experimental import pallas as pl
from jax.experimental.pallas import tpu as pltpu
from jax.sharding import PartitionSpec as P

D = 1024
H = 16
DK = 64
PLEN = 512
PREF_GRP = 2
LANES = 128
MESH = pl.DeviceIdType.MESH


epsilon = 1e-06
far_marks = (12, 16, 23, 32, 46, 64, 91)
masked_score = -1e30


def padded(value, sides, width):
    for axis, dim in sides:
        count, length = (lax.axis_size(axis), value.shape[dim])
        up = [(i, (i + 1) % count) for i in range(count - 1)]
        down = [(j, i) for i, j in up]
        last = lax.slice_in_dim(value, length - width, length, axis=dim)
        leading = lax.slice_in_dim(value, 0, width, axis=dim)
        before = lax.ppermute(last, axis, up)
        after = lax.ppermute(leading, axis, down)
        value = jnp.concatenate([before, value, after], axis=dim)
    return value


def bucket_of(relative):
    distance = jnp.abs(relative)
    far_bucket = 8 + sum([(distance >= threshold).astype(jnp.int32) for threshold in far_marks])
    bucket = jnp.where(distance < 8, distance, far_bucket)
    return bucket + jnp.where(relative > 0, 16, 0)


def bias_lookup(relative, rel_bias):
    buckets = bucket_of(relative)
    marks = jnp.arange(rel_bias.shape[0], dtype=jnp.int32)
    one_hot = (buckets[:, :, None] == marks[None, None, :]).astype(jnp.float32)
    return jnp.einsum(
        "qkb,bh->hqk",
        one_hot,
        rel_bias,
        precision=lax.Precision.HIGHEST,
        preferred_element_type=jnp.float32,
    )


def norm_rows(values_in, gain):
    widened = values_in.astype(jnp.float32)
    scale = lax.rsqrt(jnp.mean(widened * widened, axis=-1, keepdims=True) + epsilon)
    return (widened * scale * gain).astype(jnp.bfloat16)


def layout(lengths_row, prefix_row, row_ids):
    req_ends = jnp.cumsum(lengths_row)
    req_starts = req_ends - lengths_row
    member = (
        (row_ids[:, None] >= req_starts[None, :]) & (row_ids[:, None] < req_ends[None, :])
    ).astype(jnp.int32)
    numbers = jnp.arange(lengths_row.shape[0], dtype=jnp.int32)
    req_index = jnp.sum(member * numbers[None, :], axis=1) + jnp.sum(member, axis=1) - 1
    offset = row_ids - jnp.sum(member * req_starts[None, :], axis=1)
    chosen = jnp.sum(member * prefix_row[None, :], axis=1)
    return (req_index, offset, chosen)


def softmax_part(scores, value_rows, allowed):
    scores = jnp.where(allowed[None], scores, masked_score)
    row_max = jnp.max(scores, axis=2)
    exp_terms = jnp.where(allowed[None], jnp.exp(scores - row_max[:, :, None]), 0.0)
    row_sum = jnp.sum(exp_terms, axis=2)
    weighted = jnp.einsum(
        "hqk,khd->hqd",
        exp_terms.astype(jnp.bfloat16),
        value_rows,
        preferred_element_type=jnp.float32,
    )
    return (row_max, row_sum, weighted)


def combine(first_part, second_part):
    row_max = jnp.maximum(first_part[0], second_part[0])
    scale_one = jnp.exp(first_part[0] - row_max)
    scale_two = jnp.exp(second_part[0] - row_max)
    row_sum = first_part[1] * scale_one + second_part[1] * scale_two
    weighted = first_part[2] * scale_one[:, :, None] + second_part[2] * scale_two[:, :, None]
    return (row_max, row_sum, weighted)


def feed_forward(rows_in, in_part, out_part):
    units = lax.dot_general(
        rows_in, in_part, (((1,), (1,)), ((), ())), preferred_element_type=jnp.float32
    )
    units = jnp.maximum(units, 0.0).astype(jnp.bfloat16)
    return jnp.dot(units, out_part, preferred_element_type=jnp.float32)


def body(
    tokens,
    attn_gain,
    w_query,
    w_key,
    w_value,
    w_attn_out,
    rel_bias,
    prefix_cache,
    lengths,
    prefix_map,
    mlp_gain,
    w_in,
    w_out,
):
    rows_here = tokens.shape[0]
    device_pos = lax.axis_index("req")
    group_lengths = lengths[0]
    group_map = prefix_map[0]
    normed = norm_rows(tokens, attn_gain)
    query = (
        jnp.dot(normed, w_query, preferred_element_type=jnp.float32)
        .astype(jnp.bfloat16)
        .reshape(rows_here, H, DK)
    )
    key_value = jnp.concatenate(
        [
            jnp.dot(normed, w_key, preferred_element_type=jnp.float32).astype(jnp.bfloat16),
            jnp.dot(normed, w_value, preferred_element_type=jnp.float32).astype(jnp.bfloat16),
        ],
        axis=1,
    )
    query_ids = device_pos * rows_here + jnp.arange(rows_here, dtype=jnp.int32)
    query_req, query_offset, query_prefix = layout(group_lengths, group_map, query_ids)
    all_positions = jnp.arange(PLEN, dtype=jnp.int32)
    prefix_bias = bias_lookup(all_positions[None, :] - PLEN - query_offset[:, None], rel_bias)
    empty_state = (
        jnp.full((H, rows_here), masked_score, jnp.float32),
        jnp.zeros((H, rows_here), jnp.float32),
        jnp.zeros((H, rows_here, DK), jnp.float32),
    )
    running = empty_state
    shard_kv = lax.all_gather(prefix_cache, "req", axis=1, tiled=True)
    prefix_ids = jnp.arange(PREF_GRP, dtype=jnp.int32)
    slices = shard_kv.shape[0]
    piece_len = shard_kv.shape[1]
    step_len = max(min(piece_len, 512 // slices), 1)
    for begin in range(0, piece_len, step_len):
        width = min(step_len, piece_len - begin)
        block = shard_kv[:, begin : begin + width]
        key_rows = block[:, :, :D].reshape(slices, width, H, DK)
        value_rows = block[:, :, D:].reshape(-1, H, DK)
        rel_terms = lax.dynamic_slice_in_dim(prefix_bias, begin, width, 2)
        prefix_scores = jnp.einsum(
            "qhd,swhd->hqsw", query, key_rows, preferred_element_type=jnp.float32
        )
        prefix_scores = (prefix_scores + rel_terms[:, :, None, :]).reshape(
            H, rows_here, slices * width
        )
        allowed = jnp.repeat(query_prefix[:, None] == prefix_ids[None, :], width, axis=1)
        running = combine(running, softmax_part(prefix_scores, value_rows, allowed))
    state = running
    window = padded(key_value, (("req", 0),), rows_here)
    window_ids = device_pos * rows_here - rows_here + jnp.arange(3 * rows_here, dtype=jnp.int32)
    window_req = layout(group_lengths, group_map, window_ids)[0]
    for part_idx in range(3):
        part_rows = window[part_idx * rows_here : (part_idx + 1) * rows_here]
        part_ids = window_ids[part_idx * rows_here : (part_idx + 1) * rows_here]
        part_req = window_req[part_idx * rows_here : (part_idx + 1) * rows_here]
        suffix_terms = bias_lookup(part_ids[None, :] - query_ids[:, None], rel_bias)
        suffix_allowed = part_req[None, :] == query_req[:, None]
        scores = (
            jnp.einsum(
                "qhd,khd->hqk",
                query,
                part_rows[:, :D].reshape(-1, H, DK),
                preferred_element_type=jnp.float32,
            )
            + suffix_terms
        )
        suffix_state = softmax_part(scores, part_rows[:, D:].reshape(-1, H, DK), suffix_allowed)
        state = combine(state, suffix_state)
    attended = (
        (state[2] / state[1][:, :, None])
        .transpose(1, 0, 2)
        .reshape(rows_here, D)
        .astype(jnp.bfloat16)
    )
    hidden_one = (
        tokens.astype(jnp.float32)
        + jnp.dot(attended, w_attn_out, preferred_element_type=jnp.float32)
    ).astype(jnp.bfloat16)
    normed_two = norm_rows(hidden_one, mlp_gain)
    gathered = lax.all_gather(normed_two, "grp", axis=0, tiled=True)
    mlp_total = lax.psum_scatter(
        feed_forward(gathered, w_in, w_out).astype(jnp.bfloat16),
        "grp",
        scatter_dimension=0,
        tiled=True,
    ).astype(jnp.float32)
    return (hidden_one.astype(jnp.float32) + mlp_total).astype(jnp.bfloat16)


def bucket_steps():
    return tuple((i, i) for i in range(1, 9)) + tuple((t, 9 + i) for i, t in enumerate(far_marks))


def chain(distance, table, head, first):
    value = jnp.full(distance.shape, table[first, head], jnp.float32)
    for threshold, number in bucket_steps():
        value = jnp.where(distance >= threshold, table[first + number, head], value)
    return value


def layer_kernel(
    n_req,
    tokens_hbm,
    attn_gain,
    wq_hbm,
    wk_hbm,
    wv_hbm,
    wo_hbm,
    rel_bias,
    cache_hbm,
    lengths,
    prefix_map,
    mlp_gain,
    win_hbm,
    wout_hbm,
    out_ref,
    tok,
    w_attn,
    w_in,
    w_out,
    normed,
    stage,
    k_cache,
    v_cache,
    q_all,
    kv_all,
    tail_bias,
    near_bias,
    key_req,
    row_prefix,
    row_max,
    row_sum,
    row_acc,
    o_send,
    att,
    h_one,
    n_two,
    units,
    part_own,
    part_far,
    fast_out,
    fast_in,
    chip_out,
    chip_in,
    far_out,
    far_in,
    load_sem,
    own_sem,
    kc_send,
    kc_recv,
    vc_send,
    vc_recv,
    q_send,
    q_recv,
    kv_send,
    kv_recv,
    o_ssem,
    o_rsem,
    f_send,
    f_recv,
):
    me = lax.axis_index("req")
    grp = lax.axis_index("grp")
    side = lax.rem(grp, 2)
    plane = lax.div(grp, 2)
    mate = plane * 2 + (1 - side)
    across = (1 - plane) * 2 + side
    rows = tokens_hbm.shape[0]
    piece = cache_hbm.shape[1]
    half = rows // 2

    def remote(src, dst, ssem, rsem, **where):
        return pltpu.make_async_remote_copy(
            src_ref=src, dst_ref=dst, send_sem=ssem, recv_sem=rsem, device_id=where, device_id_type=MESH
        )

    def lanes_of(index):
        return pl.ds(pl.multiple_of(index * LANES, LANES), LANES)

    def rows_of(index):
        return pl.ds(pl.multiple_of(index * rows, rows), rows)

    loads = [
        pltpu.make_async_copy(src, dst, load_sem.at[i])
        for i, (src, dst) in enumerate(
            [
                (tokens_hbm, tok),
                (wq_hbm, w_attn.at[0]),
                (wk_hbm, w_attn.at[1]),
                (wv_hbm, w_attn.at[2]),
                (wo_hbm, w_attn.at[3]),
                (win_hbm, w_in),
                (wout_hbm, w_out),
            ]
        )
    ]
    for load in loads:
        load.start()

    barrier = pltpu.get_barrier_semaphore()
    for d in range(1, n_req):
        pl.semaphore_signal(
            barrier, inc=1, device_id={"req": lax.rem(me + d, n_req)}, device_id_type=MESH
        )
    for other in (mate, across):
        pl.semaphore_signal(barrier, inc=1, device_id={"grp": other}, device_id_type=MESH)
    pl.semaphore_wait(barrier, n_req + 1)

    def cache_copy(buf, first, sends, recvs, d, peer, owner):
        return remote(
            cache_hbm.at[:, :, pl.ds(pl.multiple_of(first + peer * LANES, LANES), LANES)],
            buf.at[:, pl.ds(pl.multiple_of(owner * piece, piece), piece), :],
            sends.at[d],
            recvs.at[d],
            req=peer,
        )

    def q_copy(d, peer, owner):
        return remote(
            stage.at[0, :, lanes_of(peer)], q_all.at[rows_of(owner), :], q_send.at[d], q_recv.at[d], req=peer
        )

    def kv_copy(d, peer, owner):
        return remote(
            stage.at[pl.ds(1, 2), :, lanes_of(peer)],
            kv_all.at[:, rows_of(owner + 1), :],
            kv_send.at[d],
            kv_recv.at[d],
            req=peer,
        )

    def o_copy(d, peer, owner):
        return remote(
            o_send.at[peer], att.at[:, lanes_of(owner)], o_ssem.at[d], o_rsem.at[d], req=peer
        )

    def outgoing(make):
        return [make(d, lax.rem(me + d, n_req), me) for d in range(1, n_req)]

    def incoming(make):
        return [
            make(d, lax.rem(me + d, n_req), lax.rem(me + n_req - d, n_req)) for d in range(1, n_req)
        ]

    def kc_copy(d, peer, owner):
        return cache_copy(k_cache, 0, kc_send, kc_recv, d, peer, owner)

    def vc_copy(d, peer, owner):
        return cache_copy(v_cache, D, vc_send, vc_recv, d, peer, owner)

    for copy in outgoing(kc_copy) + outgoing(vc_copy):
        copy.start()
    own_copies = [
        pltpu.make_async_copy(
            cache_hbm.at[:, :, pl.ds(pl.multiple_of(first + me * LANES, LANES), LANES)],
            buf.at[:, pl.ds(pl.multiple_of(me * piece, piece), piece), :],
            own_sem.at[i],
        )
        for i, (buf, first) in enumerate([(k_cache, 0), (v_cache, D)])
    ]
    for copy in own_copies:
        copy.start()

    loads[0].wait()
    wide = tok[...].astype(jnp.float32)
    scale = lax.rsqrt(jnp.mean(wide * wide, axis=-1, keepdims=True) + epsilon)
    normed[...] = (wide * scale * attn_gain[...]).astype(jnp.bfloat16)

    tile = 256
    for part in range(3):
        loads[1 + part].wait()

        @pl.loop(0, D // tile)
        def _(t, part=part):
            cols = pl.ds(pl.multiple_of(t * tile, tile), tile)
            stage[part, :, cols] = jnp.dot(
                normed[...], w_attn[part, :, cols], preferred_element_type=jnp.float32
            ).astype(jnp.bfloat16)

        if part == 0:
            for copy in outgoing(q_copy):
                copy.start()
        if part == 2:
            for copy in outgoing(kv_copy):
                copy.start()
    q_all[rows_of(me), :] = stage[0, :, lanes_of(me)]
    zeros = jnp.zeros((rows, LANES), jnp.bfloat16)
    for part in range(2):
        kv_all[part, rows_of(me + 1), :] = stage[1 + part, :, lanes_of(me)]
        kv_all[part, pl.ds(0, rows), :] = zeros
        kv_all[part, pl.ds((n_req + 1) * rows, rows), :] = zeros

    ends = []
    total = 0
    n_requests = lengths.shape[1]
    for j in range(n_requests):
        total = total + lengths[0, j]
        ends.append(total)
    key_ids = lax.broadcasted_iota(jnp.int32, key_req.shape, 1) - rows
    key_number = jnp.where(key_ids < 0, -1, 0)
    for end in ends:
        key_number = key_number + jnp.where(key_ids >= end, 1, 0)
    key_req[...] = key_number

    row_iota = lax.broadcasted_iota(jnp.int32, (rows, LANES), 0)
    lane_iota = lax.broadcasted_iota(jnp.int32, (rows, LANES), 1)
    for head in range(2):
        for part in range(3):
            ahead = lane_iota + (part - 1) * rows - row_iota
            distance = jnp.abs(ahead)
            before = chain(distance, rel_bias, 2 * me + head, 0)
            after = chain(distance, rel_bias, 2 * me + head, 16)
            near_bias[0, pl.ds(head * rows, rows), pl.ds(part * LANES, LANES)] = jnp.where(
                ahead > 0, after, before
            )

    @pl.loop(0, n_req)
    def _(step):
        b = n_req - 1 - step
        ids = row_iota + b * rows
        number = jnp.zeros_like(ids)
        start = jnp.zeros_like(ids)
        prefix = jnp.full(ids.shape, prefix_map[0, 0], jnp.int32)
        for j in range(n_requests):
            past = ids >= ends[j]
            number = number + jnp.where(past, 1, 0)
            start = start + jnp.where(past, lengths[0, j], 0)
            if j + 1 < n_requests:
                prefix = jnp.where(past, prefix_map[0, j + 1], prefix)
        row_prefix[b] = prefix
        distance = LANES + ids - start - lane_iota
        for head in range(2):
            tail_bias[b, pl.ds(head * rows, rows), :] = chain(distance, rel_bias, 2 * me + head, 0)
        for part in range(3):
            other = key_req[pl.ds(0, 1), pl.ds(pl.multiple_of(b * rows + part * LANES, LANES), LANES)]
            same = other == number
            for head in range(2):
                here = (pl.ds(head * rows, rows), pl.ds(part * LANES, LANES))
                near_bias[b, here[0], here[1]] = jnp.where(
                    same, near_bias[0, here[0], here[1]], masked_score
                )

    first_head = lane_iota < DK

    def query_heads(b):
        q = q_all[rows_of(b), :]
        nothing = jnp.zeros_like(q)
        return jnp.concatenate(
            [jnp.where(first_head, q, nothing), jnp.where(first_head, nothing, q)], axis=0
        )

    for copy in own_copies:
        copy.wait()
    for make in (kc_copy, q_copy, vc_copy):
        for copy in incoming(make):
            copy.wait_recv()

    far_bias = jnp.concatenate(
        [jnp.full((rows, 1), rel_bias[15, 2 * me + head], jnp.float32) for head in range(2)], axis=0
    )
    far_keys = PLEN - LANES

    @pl.loop(0, n_req)
    def _(b):
        qh = query_heads(b)
        choice = row_prefix[b]
        zero_first = jnp.concatenate([choice, choice], axis=0) == 0
        nothing = jnp.zeros_like(qh)
        q2 = jnp.concatenate(
            [jnp.where(zero_first, qh, nothing), jnp.where(zero_first, nothing, qh)], axis=1
        )
        keys = jnp.concatenate([k_cache[0], k_cache[1]], axis=1)
        scores = lax.dot_general(
            q2, keys, (((1,), (1,)), ((), ())), preferred_element_type=jnp.float32
        )
        scores = jnp.concatenate(
            [scores[:, :far_keys] + far_bias, scores[:, far_keys:] + tail_bias[b]], axis=1
        )
        top = jnp.max(scores, axis=1, keepdims=True)
        terms = jnp.exp(scores - top)
        row_max[b] = jnp.broadcast_to(top, (2 * rows, LANES))
        row_sum[b] = jnp.broadcast_to(jnp.sum(terms, axis=1, keepdims=True), (2 * rows, LANES))
        values = jnp.concatenate([v_cache[0], v_cache[1]], axis=1)
        acc = jnp.dot(terms.astype(jnp.bfloat16), values, preferred_element_type=jnp.float32)
        row_acc[b] = jnp.where(zero_first, acc[:, :LANES], acc[:, LANES:])

    for copy in incoming(kv_copy):
        copy.wait_recv()

    def near(b):
        qh = query_heads(b)
        window = pl.ds(pl.multiple_of(b * rows, rows), 3 * rows)
        scores = (
            lax.dot_general(
                qh,
                kv_all[0, window, :],
                (((1,), (1,)), ((), ())),
                preferred_element_type=jnp.float32,
            )
            + near_bias[b]
        )
        old = row_max[b]
        top = jnp.maximum(old, jnp.max(scores, axis=1, keepdims=True))
        terms = jnp.exp(scores - jnp.concatenate([top, top, top], axis=1))
        shrink = jnp.exp(old - top)
        denom = row_sum[b] * shrink + jnp.sum(terms, axis=1, keepdims=True)
        acc = row_acc[b] * shrink + jnp.dot(
            terms.astype(jnp.bfloat16), kv_all[1, window, :], preferred_element_type=jnp.float32
        )
        result = acc / denom
        return jnp.where(first_head, result[:rows], result[rows:]).astype(jnp.bfloat16)

    @pl.loop(1, n_req)
    def _(d):
        b = lax.rem(me + d, n_req)
        o_send[b] = near(b)
        o_copy(d, b, me).start()

    att[:, lanes_of(me)] = near(me)

    loads[4].wait()
    for copy in incoming(o_copy):
        copy.wait_recv()

    @pl.loop(0, D // tile)
    def _(t):
        cols = pl.ds(pl.multiple_of(t * tile, tile), tile)
        h_one[:, cols] = (
            tok[:, cols].astype(jnp.float32)
            + jnp.dot(att[...], w_attn[3, :, cols], preferred_element_type=jnp.float32)
        ).astype(jnp.bfloat16)

    wide = h_one[...].astype(jnp.float32)
    scale = lax.rsqrt(jnp.mean(wide * wide, axis=-1, keepdims=True) + epsilon)
    n_two[0] = (wide * scale * mlp_gain[...]).astype(jnp.bfloat16)

    mine = remote(n_two.at[0], n_two.at[1], f_send.at[0], f_recv.at[0], grp=mate)
    parts = [pl.ds(r * half, half) for r in range(2)]
    cross = [
        remote(n_two.at[0, parts[r]], n_two.at[2, parts[r]], f_send.at[1 + r], f_recv.at[1 + r], grp=across)
        for r in range(2)
    ]
    relay = [
        remote(n_two.at[2, parts[r]], n_two.at[3, parts[r]], f_send.at[3 + r], f_recv.at[3 + r], grp=mate)
        for r in range(2)
    ]
    back = remote(fast_out, fast_in, f_send.at[5], f_recv.at[5], grp=mate)
    swap = [
        remote(chip_out.at[r], chip_in.at[r], f_send.at[6 + r], f_recv.at[6 + r], grp=mate) for r in range(2)
    ]
    home = [
        remote(far_out.at[r], far_in.at[r], f_send.at[8 + r], f_recv.at[8 + r], grp=across) for r in range(2)
    ]
    for copy in cross:
        copy.start()
    mine.start()
    loads[5].wait()
    loads[6].wait()

    def feed(rows_in, count, out):
        @pl.loop(0, w_in.shape[0] // tile)
        def _(t):
            cols = pl.ds(pl.multiple_of(t * tile, tile), tile)
            units[pl.ds(0, count), cols] = jnp.maximum(
                lax.dot_general(
                    rows_in,
                    w_in[cols, :],
                    (((1,), (1,)), ((), ())),
                    preferred_element_type=jnp.float32,
                ),
                0.0,
            ).astype(jnp.bfloat16)

        @pl.loop(0, D // tile)
        def _(t):
            cols = pl.ds(pl.multiple_of(t * tile, tile), tile)
            out[pl.ds(0, count), cols] = jnp.dot(
                units[pl.ds(0, count), :], w_out[:, cols], preferred_element_type=jnp.float32
            )

    mine.wait_recv()
    feed(jnp.concatenate([n_two[0], n_two[1]], axis=0), 2 * rows, part_own)
    fast_out[...] = part_own[pl.ds(rows, rows), :].astype(jnp.bfloat16)
    back.start()
    for r in range(2):
        cross[r].wait_recv()
        relay[r].start()
    for r in range(2):
        relay[r].wait_recv()
        feed(jnp.concatenate([n_two[2, parts[r]], n_two[3, parts[r]]], axis=0), rows, part_far)
        chip_out[r] = part_far[pl.ds(half, half), :].astype(jnp.bfloat16)
        swap[r].start()
        swap[r].wait_recv()
        far_out[r] = (part_far[pl.ds(0, half), :] + chip_in[r].astype(jnp.float32)).astype(jnp.bfloat16)
        home[r].start()
    back.wait_recv()
    for r in range(2):
        home[r].wait_recv()
        out_ref[parts[r], :] = (
            h_one[parts[r], :].astype(jnp.float32)
            + part_own[parts[r], :]
            + fast_in[parts[r], :].astype(jnp.float32)
            + far_in[r].astype(jnp.float32)
        ).astype(jnp.bfloat16)

    for make in (kc_copy, vc_copy, q_copy, kv_copy, o_copy):
        for copy in outgoing(make):
            copy.wait_send()
    for copy in [mine, back] + cross + relay + swap + home:
        copy.wait_send()


def fused(
    tokens,
    attn_gain,
    w_query,
    w_key,
    w_value,
    w_attn_out,
    rel_bias,
    prefix_cache,
    lengths,
    prefix_map,
    mlp_gain,
    w_in,
    w_out,
):
    n_req = lax.axis_size("req")
    rows = tokens.shape[0]
    group = n_req * rows
    hbm = pl.BlockSpec(memory_space=pl.ANY)
    vmem = pl.BlockSpec(memory_space=pltpu.VMEM)
    smem = pl.BlockSpec(memory_space=pltpu.SMEM)
    half = rows // 2
    bf16, f32 = jnp.bfloat16, jnp.float32
    sems = pltpu.SemaphoreType.DMA
    return pl.pallas_call(
        functools.partial(layer_kernel, n_req),
        out_shape=jax.ShapeDtypeStruct((rows, D), bf16),
        in_specs=[hbm, vmem, hbm, hbm, hbm, hbm, smem, hbm, smem, smem, vmem, hbm, hbm],
        out_specs=vmem,
        scratch_shapes=[
            pltpu.VMEM((rows, D), bf16),
            pltpu.VMEM((4, D, D), bf16),
            pltpu.VMEM(w_in.shape, bf16),
            pltpu.VMEM(w_out.shape, bf16),
            pltpu.VMEM((rows, D), bf16),
            pltpu.VMEM((3, rows, D), bf16),
            pltpu.VMEM((PREF_GRP, PLEN, LANES), bf16),
            pltpu.VMEM((PREF_GRP, PLEN, LANES), bf16),
            pltpu.VMEM((group, LANES), bf16),
            pltpu.VMEM((2, group + 2 * rows, LANES), bf16),
            pltpu.VMEM((n_req, 2 * rows, LANES), f32),
            pltpu.VMEM((n_req, 2 * rows, 3 * LANES), f32),
            pltpu.VMEM((8, group + 2 * rows), jnp.int32),
            pltpu.VMEM((n_req, rows, LANES), jnp.int32),
            pltpu.VMEM((n_req, 2 * rows, LANES), f32),
            pltpu.VMEM((n_req, 2 * rows, LANES), f32),
            pltpu.VMEM((n_req, 2 * rows, LANES), f32),
            pltpu.VMEM((n_req, rows, LANES), bf16),
            pltpu.VMEM((rows, D), bf16),
            pltpu.VMEM((rows, D), bf16),
            pltpu.VMEM((4, rows, D), bf16),
            pltpu.VMEM((2 * rows, w_in.shape[0]), bf16),
            pltpu.VMEM((2 * rows, D), f32),
            pltpu.VMEM((rows, D), f32),
            pltpu.VMEM((rows, D), bf16),
            pltpu.VMEM((rows, D), bf16),
            pltpu.VMEM((2, half, D), bf16),
            pltpu.VMEM((2, half, D), bf16),
            pltpu.VMEM((2, half, D), bf16),
            pltpu.VMEM((2, half, D), bf16),
            sems((7,)),
            sems((2,)),
        ]
        + [sems((n_req,)) for _ in range(10)]
        + [sems((10,)), sems((10,))],
        compiler_params=pltpu.CompilerParams(
            collective_id=0, has_side_effects=True, vmem_limit_bytes=48 * 1024 * 1024
        ),
    )(
        tokens,
        attn_gain.reshape(1, D),
        w_query,
        w_key,
        w_value,
        w_attn_out,
        rel_bias,
        prefix_cache,
        lengths,
        prefix_map,
        mlp_gain.reshape(1, D),
        w_in,
        w_out,
    )


def pairs_fit(mesh):
    return mesh.shape["req"] * LANES == D and mesh.shape["grp"] == 4


def solution(mesh):
    return jax.shard_map(
        fused if pairs_fit(mesh) else body,
        mesh=mesh,
        in_specs=(
            P(("grp", "req"), None),
            P(),
            P(),
            P(),
            P(),
            P(),
            P(),
            P("grp", "req", None),
            P("grp", None),
            P("grp", None),
            P(),
            P("grp", None),
            P("grp", None),
        ),
        out_specs=P(("grp", "req"), None),
        check_vma=False,
    )
```

```python
import functools

import jax
import jax.numpy as jnp
from jax import lax
from jax.experimental import pallas as pl
from jax.experimental.pallas import tpu as pltpu
from jax.sharding import PartitionSpec as P

D = 1024
H = 16
DK = 64
PLEN = 512
PREF_GRP = 2
LANES = 128
MESH = pl.DeviceIdType.MESH


epsilon = 1e-06
far_marks = (12, 16, 23, 32, 46, 64, 91)
masked_score = -1e30


def padded(value, sides, width):
    for axis, dim in sides:
        count, length = (lax.axis_size(axis), value.shape[dim])
        up = [(i, (i + 1) % count) for i in range(count - 1)]
        down = [(j, i) for i, j in up]
        last = lax.slice_in_dim(value, length - width, length, axis=dim)
        leading = lax.slice_in_dim(value, 0, width, axis=dim)
        before = lax.ppermute(last, axis, up)
        after = lax.ppermute(leading, axis, down)
        value = jnp.concatenate([before, value, after], axis=dim)
    return value


def bucket_of(relative):
    distance = jnp.abs(relative)
    far_bucket = 8 + sum([(distance >= threshold).astype(jnp.int32) for threshold in far_marks])
    bucket = jnp.where(distance < 8, distance, far_bucket)
    return bucket + jnp.where(relative > 0, 16, 0)


def bias_lookup(relative, rel_bias):
    buckets = bucket_of(relative)
    marks = jnp.arange(rel_bias.shape[0], dtype=jnp.int32)
    one_hot = (buckets[:, :, None] == marks[None, None, :]).astype(jnp.float32)
    return jnp.einsum(
        "qkb,bh->hqk",
        one_hot,
        rel_bias,
        precision=lax.Precision.HIGHEST,
        preferred_element_type=jnp.float32,
    )


def norm_rows(values_in, gain):
    widened = values_in.astype(jnp.float32)
    scale = lax.rsqrt(jnp.mean(widened * widened, axis=-1, keepdims=True) + epsilon)
    return (widened * scale * gain).astype(jnp.bfloat16)


def layout(lengths_row, prefix_row, row_ids):
    req_ends = jnp.cumsum(lengths_row)
    req_starts = req_ends - lengths_row
    member = (
        (row_ids[:, None] >= req_starts[None, :]) & (row_ids[:, None] < req_ends[None, :])
    ).astype(jnp.int32)
    numbers = jnp.arange(lengths_row.shape[0], dtype=jnp.int32)
    req_index = jnp.sum(member * numbers[None, :], axis=1) + jnp.sum(member, axis=1) - 1
    offset = row_ids - jnp.sum(member * req_starts[None, :], axis=1)
    chosen = jnp.sum(member * prefix_row[None, :], axis=1)
    return (req_index, offset, chosen)


def softmax_part(scores, value_rows, allowed):
    scores = jnp.where(allowed[None], scores, masked_score)
    row_max = jnp.max(scores, axis=2)
    exp_terms = jnp.where(allowed[None], jnp.exp(scores - row_max[:, :, None]), 0.0)
    row_sum = jnp.sum(exp_terms, axis=2)
    weighted = jnp.einsum(
        "hqk,khd->hqd",
        exp_terms.astype(jnp.bfloat16),
        value_rows,
        preferred_element_type=jnp.float32,
    )
    return (row_max, row_sum, weighted)


def combine(first_part, second_part):
    row_max = jnp.maximum(first_part[0], second_part[0])
    scale_one = jnp.exp(first_part[0] - row_max)
    scale_two = jnp.exp(second_part[0] - row_max)
    row_sum = first_part[1] * scale_one + second_part[1] * scale_two
    weighted = first_part[2] * scale_one[:, :, None] + second_part[2] * scale_two[:, :, None]
    return (row_max, row_sum, weighted)


def feed_forward(rows_in, in_part, out_part):
    units = lax.dot_general(
        rows_in, in_part, (((1,), (1,)), ((), ())), preferred_element_type=jnp.float32
    )
    units = jnp.maximum(units, 0.0).astype(jnp.bfloat16)
    return jnp.dot(units, out_part, preferred_element_type=jnp.float32)


def body(
    tokens,
    attn_gain,
    w_query,
    w_key,
    w_value,
    w_attn_out,
    rel_bias,
    prefix_cache,
    lengths,
    prefix_map,
    mlp_gain,
    w_in,
    w_out,
):
    rows_here = tokens.shape[0]
    device_pos = lax.axis_index("req")
    group_lengths = lengths[0]
    group_map = prefix_map[0]
    normed = norm_rows(tokens, attn_gain)
    query = (
        jnp.dot(normed, w_query, preferred_element_type=jnp.float32)
        .astype(jnp.bfloat16)
        .reshape(rows_here, H, DK)
    )
    key_value = jnp.concatenate(
        [
            jnp.dot(normed, w_key, preferred_element_type=jnp.float32).astype(jnp.bfloat16),
            jnp.dot(normed, w_value, preferred_element_type=jnp.float32).astype(jnp.bfloat16),
        ],
        axis=1,
    )
    query_ids = device_pos * rows_here + jnp.arange(rows_here, dtype=jnp.int32)
    query_req, query_offset, query_prefix = layout(group_lengths, group_map, query_ids)
    all_positions = jnp.arange(PLEN, dtype=jnp.int32)
    prefix_bias = bias_lookup(all_positions[None, :] - PLEN - query_offset[:, None], rel_bias)
    empty_state = (
        jnp.full((H, rows_here), masked_score, jnp.float32),
        jnp.zeros((H, rows_here), jnp.float32),
        jnp.zeros((H, rows_here, DK), jnp.float32),
    )
    running = empty_state
    shard_kv = lax.all_gather(prefix_cache, "req", axis=1, tiled=True)
    prefix_ids = jnp.arange(PREF_GRP, dtype=jnp.int32)
    slices = shard_kv.shape[0]
    piece_len = shard_kv.shape[1]
    step_len = max(min(piece_len, 512 // slices), 1)
    for begin in range(0, piece_len, step_len):
        width = min(step_len, piece_len - begin)
        block = shard_kv[:, begin : begin + width]
        key_rows = block[:, :, :D].reshape(slices, width, H, DK)
        value_rows = block[:, :, D:].reshape(-1, H, DK)
        rel_terms = lax.dynamic_slice_in_dim(prefix_bias, begin, width, 2)
        prefix_scores = jnp.einsum(
            "qhd,swhd->hqsw", query, key_rows, preferred_element_type=jnp.float32
        )
        prefix_scores = (prefix_scores + rel_terms[:, :, None, :]).reshape(
            H, rows_here, slices * width
        )
        allowed = jnp.repeat(query_prefix[:, None] == prefix_ids[None, :], width, axis=1)
        running = combine(running, softmax_part(prefix_scores, value_rows, allowed))
    state = running
    window = padded(key_value, (("req", 0),), rows_here)
    window_ids = device_pos * rows_here - rows_here + jnp.arange(3 * rows_here, dtype=jnp.int32)
    window_req = layout(group_lengths, group_map, window_ids)[0]
    for part_idx in range(3):
        part_rows = window[part_idx * rows_here : (part_idx + 1) * rows_here]
        part_ids = window_ids[part_idx * rows_here : (part_idx + 1) * rows_here]
        part_req = window_req[part_idx * rows_here : (part_idx + 1) * rows_here]
        suffix_terms = bias_lookup(part_ids[None, :] - query_ids[:, None], rel_bias)
        suffix_allowed = part_req[None, :] == query_req[:, None]
        scores = (
            jnp.einsum(
                "qhd,khd->hqk",
                query,
                part_rows[:, :D].reshape(-1, H, DK),
                preferred_element_type=jnp.float32,
            )
            + suffix_terms
        )
        suffix_state = softmax_part(scores, part_rows[:, D:].reshape(-1, H, DK), suffix_allowed)
        state = combine(state, suffix_state)
    attended = (
        (state[2] / state[1][:, :, None])
        .transpose(1, 0, 2)
        .reshape(rows_here, D)
        .astype(jnp.bfloat16)
    )
    hidden_one = (
        tokens.astype(jnp.float32)
        + jnp.dot(attended, w_attn_out, preferred_element_type=jnp.float32)
    ).astype(jnp.bfloat16)
    normed_two = norm_rows(hidden_one, mlp_gain)
    gathered = lax.all_gather(normed_two, "grp", axis=0, tiled=True)
    mlp_total = lax.psum_scatter(
        feed_forward(gathered, w_in, w_out).astype(jnp.bfloat16),
        "grp",
        scatter_dimension=0,
        tiled=True,
    ).astype(jnp.float32)
    return (hidden_one.astype(jnp.float32) + mlp_total).astype(jnp.bfloat16)


def bucket_steps():
    return tuple((i, i) for i in range(1, 9)) + tuple((t, 9 + i) for i, t in enumerate(far_marks))


def chain(distance, table, head, first):
    value = jnp.full(distance.shape, table[head, first], jnp.float32)
    for threshold, number in bucket_steps():
        value = jnp.where(distance >= threshold, table[head, first + number], value)
    return value


def layer_kernel(
    n_req,
    tokens_hbm,
    attn_gain,
    wq_hbm,
    wk_hbm,
    wv_hbm,
    wo_hbm,
    rel_bias,
    cache_hbm,
    lengths,
    prefix_map,
    mlp_gain,
    win_hbm,
    wout_hbm,
    out_ref,
    tok,
    w_attn,
    w_in,
    w_out,
    normed,
    stage,
    k_cache,
    v_cache,
    q_all,
    kv_all,
    tail_bias,
    near_bias,
    key_req,
    row_prefix,
    row_max,
    row_sum,
    row_acc,
    o_send,
    att,
    h_one,
    n_two,
    units,
    part_own,
    part_far,
    fast_out,
    fast_in,
    chip_out,
    chip_in,
    far_out,
    far_in,
    load_sem,
    own_sem,
    kc_send,
    kc_recv,
    vc_send,
    vc_recv,
    q_send,
    q_recv,
    kv_send,
    kv_recv,
    o_ssem,
    o_rsem,
    f_send,
    f_recv,
):
    me = lax.axis_index("req")
    grp = lax.axis_index("grp")
    side = lax.rem(grp, 2)
    plane = lax.div(grp, 2)
    mate = plane * 2 + (1 - side)
    across = (1 - plane) * 2 + side
    rows = tokens_hbm.shape[0]
    piece = cache_hbm.shape[1]
    half = rows // 2

    def remote(src, dst, ssem, rsem, **where):
        return pltpu.make_async_remote_copy(
            src_ref=src, dst_ref=dst, send_sem=ssem, recv_sem=rsem, device_id=where, device_id_type=MESH
        )

    def lanes_of(index):
        return pl.ds(pl.multiple_of(index * LANES, LANES), LANES)

    def rows_of(index):
        return pl.ds(pl.multiple_of(index * rows, rows), rows)

    loads = [
        pltpu.make_async_copy(src, dst, load_sem.at[i])
        for i, (src, dst) in enumerate(
            [
                (tokens_hbm, tok),
                (wq_hbm, w_attn.at[0]),
                (wk_hbm, w_attn.at[1]),
                (wv_hbm, w_attn.at[2]),
                (wo_hbm, w_attn.at[3]),
                (win_hbm, w_in),
                (wout_hbm, w_out),
            ]
        )
    ]
    for load in loads[:4]:
        load.start()

    barrier = pltpu.get_barrier_semaphore()
    for d in range(1, n_req):
        pl.semaphore_signal(
            barrier, inc=1, device_id={"req": lax.rem(me + d, n_req)}, device_id_type=MESH
        )
    for other in (mate, across):
        pl.semaphore_signal(barrier, inc=1, device_id={"grp": other}, device_id_type=MESH)
    pl.semaphore_wait(barrier, n_req + 1)

    def cache_copy(buf, first, sends, recvs, d, peer, owner):
        return remote(
            cache_hbm.at[:, :, pl.ds(pl.multiple_of(first + peer * LANES, LANES), LANES)],
            buf.at[:, pl.ds(pl.multiple_of(owner * piece, piece), piece), :],
            sends.at[d],
            recvs.at[d],
            req=peer,
        )

    def q_copy(d, peer, owner):
        return remote(
            stage.at[0, :, lanes_of(peer)], q_all.at[rows_of(owner), :], q_send.at[d], q_recv.at[d], req=peer
        )

    def kv_copy(d, peer, owner):
        return remote(
            stage.at[pl.ds(1, 2), :, lanes_of(peer)],
            kv_all.at[:, rows_of(owner + 1), :],
            kv_send.at[d],
            kv_recv.at[d],
            req=peer,
        )

    parts = [pl.ds(r * half, half) for r in range(2)]

    def o_copy(r):
        def make(d, peer, owner):
            return remote(
                o_send.at[peer, parts[r]],
                att.at[parts[r], lanes_of(owner)],
                o_ssem.at[r, d],
                o_rsem.at[r, d],
                req=peer,
            )

        return make

    def outgoing(make):
        return [make(d, lax.rem(me + d, n_req), me) for d in range(1, n_req)]

    def incoming(make):
        return [
            make(d, lax.rem(me + d, n_req), lax.rem(me + n_req - d, n_req)) for d in range(1, n_req)
        ]

    def kc_copy(d, peer, owner):
        return cache_copy(k_cache, 0, kc_send, kc_recv, d, peer, owner)

    def vc_copy(d, peer, owner):
        return cache_copy(v_cache, D, vc_send, vc_recv, d, peer, owner)

    for copy in outgoing(kc_copy) + outgoing(vc_copy):
        copy.start()
    own_copies = [
        pltpu.make_async_copy(
            cache_hbm.at[:, :, pl.ds(pl.multiple_of(first + me * LANES, LANES), LANES)],
            buf.at[:, pl.ds(pl.multiple_of(me * piece, piece), piece), :],
            own_sem.at[i],
        )
        for i, (buf, first) in enumerate([(k_cache, 0), (v_cache, D)])
    ]
    for copy in own_copies:
        copy.start()

    loads[0].wait()
    wide = tok[...].astype(jnp.float32)
    scale = lax.rsqrt(jnp.mean(wide * wide, axis=-1, keepdims=True) + epsilon)
    normed[...] = (wide * scale * attn_gain[...]).astype(jnp.bfloat16)

    tile = 256
    for part in range(3):
        loads[1 + part].wait()

        @pl.loop(0, D // tile)
        def _(t, part=part):
            cols = pl.ds(pl.multiple_of(t * tile, tile), tile)
            stage[part, :, cols] = jnp.dot(
                normed[...], w_attn[part, :, cols], preferred_element_type=jnp.float32
            ).astype(jnp.bfloat16)

        if part == 0:
            for copy in outgoing(q_copy):
                copy.start()
            for load in loads[4:]:
                load.start()
        if part == 2:
            for copy in outgoing(kv_copy):
                copy.start()
    q_all[rows_of(me), :] = stage[0, :, lanes_of(me)]
    zeros = jnp.zeros((rows, LANES), jnp.bfloat16)
    for part in range(2):
        kv_all[part, rows_of(me + 1), :] = stage[1 + part, :, lanes_of(me)]
        kv_all[part, pl.ds(0, rows), :] = zeros
        kv_all[part, pl.ds((n_req + 1) * rows, rows), :] = zeros

    ends = []
    total = 0
    n_requests = lengths.shape[1]
    for j in range(n_requests):
        total = total + lengths[0, j]
        ends.append(total)
    key_ids = lax.broadcasted_iota(jnp.int32, key_req.shape, 1) - rows
    key_number = jnp.where(key_ids < 0, -1, 0)
    for end in ends:
        key_number = key_number + jnp.where(key_ids >= end, 1, 0)
    key_req[...] = key_number

    def stacked(r, head):
        return pl.ds((2 * r + head) * half, half)

    row_iota = lax.broadcasted_iota(jnp.int32, (rows, LANES), 0)
    lane_iota = lax.broadcasted_iota(jnp.int32, (rows, LANES), 1)
    for head in range(2):
        for part in range(3):
            ahead = lane_iota + (part - 1) * rows - row_iota
            distance = jnp.abs(ahead)
            before = chain(distance, rel_bias, 2 * me + head, 0)
            after = chain(distance, rel_bias, 2 * me + head, 16)
            both = jnp.where(ahead > 0, after, before)
            for r in range(2):
                near_bias[0, stacked(r, head), pl.ds(part * LANES, LANES)] = both[r * half : (r + 1) * half]

    @pl.loop(0, n_req)
    def _(step):
        b = n_req - 1 - step
        ids = row_iota + b * rows
        number = jnp.zeros_like(ids)
        start = jnp.zeros_like(ids)
        prefix = jnp.full(ids.shape, prefix_map[0, 0], jnp.int32)
        for j in range(n_requests):
            past = ids >= ends[j]
            number = number + jnp.where(past, 1, 0)
            start = start + jnp.where(past, lengths[0, j], 0)
            if j + 1 < n_requests:
                prefix = jnp.where(past, prefix_map[0, j + 1], prefix)
        row_prefix[b] = prefix
        distance = LANES + ids - start - lane_iota
        for head in range(2):
            terms = chain(distance, rel_bias, 2 * me + head, 0)
            for r in range(2):
                tail_bias[b, stacked(r, head), :] = terms[r * half : (r + 1) * half]
        for part in range(3):
            other = key_req[pl.ds(0, 1), pl.ds(pl.multiple_of(b * rows + part * LANES, LANES), LANES)]
            same = other == number
            cols = pl.ds(part * LANES, LANES)
            for r in range(2):
                same_half = same[r * half : (r + 1) * half]
                for head in range(2):
                    near_bias[b, stacked(r, head), cols] = jnp.where(
                        same_half, near_bias[0, stacked(r, head), cols], masked_score
                    )

    first_head = lane_iota < DK

    def query_heads(b, r):
        q = q_all[pl.ds(pl.multiple_of(b * rows + r * half, half), half), :]
        nothing = jnp.zeros_like(q)
        first = first_head[:half]
        return jnp.concatenate(
            [jnp.where(first, q, nothing), jnp.where(first, nothing, q)], axis=0
        )

    for copy in own_copies:
        copy.wait()
    for make in (kc_copy, q_copy, vc_copy):
        for copy in incoming(make):
            copy.wait_recv()

    far_bias = jnp.concatenate(
        [jnp.full((half, 1), rel_bias[2 * me + head, 15], jnp.float32) for head in range(2)] * 2, axis=0
    )
    far_keys = PLEN - LANES

    @pl.loop(0, n_req)
    def _(b):
        qh = jnp.concatenate([query_heads(b, 0), query_heads(b, 1)], axis=0)
        choice = row_prefix[b]
        zero_first = jnp.concatenate(
            [choice[:half], choice[:half], choice[half:], choice[half:]], axis=0
        ) == 0
        nothing = jnp.zeros_like(qh)
        q2 = jnp.concatenate(
            [jnp.where(zero_first, qh, nothing), jnp.where(zero_first, nothing, qh)], axis=1
        )
        keys = jnp.concatenate([k_cache[0], k_cache[1]], axis=1)
        scores = lax.dot_general(
            q2, keys, (((1,), (1,)), ((), ())), preferred_element_type=jnp.float32
        )
        scores = jnp.concatenate(
            [scores[:, :far_keys] + far_bias, scores[:, far_keys:] + tail_bias[b]], axis=1
        )
        top = jnp.max(scores, axis=1, keepdims=True)
        terms = jnp.exp(scores - top)
        row_max[b] = jnp.broadcast_to(top, (2 * rows, LANES))
        row_sum[b] = jnp.broadcast_to(jnp.sum(terms, axis=1, keepdims=True), (2 * rows, LANES))
        values = jnp.concatenate([v_cache[0], v_cache[1]], axis=1)
        acc = jnp.dot(terms.astype(jnp.bfloat16), values, preferred_element_type=jnp.float32)
        row_acc[b] = jnp.where(zero_first, acc[:, :LANES], acc[:, LANES:])

    for copy in incoming(kv_copy):
        copy.wait_recv()

    def near(b, r):
        qh = query_heads(b, r)
        window = pl.ds(pl.multiple_of(b * rows, rows), 3 * rows)
        here = pl.ds(r * rows, rows)
        scores = (
            lax.dot_general(
                qh,
                kv_all[0, window, :],
                (((1,), (1,)), ((), ())),
                preferred_element_type=jnp.float32,
            )
            + near_bias[b, here, :]
        )
        old = row_max[b, here, :]
        top = jnp.maximum(old, jnp.max(scores, axis=1, keepdims=True))
        terms = jnp.exp(scores - jnp.concatenate([top, top, top], axis=1))
        shrink = jnp.exp(old - top)
        denom = row_sum[b, here, :] * shrink + jnp.sum(terms, axis=1, keepdims=True)
        acc = row_acc[b, here, :] * shrink + jnp.dot(
            terms.astype(jnp.bfloat16), kv_all[1, window, :], preferred_element_type=jnp.float32
        )
        result = acc / denom
        return jnp.where(first_head[:half], result[:half], result[half:]).astype(jnp.bfloat16)

    for r in range(2):

        @pl.loop(1, n_req)
        def _(d, r=r):
            b = lax.rem(me + d, n_req)
            o_send[b, parts[r], :] = near(b, r)
            o_copy(r)(d, b, me).start()

        att[parts[r], lanes_of(me)] = near(me, r)

    mine = [
        remote(n_two.at[0, parts[r]], n_two.at[1, parts[r]], f_send.at[10 + r], f_recv.at[10 + r], grp=mate)
        for r in range(2)
    ]
    cross = [
        remote(n_two.at[0, parts[r]], n_two.at[2, parts[r]], f_send.at[1 + r], f_recv.at[1 + r], grp=across)
        for r in range(2)
    ]
    relay = [
        remote(n_two.at[2, parts[r]], n_two.at[3, parts[r]], f_send.at[3 + r], f_recv.at[3 + r], grp=mate)
        for r in range(2)
    ]
    back = remote(fast_out, fast_in, f_send.at[5], f_recv.at[5], grp=mate)
    swap = [
        remote(chip_out.at[r], chip_in.at[r], f_send.at[6 + r], f_recv.at[6 + r], grp=mate) for r in range(2)
    ]
    home = [
        remote(far_out.at[r], far_in.at[r], f_send.at[8 + r], f_recv.at[8 + r], grp=across) for r in range(2)
    ]

    loads[4].wait()
    for r in range(2):
        for copy in incoming(o_copy(r)):
            copy.wait_recv()

        @pl.loop(0, D // tile)
        def _(t, r=r):
            cols = pl.ds(pl.multiple_of(t * tile, tile), tile)
            h_one[parts[r], cols] = (
                tok[parts[r], cols].astype(jnp.float32)
                + jnp.dot(
                    att[parts[r], :], w_attn[3, :, cols], preferred_element_type=jnp.float32
                )
            ).astype(jnp.bfloat16)

        wide = h_one[parts[r], :].astype(jnp.float32)
        scale = lax.rsqrt(jnp.mean(wide * wide, axis=-1, keepdims=True) + epsilon)
        n_two[0, parts[r], :] = (wide * scale * mlp_gain[...]).astype(jnp.bfloat16)
        cross[r].start()
        mine[r].start()

    loads[5].wait()
    loads[6].wait()

    def up(rows_in):
        @pl.loop(0, w_in.shape[0] // tile)
        def _(t):
            cols = pl.ds(pl.multiple_of(t * tile, tile), tile)
            units[:, cols] = jnp.maximum(
                lax.dot_general(
                    rows_in,
                    w_in[cols, :],
                    (((1,), (1,)), ((), ())),
                    preferred_element_type=jnp.float32,
                ),
                0.0,
            ).astype(jnp.bfloat16)

    def down(out):
        @pl.loop(0, D // tile)
        def _(t):
            cols = pl.ds(pl.multiple_of(t * tile, tile), tile)
            out[:, cols] = jnp.dot(
                units[...], w_out[:, cols], preferred_element_type=jnp.float32
            ).astype(out.dtype)

    def far_rows(r):
        return jnp.concatenate([n_two[2, parts[r]], n_two[3, parts[r]]], axis=0)

    def send_home(r):
        swap[r].wait_recv()
        far_out[r] = (part_far[r, pl.ds(0, half), :] + chip_in[r].astype(jnp.float32)).astype(jnp.bfloat16)
        home[r].start()

    def finish_far(r):
        down(part_far.at[r])
        chip_out[r] = part_far[r, pl.ds(half, half), :].astype(jnp.bfloat16)
        swap[r].start()

    up(n_two[0])
    cross[0].wait_recv()
    relay[0].start()
    down(part_own)
    for copy in mine:
        copy.wait_recv()
    up(n_two[1])
    down(fast_out)
    back.start()
    cross[1].wait_recv()
    relay[1].start()
    relay[0].wait_recv()
    up(far_rows(0))
    finish_far(0)
    relay[1].wait_recv()
    up(far_rows(1))
    send_home(0)
    finish_far(1)
    back.wait_recv()
    part_own[...] = (
        part_own[...] + h_one[...].astype(jnp.float32) + fast_in[...].astype(jnp.float32)
    )
    send_home(1)
    for r in range(2):
        home[r].wait_recv()
        out_ref[parts[r], :] = (
            part_own[parts[r], :] + far_in[r].astype(jnp.float32)
        ).astype(jnp.bfloat16)

    for make in (kc_copy, vc_copy, q_copy, kv_copy, o_copy(0), o_copy(1)):
        for copy in outgoing(make):
            copy.wait_send()
    for copy in [back] + mine + cross + relay + swap + home:
        copy.wait_send()


def fused(
    tokens,
    attn_gain,
    w_query,
    w_key,
    w_value,
    w_attn_out,
    rel_bias,
    prefix_cache,
    lengths,
    prefix_map,
    mlp_gain,
    w_in,
    w_out,
):
    n_req = lax.axis_size("req")
    rows = tokens.shape[0]
    group = n_req * rows
    hbm = pl.BlockSpec(memory_space=pl.ANY)
    vmem = pl.BlockSpec(memory_space=pltpu.VMEM)
    smem = pl.BlockSpec(memory_space=pltpu.SMEM)
    half = rows // 2
    bf16, f32 = jnp.bfloat16, jnp.float32
    sems = pltpu.SemaphoreType.DMA
    return pl.pallas_call(
        functools.partial(layer_kernel, n_req),
        out_shape=jax.ShapeDtypeStruct((rows, D), bf16),
        in_specs=[hbm, vmem, hbm, hbm, hbm, hbm, smem, hbm, smem, smem, vmem, hbm, hbm],
        out_specs=vmem,
        scratch_shapes=[
            pltpu.VMEM((rows, D), bf16),
            pltpu.VMEM((4, D, D), bf16),
            pltpu.VMEM(w_in.shape, bf16),
            pltpu.VMEM(w_out.shape, bf16),
            pltpu.VMEM((rows, D), bf16),
            pltpu.VMEM((3, rows, D), bf16),
            pltpu.VMEM((PREF_GRP, PLEN, LANES), bf16),
            pltpu.VMEM((PREF_GRP, PLEN, LANES), bf16),
            pltpu.VMEM((group, LANES), bf16),
            pltpu.VMEM((2, group + 2 * rows, LANES), bf16),
            pltpu.VMEM((n_req, 2 * rows, LANES), f32),
            pltpu.VMEM((n_req, 2 * rows, 3 * LANES), f32),
            pltpu.VMEM((8, group + 2 * rows), jnp.int32),
            pltpu.VMEM((n_req, rows, LANES), jnp.int32),
            pltpu.VMEM((n_req, 2 * rows, LANES), f32),
            pltpu.VMEM((n_req, 2 * rows, LANES), f32),
            pltpu.VMEM((n_req, 2 * rows, LANES), f32),
            pltpu.VMEM((n_req, rows, LANES), bf16),
            pltpu.VMEM((rows, D), bf16),
            pltpu.VMEM((rows, D), bf16),
            pltpu.VMEM((4, rows, D), bf16),
            pltpu.VMEM((rows, w_in.shape[0]), bf16),
            pltpu.VMEM((rows, D), f32),
            pltpu.VMEM((2, rows, D), f32),
            pltpu.VMEM((rows, D), bf16),
            pltpu.VMEM((rows, D), bf16),
            pltpu.VMEM((2, half, D), bf16),
            pltpu.VMEM((2, half, D), bf16),
            pltpu.VMEM((2, half, D), bf16),
            pltpu.VMEM((2, half, D), bf16),
            sems((7,)),
            sems((2,)),
        ]
        + [sems((n_req,)) for _ in range(8)]
        + [sems((2, n_req)) for _ in range(2)]
        + [sems((12,)), sems((12,))],
        compiler_params=pltpu.CompilerParams(
            collective_id=0, has_side_effects=True, vmem_limit_bytes=63 * 1024 * 1024
        ),
    )(
        tokens,
        attn_gain.reshape(1, D),
        w_query,
        w_key,
        w_value,
        w_attn_out,
        rel_bias.T,
        prefix_cache,
        lengths,
        prefix_map,
        mlp_gain.reshape(1, D),
        w_in,
        w_out,
    )


def pairs_fit(mesh):
    return mesh.shape["req"] * LANES == D and mesh.shape["grp"] == 4


def solution(mesh):
    return jax.shard_map(
        fused if pairs_fit(mesh) else body,
        mesh=mesh,
        in_specs=(
            P(("grp", "req"), None),
            P(),
            P(),
            P(),
            P(),
            P(),
            P(),
            P("grp", "req", None),
            P("grp", None),
            P("grp", None),
            P(),
            P("grp", None),
            P("grp", None),
        ),
        out_specs=P(("grp", "req"), None),
        check_vma=False,
    )
```

```python
import functools

import jax
import jax.numpy as jnp
from jax import lax
from jax.experimental import pallas as pl
from jax.experimental.pallas import tpu as pltpu
from jax.sharding import PartitionSpec as P

D = 1024
H = 16
DK = 64
PLEN = 512
PREF_GRP = 2
LANES = 128
MESH = pl.DeviceIdType.MESH


epsilon = 1e-06
far_marks = (12, 16, 23, 32, 46, 64, 91)
masked_score = -1e30


def padded(value, sides, width):
    for axis, dim in sides:
        count, length = (lax.axis_size(axis), value.shape[dim])
        up = [(i, (i + 1) % count) for i in range(count - 1)]
        down = [(j, i) for i, j in up]
        last = lax.slice_in_dim(value, length - width, length, axis=dim)
        leading = lax.slice_in_dim(value, 0, width, axis=dim)
        before = lax.ppermute(last, axis, up)
        after = lax.ppermute(leading, axis, down)
        value = jnp.concatenate([before, value, after], axis=dim)
    return value


def bucket_of(relative):
    distance = jnp.abs(relative)
    far_bucket = 8 + sum([(distance >= threshold).astype(jnp.int32) for threshold in far_marks])
    bucket = jnp.where(distance < 8, distance, far_bucket)
    return bucket + jnp.where(relative > 0, 16, 0)


def bias_lookup(relative, rel_bias):
    buckets = bucket_of(relative)
    marks = jnp.arange(rel_bias.shape[0], dtype=jnp.int32)
    one_hot = (buckets[:, :, None] == marks[None, None, :]).astype(jnp.float32)
    return jnp.einsum(
        "qkb,bh->hqk",
        one_hot,
        rel_bias,
        precision=lax.Precision.HIGHEST,
        preferred_element_type=jnp.float32,
    )


def norm_rows(values_in, gain):
    widened = values_in.astype(jnp.float32)
    scale = lax.rsqrt(jnp.mean(widened * widened, axis=-1, keepdims=True) + epsilon)
    return (widened * scale * gain).astype(jnp.bfloat16)


def layout(lengths_row, prefix_row, row_ids):
    req_ends = jnp.cumsum(lengths_row)
    req_starts = req_ends - lengths_row
    member = (
        (row_ids[:, None] >= req_starts[None, :]) & (row_ids[:, None] < req_ends[None, :])
    ).astype(jnp.int32)
    numbers = jnp.arange(lengths_row.shape[0], dtype=jnp.int32)
    req_index = jnp.sum(member * numbers[None, :], axis=1) + jnp.sum(member, axis=1) - 1
    offset = row_ids - jnp.sum(member * req_starts[None, :], axis=1)
    chosen = jnp.sum(member * prefix_row[None, :], axis=1)
    return (req_index, offset, chosen)


def softmax_part(scores, value_rows, allowed):
    scores = jnp.where(allowed[None], scores, masked_score)
    row_max = jnp.max(scores, axis=2)
    exp_terms = jnp.where(allowed[None], jnp.exp(scores - row_max[:, :, None]), 0.0)
    row_sum = jnp.sum(exp_terms, axis=2)
    weighted = jnp.einsum(
        "hqk,khd->hqd",
        exp_terms.astype(jnp.bfloat16),
        value_rows,
        preferred_element_type=jnp.float32,
    )
    return (row_max, row_sum, weighted)


def combine(first_part, second_part):
    row_max = jnp.maximum(first_part[0], second_part[0])
    scale_one = jnp.exp(first_part[0] - row_max)
    scale_two = jnp.exp(second_part[0] - row_max)
    row_sum = first_part[1] * scale_one + second_part[1] * scale_two
    weighted = first_part[2] * scale_one[:, :, None] + second_part[2] * scale_two[:, :, None]
    return (row_max, row_sum, weighted)


def feed_forward(rows_in, in_part, out_part):
    units = lax.dot_general(
        rows_in, in_part, (((1,), (1,)), ((), ())), preferred_element_type=jnp.float32
    )
    units = jnp.maximum(units, 0.0).astype(jnp.bfloat16)
    return jnp.dot(units, out_part, preferred_element_type=jnp.float32)


def body(
    tokens,
    attn_gain,
    w_query,
    w_key,
    w_value,
    w_attn_out,
    rel_bias,
    prefix_cache,
    lengths,
    prefix_map,
    mlp_gain,
    w_in,
    w_out,
):
    rows_here = tokens.shape[0]
    device_pos = lax.axis_index("req")
    group_lengths = lengths[0]
    group_map = prefix_map[0]
    normed = norm_rows(tokens, attn_gain)
    query = (
        jnp.dot(normed, w_query, preferred_element_type=jnp.float32)
        .astype(jnp.bfloat16)
        .reshape(rows_here, H, DK)
    )
    key_value = jnp.concatenate(
        [
            jnp.dot(normed, w_key, preferred_element_type=jnp.float32).astype(jnp.bfloat16),
            jnp.dot(normed, w_value, preferred_element_type=jnp.float32).astype(jnp.bfloat16),
        ],
        axis=1,
    )
    query_ids = device_pos * rows_here + jnp.arange(rows_here, dtype=jnp.int32)
    query_req, query_offset, query_prefix = layout(group_lengths, group_map, query_ids)
    all_positions = jnp.arange(PLEN, dtype=jnp.int32)
    prefix_bias = bias_lookup(all_positions[None, :] - PLEN - query_offset[:, None], rel_bias)
    empty_state = (
        jnp.full((H, rows_here), masked_score, jnp.float32),
        jnp.zeros((H, rows_here), jnp.float32),
        jnp.zeros((H, rows_here, DK), jnp.float32),
    )
    running = empty_state
    shard_kv = lax.all_gather(prefix_cache, "req", axis=1, tiled=True)
    prefix_ids = jnp.arange(PREF_GRP, dtype=jnp.int32)
    slices = shard_kv.shape[0]
    piece_len = shard_kv.shape[1]
    step_len = max(min(piece_len, 512 // slices), 1)
    for begin in range(0, piece_len, step_len):
        width = min(step_len, piece_len - begin)
        block = shard_kv[:, begin : begin + width]
        key_rows = block[:, :, :D].reshape(slices, width, H, DK)
        value_rows = block[:, :, D:].reshape(-1, H, DK)
        rel_terms = lax.dynamic_slice_in_dim(prefix_bias, begin, width, 2)
        prefix_scores = jnp.einsum(
            "qhd,swhd->hqsw", query, key_rows, preferred_element_type=jnp.float32
        )
        prefix_scores = (prefix_scores + rel_terms[:, :, None, :]).reshape(
            H, rows_here, slices * width
        )
        allowed = jnp.repeat(query_prefix[:, None] == prefix_ids[None, :], width, axis=1)
        running = combine(running, softmax_part(prefix_scores, value_rows, allowed))
    state = running
    window = padded(key_value, (("req", 0),), rows_here)
    window_ids = device_pos * rows_here - rows_here + jnp.arange(3 * rows_here, dtype=jnp.int32)
    window_req = layout(group_lengths, group_map, window_ids)[0]
    for part_idx in range(3):
        part_rows = window[part_idx * rows_here : (part_idx + 1) * rows_here]
        part_ids = window_ids[part_idx * rows_here : (part_idx + 1) * rows_here]
        part_req = window_req[part_idx * rows_here : (part_idx + 1) * rows_here]
        suffix_terms = bias_lookup(part_ids[None, :] - query_ids[:, None], rel_bias)
        suffix_allowed = part_req[None, :] == query_req[:, None]
        scores = (
            jnp.einsum(
                "qhd,khd->hqk",
                query,
                part_rows[:, :D].reshape(-1, H, DK),
                preferred_element_type=jnp.float32,
            )
            + suffix_terms
        )
        suffix_state = softmax_part(scores, part_rows[:, D:].reshape(-1, H, DK), suffix_allowed)
        state = combine(state, suffix_state)
    attended = (
        (state[2] / state[1][:, :, None])
        .transpose(1, 0, 2)
        .reshape(rows_here, D)
        .astype(jnp.bfloat16)
    )
    hidden_one = (
        tokens.astype(jnp.float32)
        + jnp.dot(attended, w_attn_out, preferred_element_type=jnp.float32)
    ).astype(jnp.bfloat16)
    normed_two = norm_rows(hidden_one, mlp_gain)
    gathered = lax.all_gather(normed_two, "grp", axis=0, tiled=True)
    mlp_total = lax.psum_scatter(
        feed_forward(gathered, w_in, w_out).astype(jnp.bfloat16),
        "grp",
        scatter_dimension=0,
        tiled=True,
    ).astype(jnp.float32)
    return (hidden_one.astype(jnp.float32) + mlp_total).astype(jnp.bfloat16)


def bucket_steps():
    return tuple((i, i) for i in range(1, 9)) + tuple((t, 9 + i) for i, t in enumerate(far_marks))


def chain(distance, table, head, first):
    value = jnp.full(distance.shape, table[head, first], jnp.float32)
    for threshold, number in bucket_steps():
        value = jnp.where(distance >= threshold, table[head, first + number], value)
    return value


def layer_kernel(
    n_req,
    tokens_hbm,
    attn_gain,
    wq_hbm,
    wk_hbm,
    wv_hbm,
    wo_hbm,
    rel_bias,
    cache_hbm,
    lengths,
    prefix_map,
    mlp_gain,
    win_hbm,
    wout_hbm,
    out_ref,
    tok,
    w_attn,
    w_in,
    w_out,
    normed,
    stage,
    k_cache,
    v_cache,
    q_all,
    k_side,
    k_all,
    v_all,
    k_cross,
    w_up,
    tail_bias,
    near_bias,
    key_req,
    row_prefix,
    row_max,
    row_sum,
    row_acc,
    o_send,
    att,
    h_one,
    n_two,
    units,
    part_own,
    part_far,
    fast_out,
    fast_in,
    chip_out,
    chip_in,
    far_out,
    far_in,
    load_sem,
    own_sem,
    kc_send,
    kc_recv,
    vc_send,
    vc_recv,
    q_send,
    q_recv,
    k_send,
    k_recv,
    v_send,
    v_recv,
    o_ssem,
    o_rsem,
    f_send,
    f_recv,
):
    me = lax.axis_index("req")
    grp = lax.axis_index("grp")
    side = lax.rem(grp, 2)
    plane = lax.div(grp, 2)
    mate = plane * 2 + (1 - side)
    across = (1 - plane) * 2 + side
    rows = tokens_hbm.shape[0]
    piece = cache_hbm.shape[1]
    half = rows // 2

    def remote(src, dst, ssem, rsem, **where):
        return pltpu.make_async_remote_copy(
            src_ref=src, dst_ref=dst, send_sem=ssem, recv_sem=rsem, device_id=where, device_id_type=MESH
        )

    def lanes_of(index):
        return pl.ds(pl.multiple_of(index * LANES, LANES), LANES)

    def rows_of(index):
        return pl.ds(pl.multiple_of(index * rows, rows), rows)

    loads = [
        pltpu.make_async_copy(src, dst, load_sem.at[i])
        for i, (src, dst) in enumerate(
            [
                (tokens_hbm, tok),
                (wq_hbm, w_attn.at[0]),
                (wk_hbm, w_attn.at[1]),
                (wv_hbm, w_attn.at[2]),
                (wo_hbm, w_attn.at[3]),
                (win_hbm, w_in),
                (wout_hbm, w_out),
            ]
        )
    ]
    for load in loads[:4]:
        load.start()

    barrier = pltpu.get_barrier_semaphore()
    for d in range(1, n_req):
        pl.semaphore_signal(
            barrier, inc=1, device_id={"req": lax.rem(me + d, n_req)}, device_id_type=MESH
        )
    for other in (mate, across):
        pl.semaphore_signal(barrier, inc=1, device_id={"grp": other}, device_id_type=MESH)
    pl.semaphore_wait(barrier, n_req + 1)

    def cache_copy(buf, first, sends, recvs, d, peer, owner):
        return remote(
            cache_hbm.at[:, :, pl.ds(pl.multiple_of(first + peer * LANES, LANES), LANES)],
            buf.at[:, pl.ds(pl.multiple_of(owner * piece, piece), piece), :],
            sends.at[d],
            recvs.at[d],
            req=peer,
        )

    def q_copy(d, peer, owner):
        return remote(
            stage.at[0, :, lanes_of(peer)], q_all.at[rows_of(owner), :], q_send.at[d], q_recv.at[d], req=peer
        )

    def k_copy(d, peer, owner):
        return remote(
            k_side.at[lanes_of(peer), :], k_all.at[:, lanes_of(owner + 1)], k_send.at[d], k_recv.at[d], req=peer
        )

    def v_copy(d, peer, owner):
        return remote(
            stage.at[1, :, lanes_of(peer)], v_all.at[rows_of(owner + 1), :], v_send.at[d], v_recv.at[d], req=peer
        )

    parts = [pl.ds(r * half, half) for r in range(2)]

    def o_copy(r):
        def make(d, peer, owner):
            return remote(
                o_send.at[peer, parts[r]],
                att.at[parts[r], lanes_of(owner)],
                o_ssem.at[r, d],
                o_rsem.at[r, d],
                req=peer,
            )

        return make

    def outgoing(make):
        return [make(d, lax.rem(me + d, n_req), me) for d in range(1, n_req)]

    def incoming(make):
        return [
            make(d, lax.rem(me + d, n_req), lax.rem(me + n_req - d, n_req)) for d in range(1, n_req)
        ]

    def kc_copy(d, peer, owner):
        return cache_copy(k_cache, 0, kc_send, kc_recv, d, peer, owner)

    def vc_copy(d, peer, owner):
        return cache_copy(v_cache, D, vc_send, vc_recv, d, peer, owner)

    for copy in outgoing(kc_copy) + outgoing(vc_copy):
        copy.start()
    own_copies = [
        pltpu.make_async_copy(
            cache_hbm.at[:, :, pl.ds(pl.multiple_of(first + me * LANES, LANES), LANES)],
            buf.at[:, pl.ds(pl.multiple_of(me * piece, piece), piece), :],
            own_sem.at[i],
        )
        for i, (buf, first) in enumerate([(k_cache, 0), (v_cache, D)])
    ]
    for copy in own_copies:
        copy.start()

    loads[0].wait()
    wide = tok[...].astype(jnp.float32)
    scale = lax.rsqrt(jnp.mean(wide * wide, axis=-1, keepdims=True) + epsilon)
    normed[...] = (wide * scale * attn_gain[...]).astype(jnp.bfloat16)

    tile = 512
    makers = (q_copy, k_copy, v_copy)
    for part in range(3):
        loads[1 + part].wait()

        @pl.loop(0, D // tile)
        def _(t, part=part):
            cols = pl.ds(pl.multiple_of(t * tile, tile), tile)
            made = jnp.dot(
                normed[...], w_attn[part, :, cols], preferred_element_type=jnp.float32
            ).astype(jnp.bfloat16)
            if part == 1:
                k_side[cols, :] = made.T
            else:
                stage[part // 2, :, cols] = made

        for copy in outgoing(makers[part]):
            copy.start()
        if part == 0:
            for load in loads[4:]:
                load.start()
    q_all[rows_of(me), :] = stage[0, :, lanes_of(me)]
    k_all[:, lanes_of(me + 1)] = k_side[lanes_of(me), :]
    v_all[rows_of(me + 1), :] = stage[1, :, lanes_of(me)]
    zeros = jnp.zeros((rows, LANES), jnp.bfloat16)
    for outer in (0, n_req + 1):
        k_all[:, pl.ds(outer * rows, rows)] = zeros
        v_all[pl.ds(outer * rows, rows), :] = zeros

    ends = []
    total = 0
    n_requests = lengths.shape[1]
    for j in range(n_requests):
        total = total + lengths[0, j]
        ends.append(total)
    key_ids = lax.broadcasted_iota(jnp.int32, key_req.shape, 1) - rows
    key_number = jnp.where(key_ids < 0, -1, 0)
    for end in ends:
        key_number = key_number + jnp.where(key_ids >= end, 1, 0)
    key_req[...] = key_number

    def stacked(r, head):
        return pl.ds((2 * r + head) * half, half)

    row_iota = lax.broadcasted_iota(jnp.int32, (rows, LANES), 0)
    lane_iota = lax.broadcasted_iota(jnp.int32, (rows, LANES), 1)
    for head in range(2):
        for part in range(3):
            ahead = lane_iota + (part - 1) * rows - row_iota
            distance = jnp.abs(ahead)
            before = chain(distance, rel_bias, 2 * me + head, 0)
            after = chain(distance, rel_bias, 2 * me + head, 16)
            both = jnp.where(ahead > 0, after, before)
            for r in range(2):
                near_bias[0, stacked(r, head), pl.ds(part * LANES, LANES)] = both[r * half : (r + 1) * half]

    @pl.loop(0, n_req)
    def _(step):
        b = n_req - 1 - step
        ids = row_iota + b * rows
        number = jnp.zeros_like(ids)
        start = jnp.zeros_like(ids)
        prefix = jnp.full(ids.shape, prefix_map[0, 0], jnp.int32)
        for j in range(n_requests):
            past = ids >= ends[j]
            number = number + jnp.where(past, 1, 0)
            start = start + jnp.where(past, lengths[0, j], 0)
            if j + 1 < n_requests:
                prefix = jnp.where(past, prefix_map[0, j + 1], prefix)
        row_prefix[b] = prefix
        distance = LANES + ids - start - lane_iota
        for head in range(2):
            terms = chain(distance, rel_bias, 2 * me + head, 0)
            for r in range(2):
                tail_bias[b, stacked(r, head), :] = terms[r * half : (r + 1) * half]
        for part in range(3):
            other = key_req[pl.ds(0, 1), pl.ds(pl.multiple_of(b * rows + part * LANES, LANES), LANES)]
            same = other == number
            cols = pl.ds(part * LANES, LANES)
            for r in range(2):
                same_half = same[r * half : (r + 1) * half]
                for head in range(2):
                    near_bias[b, stacked(r, head), cols] = jnp.where(
                        same_half, near_bias[0, stacked(r, head), cols], masked_score
                    )

    loads[5].wait()

    @pl.loop(0, w_in.shape[0] // tile)
    def _(t):
        cols = pl.ds(pl.multiple_of(t * tile, tile), tile)
        w_up[:, cols] = w_in[cols, :].T

    first_head = lane_iota < DK

    def query_heads(b, r):
        q = q_all[pl.ds(pl.multiple_of(b * rows + r * half, half), half), :]
        nothing = jnp.zeros_like(q)
        first = first_head[:half]
        return jnp.concatenate(
            [jnp.where(first, q, nothing), jnp.where(first, nothing, q)], axis=0
        )

    for copy in own_copies:
        copy.wait()
    for copy in incoming(kc_copy):
        copy.wait_recv()
    for which in range(PREF_GRP):
        k_cross[pl.ds(which * LANES, LANES), :] = k_cache[which].T
    for make in (q_copy, vc_copy):
        for copy in incoming(make):
            copy.wait_recv()

    far_bias = jnp.concatenate(
        [jnp.full((half, 1), rel_bias[2 * me + head, 15], jnp.float32) for head in range(2)] * 2, axis=0
    )
    far_keys = PLEN - LANES

    def far_scores(b):
        qh = jnp.concatenate([query_heads(b, 0), query_heads(b, 1)], axis=0)
        choice = row_prefix[b]
        zero_first = (
            jnp.concatenate([choice[:half], choice[:half], choice[half:], choice[half:]], axis=0) == 0
        )
        nothing = jnp.zeros_like(qh)
        q2 = jnp.concatenate(
            [jnp.where(zero_first, qh, nothing), jnp.where(zero_first, nothing, qh)], axis=1
        )
        scores = jnp.dot(q2, k_cross[...], preferred_element_type=jnp.float32)
        scores = jnp.concatenate(
            [scores[:, :far_keys] + far_bias, scores[:, far_keys:] + tail_bias[b]], axis=1
        )
        return zero_first, scores

    def far_terms(scores):
        top = jnp.max(scores, axis=1, keepdims=True)
        terms = jnp.exp(scores - top)
        return top, jnp.sum(terms, axis=1, keepdims=True), terms.astype(jnp.bfloat16)

    far_step = 2

    @pl.loop(0, n_req // far_step)
    def _(step):
        blocks = [step * far_step + i for i in range(far_step)]
        values = jnp.concatenate([v_cache[0], v_cache[1]], axis=1)
        scored = [far_scores(b) for b in blocks]
        termed = [far_terms(scores) for _, scores in scored]
        accs = [jnp.dot(t[2], values, preferred_element_type=jnp.float32) for t in termed]
        for b, (zero_first, _), (top, total, _), acc in zip(blocks, scored, termed, accs):
            row_max[b] = jnp.broadcast_to(top, (2 * rows, LANES))
            row_sum[b] = jnp.broadcast_to(total, (2 * rows, LANES))
            row_acc[b] = jnp.where(zero_first, acc[:, :LANES], acc[:, LANES:])

    for make in (k_copy, v_copy):
        for copy in incoming(make):
            copy.wait_recv()

    def near(blocks, r):
        here = pl.ds(r * rows, rows)
        windows = [pl.ds(pl.multiple_of(b * rows, rows), 3 * rows) for b in blocks]
        scores = [
            jnp.dot(query_heads(b, r), k_all[:, w], preferred_element_type=jnp.float32)
            + near_bias[b, here, :]
            for b, w in zip(blocks, windows)
        ]
        olds = [row_max[b, here, :] for b in blocks]
        tops = [jnp.maximum(o, jnp.max(x, axis=1, keepdims=True)) for o, x in zip(olds, scores)]
        terms = [jnp.exp(x - jnp.concatenate([t, t, t], axis=1)) for x, t in zip(scores, tops)]
        shrinks = [jnp.exp(o - t) for o, t in zip(olds, tops)]
        sums = [
            row_sum[b, here, :] * z + jnp.sum(x, axis=1, keepdims=True)
            for b, z, x in zip(blocks, shrinks, terms)
        ]
        accs = [
            row_acc[b, here, :] * z
            + jnp.dot(x.astype(jnp.bfloat16), v_all[w, :], preferred_element_type=jnp.float32)
            for b, z, x, w in zip(blocks, shrinks, terms, windows)
        ]
        results = [a / x for a, x in zip(accs, sums)]
        return [jnp.where(first_head[:half], x[:half], x[half:]).astype(jnp.bfloat16) for x in results]

    near_step = 4
    for r in range(2):
        for begin in range(1, n_req + 1, near_step):
            turns = range(begin, begin + near_step)
            blocks = [lax.rem(me + d, n_req) for d in turns]
            for d, b, result in zip(turns, blocks, near(blocks, r)):
                if d < n_req:
                    o_send[b, parts[r], :] = result
                else:
                    att[parts[r], lanes_of(me)] = result
            for d, b in zip(turns, blocks):
                if d < n_req:
                    o_copy(r)(d, b, me).start()

    mine = [
        remote(n_two.at[0, parts[r]], n_two.at[1, parts[r]], f_send.at[10 + r], f_recv.at[10 + r], grp=mate)
        for r in range(2)
    ]
    cross = [
        remote(n_two.at[0, parts[r]], n_two.at[2, parts[r]], f_send.at[1 + r], f_recv.at[1 + r], grp=across)
        for r in range(2)
    ]
    relay = [
        remote(n_two.at[2, parts[r]], n_two.at[3, parts[r]], f_send.at[3 + r], f_recv.at[3 + r], grp=mate)
        for r in range(2)
    ]
    back = remote(fast_out, fast_in, f_send.at[5], f_recv.at[5], grp=mate)
    swap = [
        remote(chip_out.at[r], chip_in.at[r], f_send.at[6 + r], f_recv.at[6 + r], grp=mate) for r in range(2)
    ]
    home = [
        remote(far_out.at[r], far_in.at[r], f_send.at[8 + r], f_recv.at[8 + r], grp=across) for r in range(2)
    ]

    loads[4].wait()
    for r in range(2):
        for copy in incoming(o_copy(r)):
            copy.wait_recv()

        @pl.loop(0, D // tile)
        def _(t, r=r):
            cols = pl.ds(pl.multiple_of(t * tile, tile), tile)
            h_one[parts[r], cols] = (
                tok[parts[r], cols].astype(jnp.float32)
                + jnp.dot(
                    att[parts[r], :], w_attn[3, :, cols], preferred_element_type=jnp.float32
                )
            ).astype(jnp.bfloat16)

        wide = h_one[parts[r], :].astype(jnp.float32)
        scale = lax.rsqrt(jnp.mean(wide * wide, axis=-1, keepdims=True) + epsilon)
        n_two[0, parts[r], :] = (wide * scale * mlp_gain[...]).astype(jnp.bfloat16)
        cross[r].start()
        mine[r].start()

    loads[6].wait()

    def up(rows_in):
        @pl.loop(0, w_in.shape[0] // tile)
        def _(t):
            cols = pl.ds(pl.multiple_of(t * tile, tile), tile)
            units[:, cols] = jnp.maximum(
                jnp.dot(rows_in, w_up[:, cols], preferred_element_type=jnp.float32), 0.0
            ).astype(jnp.bfloat16)

    def down(out):
        @pl.loop(0, D // tile)
        def _(t):
            cols = pl.ds(pl.multiple_of(t * tile, tile), tile)
            out[:, cols] = jnp.dot(
                units[...], w_out[:, cols], preferred_element_type=jnp.float32
            ).astype(out.dtype)

    def far_rows(r):
        return jnp.concatenate([n_two[2, parts[r]], n_two[3, parts[r]]], axis=0)

    def send_home(r):
        swap[r].wait_recv()
        far_out[r] = (part_far[r, pl.ds(0, half), :] + chip_in[r].astype(jnp.float32)).astype(jnp.bfloat16)
        home[r].start()

    def finish_far(r):
        down(part_far.at[r])
        chip_out[r] = part_far[r, pl.ds(half, half), :].astype(jnp.bfloat16)
        swap[r].start()

    up(n_two[0])
    cross[0].wait_recv()
    relay[0].start()
    down(part_own)
    for copy in mine:
        copy.wait_recv()
    up(n_two[1])
    down(fast_out)
    back.start()
    cross[1].wait_recv()
    relay[1].start()
    relay[0].wait_recv()
    up(far_rows(0))
    finish_far(0)
    relay[1].wait_recv()
    up(far_rows(1))
    send_home(0)
    finish_far(1)
    back.wait_recv()
    part_own[...] = (
        part_own[...] + h_one[...].astype(jnp.float32) + fast_in[...].astype(jnp.float32)
    )
    send_home(1)
    for r in range(2):
        home[r].wait_recv()
        out_ref[parts[r], :] = (
            part_own[parts[r], :] + far_in[r].astype(jnp.float32)
        ).astype(jnp.bfloat16)

    for make in (kc_copy, vc_copy, q_copy, k_copy, v_copy, o_copy(0), o_copy(1)):
        for copy in outgoing(make):
            copy.wait_send()
    for copy in [back] + mine + cross + relay + swap + home:
        copy.wait_send()


def fused(
    tokens,
    attn_gain,
    w_query,
    w_key,
    w_value,
    w_attn_out,
    rel_bias,
    prefix_cache,
    lengths,
    prefix_map,
    mlp_gain,
    w_in,
    w_out,
):
    n_req = lax.axis_size("req")
    rows = tokens.shape[0]
    group = n_req * rows
    hbm = pl.BlockSpec(memory_space=pl.ANY)
    vmem = pl.BlockSpec(memory_space=pltpu.VMEM)
    smem = pl.BlockSpec(memory_space=pltpu.SMEM)
    half = rows // 2
    bf16, f32 = jnp.bfloat16, jnp.float32
    sems = pltpu.SemaphoreType.DMA
    return pl.pallas_call(
        functools.partial(layer_kernel, n_req),
        out_shape=jax.ShapeDtypeStruct((rows, D), bf16),
        in_specs=[hbm, vmem, hbm, hbm, hbm, hbm, smem, hbm, smem, smem, vmem, hbm, hbm],
        out_specs=vmem,
        scratch_shapes=[
            pltpu.VMEM((rows, D), bf16),
            pltpu.VMEM((4, D, D), bf16),
            pltpu.VMEM(w_in.shape, bf16),
            pltpu.VMEM(w_out.shape, bf16),
            pltpu.VMEM((rows, D), bf16),
            pltpu.VMEM((2, rows, D), bf16),
            pltpu.VMEM((PREF_GRP, PLEN, LANES), bf16),
            pltpu.VMEM((PREF_GRP, PLEN, LANES), bf16),
            pltpu.VMEM((group, LANES), bf16),
            pltpu.VMEM((D, rows), bf16),
            pltpu.VMEM((LANES, group + 2 * rows), bf16),
            pltpu.VMEM((group + 2 * rows, LANES), bf16),
            pltpu.VMEM((PREF_GRP * LANES, PLEN), bf16),
            pltpu.VMEM(w_in.shape[::-1], bf16),
            pltpu.VMEM((n_req, 2 * rows, LANES), f32),
            pltpu.VMEM((n_req, 2 * rows, 3 * LANES), f32),
            pltpu.VMEM((8, group + 2 * rows), jnp.int32),
            pltpu.VMEM((n_req, rows, LANES), jnp.int32),
            pltpu.VMEM((n_req, 2 * rows, LANES), f32),
            pltpu.VMEM((n_req, 2 * rows, LANES), f32),
            pltpu.VMEM((n_req, 2 * rows, LANES), f32),
            pltpu.VMEM((n_req, rows, LANES), bf16),
            pltpu.VMEM((rows, D), bf16),
            pltpu.VMEM((rows, D), bf16),
            pltpu.VMEM((4, rows, D), bf16),
            pltpu.VMEM((rows, w_in.shape[0]), bf16),
            pltpu.VMEM((rows, D), f32),
            pltpu.VMEM((2, rows, D), f32),
            pltpu.VMEM((rows, D), bf16),
            pltpu.VMEM((rows, D), bf16),
            pltpu.VMEM((2, half, D), bf16),
            pltpu.VMEM((2, half, D), bf16),
            pltpu.VMEM((2, half, D), bf16),
            pltpu.VMEM((2, half, D), bf16),
            sems((7,)),
            sems((2,)),
        ]
        + [sems((n_req,)) for _ in range(10)]
        + [sems((2, n_req)) for _ in range(2)]
        + [sems((12,)), sems((12,))],
        compiler_params=pltpu.CompilerParams(
            collective_id=0, has_side_effects=True, vmem_limit_bytes=63 * 1024 * 1024
        ),
    )(
        tokens,
        attn_gain.reshape(1, D),
        w_query,
        w_key,
        w_value,
        w_attn_out,
        rel_bias.T,
        prefix_cache,
        lengths,
        prefix_map,
        mlp_gain.reshape(1, D),
        w_in,
        w_out,
    )


def pairs_fit(mesh):
    return mesh.shape["req"] * LANES == D and mesh.shape["grp"] == 4


def solution(mesh):
    return jax.shard_map(
        fused if pairs_fit(mesh) else body,
        mesh=mesh,
        in_specs=(
            P(("grp", "req"), None),
            P(),
            P(),
            P(),
            P(),
            P(),
            P(),
            P("grp", "req", None),
            P("grp", None),
            P("grp", None),
            P(),
            P("grp", None),
            P("grp", None),
        ),
        out_specs=P(("grp", "req"), None),
        check_vma=False,
    )
```

```python
import functools

import jax
import jax.numpy as jnp
from jax import lax
from jax.experimental import pallas as pl
from jax.experimental.pallas import tpu as pltpu
from jax.sharding import PartitionSpec as P

D = 1024
H = 16
DK = 64
PLEN = 512
PREF_GRP = 2
LANES = 128
MESH = pl.DeviceIdType.MESH


epsilon = 1e-06
far_marks = (12, 16, 23, 32, 46, 64, 91)
masked_score = -1e30


def padded(value, sides, width):
    for axis, dim in sides:
        count, length = (lax.axis_size(axis), value.shape[dim])
        up = [(i, (i + 1) % count) for i in range(count - 1)]
        down = [(j, i) for i, j in up]
        last = lax.slice_in_dim(value, length - width, length, axis=dim)
        leading = lax.slice_in_dim(value, 0, width, axis=dim)
        before = lax.ppermute(last, axis, up)
        after = lax.ppermute(leading, axis, down)
        value = jnp.concatenate([before, value, after], axis=dim)
    return value


def bucket_of(relative):
    distance = jnp.abs(relative)
    far_bucket = 8 + sum([(distance >= threshold).astype(jnp.int32) for threshold in far_marks])
    bucket = jnp.where(distance < 8, distance, far_bucket)
    return bucket + jnp.where(relative > 0, 16, 0)


def bias_lookup(relative, rel_bias):
    buckets = bucket_of(relative)
    marks = jnp.arange(rel_bias.shape[0], dtype=jnp.int32)
    one_hot = (buckets[:, :, None] == marks[None, None, :]).astype(jnp.float32)
    return jnp.einsum(
        "qkb,bh->hqk",
        one_hot,
        rel_bias,
        precision=lax.Precision.HIGHEST,
        preferred_element_type=jnp.float32,
    )


def norm_rows(values_in, gain):
    widened = values_in.astype(jnp.float32)
    scale = lax.rsqrt(jnp.mean(widened * widened, axis=-1, keepdims=True) + epsilon)
    return (widened * scale * gain).astype(jnp.bfloat16)


def layout(lengths_row, prefix_row, row_ids):
    req_ends = jnp.cumsum(lengths_row)
    req_starts = req_ends - lengths_row
    member = (
        (row_ids[:, None] >= req_starts[None, :]) & (row_ids[:, None] < req_ends[None, :])
    ).astype(jnp.int32)
    numbers = jnp.arange(lengths_row.shape[0], dtype=jnp.int32)
    req_index = jnp.sum(member * numbers[None, :], axis=1) + jnp.sum(member, axis=1) - 1
    offset = row_ids - jnp.sum(member * req_starts[None, :], axis=1)
    chosen = jnp.sum(member * prefix_row[None, :], axis=1)
    return (req_index, offset, chosen)


def softmax_part(scores, value_rows, allowed):
    scores = jnp.where(allowed[None], scores, masked_score)
    row_max = jnp.max(scores, axis=2)
    exp_terms = jnp.where(allowed[None], jnp.exp(scores - row_max[:, :, None]), 0.0)
    row_sum = jnp.sum(exp_terms, axis=2)
    weighted = jnp.einsum(
        "hqk,khd->hqd",
        exp_terms.astype(jnp.bfloat16),
        value_rows,
        preferred_element_type=jnp.float32,
    )
    return (row_max, row_sum, weighted)


def combine(first_part, second_part):
    row_max = jnp.maximum(first_part[0], second_part[0])
    scale_one = jnp.exp(first_part[0] - row_max)
    scale_two = jnp.exp(second_part[0] - row_max)
    row_sum = first_part[1] * scale_one + second_part[1] * scale_two
    weighted = first_part[2] * scale_one[:, :, None] + second_part[2] * scale_two[:, :, None]
    return (row_max, row_sum, weighted)


def feed_forward(rows_in, in_part, out_part):
    units = lax.dot_general(
        rows_in, in_part, (((1,), (1,)), ((), ())), preferred_element_type=jnp.float32
    )
    units = jnp.maximum(units, 0.0).astype(jnp.bfloat16)
    return jnp.dot(units, out_part, preferred_element_type=jnp.float32)


def body(
    tokens,
    attn_gain,
    w_query,
    w_key,
    w_value,
    w_attn_out,
    rel_bias,
    prefix_cache,
    lengths,
    prefix_map,
    mlp_gain,
    w_in,
    w_out,
):
    rows_here = tokens.shape[0]
    device_pos = lax.axis_index("req")
    group_lengths = lengths[0]
    group_map = prefix_map[0]
    normed = norm_rows(tokens, attn_gain)
    query = (
        jnp.dot(normed, w_query, preferred_element_type=jnp.float32)
        .astype(jnp.bfloat16)
        .reshape(rows_here, H, DK)
    )
    key_value = jnp.concatenate(
        [
            jnp.dot(normed, w_key, preferred_element_type=jnp.float32).astype(jnp.bfloat16),
            jnp.dot(normed, w_value, preferred_element_type=jnp.float32).astype(jnp.bfloat16),
        ],
        axis=1,
    )
    query_ids = device_pos * rows_here + jnp.arange(rows_here, dtype=jnp.int32)
    query_req, query_offset, query_prefix = layout(group_lengths, group_map, query_ids)
    all_positions = jnp.arange(PLEN, dtype=jnp.int32)
    prefix_bias = bias_lookup(all_positions[None, :] - PLEN - query_offset[:, None], rel_bias)
    empty_state = (
        jnp.full((H, rows_here), masked_score, jnp.float32),
        jnp.zeros((H, rows_here), jnp.float32),
        jnp.zeros((H, rows_here, DK), jnp.float32),
    )
    running = empty_state
    shard_kv = lax.all_gather(prefix_cache, "req", axis=1, tiled=True)
    prefix_ids = jnp.arange(PREF_GRP, dtype=jnp.int32)
    slices = shard_kv.shape[0]
    piece_len = shard_kv.shape[1]
    step_len = max(min(piece_len, 512 // slices), 1)
    for begin in range(0, piece_len, step_len):
        width = min(step_len, piece_len - begin)
        block = shard_kv[:, begin : begin + width]
        key_rows = block[:, :, :D].reshape(slices, width, H, DK)
        value_rows = block[:, :, D:].reshape(-1, H, DK)
        rel_terms = lax.dynamic_slice_in_dim(prefix_bias, begin, width, 2)
        prefix_scores = jnp.einsum(
            "qhd,swhd->hqsw", query, key_rows, preferred_element_type=jnp.float32
        )
        prefix_scores = (prefix_scores + rel_terms[:, :, None, :]).reshape(
            H, rows_here, slices * width
        )
        allowed = jnp.repeat(query_prefix[:, None] == prefix_ids[None, :], width, axis=1)
        running = combine(running, softmax_part(prefix_scores, value_rows, allowed))
    state = running
    window = padded(key_value, (("req", 0),), rows_here)
    window_ids = device_pos * rows_here - rows_here + jnp.arange(3 * rows_here, dtype=jnp.int32)
    window_req = layout(group_lengths, group_map, window_ids)[0]
    for part_idx in range(3):
        part_rows = window[part_idx * rows_here : (part_idx + 1) * rows_here]
        part_ids = window_ids[part_idx * rows_here : (part_idx + 1) * rows_here]
        part_req = window_req[part_idx * rows_here : (part_idx + 1) * rows_here]
        suffix_terms = bias_lookup(part_ids[None, :] - query_ids[:, None], rel_bias)
        suffix_allowed = part_req[None, :] == query_req[:, None]
        scores = (
            jnp.einsum(
                "qhd,khd->hqk",
                query,
                part_rows[:, :D].reshape(-1, H, DK),
                preferred_element_type=jnp.float32,
            )
            + suffix_terms
        )
        suffix_state = softmax_part(scores, part_rows[:, D:].reshape(-1, H, DK), suffix_allowed)
        state = combine(state, suffix_state)
    attended = (
        (state[2] / state[1][:, :, None])
        .transpose(1, 0, 2)
        .reshape(rows_here, D)
        .astype(jnp.bfloat16)
    )
    hidden_one = (
        tokens.astype(jnp.float32)
        + jnp.dot(attended, w_attn_out, preferred_element_type=jnp.float32)
    ).astype(jnp.bfloat16)
    normed_two = norm_rows(hidden_one, mlp_gain)
    gathered = lax.all_gather(normed_two, "grp", axis=0, tiled=True)
    mlp_total = lax.psum_scatter(
        feed_forward(gathered, w_in, w_out).astype(jnp.bfloat16),
        "grp",
        scatter_dimension=0,
        tiled=True,
    ).astype(jnp.float32)
    return (hidden_one.astype(jnp.float32) + mlp_total).astype(jnp.bfloat16)


def bucket_steps():
    return tuple((i, i) for i in range(1, 9)) + tuple((t, 9 + i) for i, t in enumerate(far_marks))


def chain(distance, table, head, first):
    value = jnp.full(distance.shape, table[head, first], jnp.float32)
    for threshold, number in bucket_steps():
        value = jnp.where(distance >= threshold, table[head, first + number], value)
    return value


def layer_kernel(
    n_req,
    tokens_hbm,
    attn_gain,
    wq_hbm,
    wk_hbm,
    wv_hbm,
    wo_hbm,
    rel_bias,
    cache_hbm,
    lengths,
    prefix_map,
    mlp_gain,
    win_hbm,
    wout_hbm,
    out_ref,
    tok,
    w_attn,
    w_in,
    w_out,
    normed,
    stage,
    k_cache,
    v_cache,
    q_all,
    k_win,
    v_win,
    k_cross,
    w_up,
    tail_bias,
    near_bias,
    row_prefix,
    row_max,
    row_sum,
    row_acc,
    o_send,
    l_send,
    att_in,
    l_in,
    att,
    h_one,
    n_two,
    units,
    part_own,
    part_far,
    fast_out,
    fast_in,
    chip_out,
    chip_in,
    far_out,
    far_in,
    load_sem,
    own_sem,
    kc_send,
    kc_recv,
    vc_send,
    vc_recv,
    q_send,
    q_recv,
    n_send,
    n_recv,
    o_ssem,
    o_rsem,
    l_ssem,
    l_rsem,
    f_send,
    f_recv,
):
    me = lax.axis_index("req")
    grp = lax.axis_index("grp")
    side = lax.rem(grp, 2)
    plane = lax.div(grp, 2)
    mate = plane * 2 + (1 - side)
    across = (1 - plane) * 2 + side
    rows = tokens_hbm.shape[0]
    piece = cache_hbm.shape[1]
    half = rows // 2

    def remote(src, dst, ssem, rsem, **where):
        return pltpu.make_async_remote_copy(
            src_ref=src, dst_ref=dst, send_sem=ssem, recv_sem=rsem, device_id=where, device_id_type=MESH
        )

    def lanes_of(index):
        return pl.ds(pl.multiple_of(index * LANES, LANES), LANES)

    def rows_of(index):
        return pl.ds(pl.multiple_of(index * rows, rows), rows)

    loads = [
        pltpu.make_async_copy(src, dst, load_sem.at[i])
        for i, (src, dst) in enumerate(
            [
                (tokens_hbm, tok),
                (wq_hbm, w_attn.at[0]),
                (wk_hbm, w_attn.at[1]),
                (wv_hbm, w_attn.at[2]),
                (wo_hbm, w_attn.at[3]),
                (win_hbm, w_in),
                (wout_hbm, w_out),
            ]
        )
    ]
    for load in loads[:4]:
        load.start()

    barrier = pltpu.get_barrier_semaphore()
    for d in range(1, n_req):
        pl.semaphore_signal(
            barrier, inc=1, device_id={"req": lax.rem(me + d, n_req)}, device_id_type=MESH
        )
    for other in (mate, across):
        pl.semaphore_signal(barrier, inc=1, device_id={"grp": other}, device_id_type=MESH)
    pl.semaphore_wait(barrier, n_req + 1)

    def cache_copy(buf, first, sends, recvs, d, peer, owner):
        return remote(
            cache_hbm.at[:, :, pl.ds(pl.multiple_of(first + peer * LANES, LANES), LANES)],
            buf.at[:, pl.ds(pl.multiple_of(owner * piece, piece), piece), :],
            sends.at[d],
            recvs.at[d],
            req=peer,
        )

    def q_copy(d, peer, owner):
        return remote(
            stage.at[:, lanes_of(peer)], q_all.at[rows_of(owner), :], q_send.at[d], q_recv.at[d], req=peer
        )

    odd = lax.rem(me, 2)
    beside = me + 1 - 2 * odd
    beyond = me - 1 + 2 * odd
    onward = me + 2 - 4 * odd
    has_beyond = jnp.logical_and(beyond >= 0, beyond < n_req)
    has_onward = jnp.logical_and(onward >= 0, onward < n_req)
    own_slot = pl.ds(rows, rows)

    def slot(late):
        return pl.ds(pl.multiple_of(2 * rows * late, LANES), rows)

    k_beside = remote(k_win.at[:, own_slot], k_win.at[:, slot(odd)], n_send.at[0], n_recv.at[0], req=beside)
    v_beside = remote(v_win.at[own_slot], v_win.at[slot(odd)], n_send.at[1], n_recv.at[1], req=beside)
    k_beyond = remote(
        k_win.at[:, own_slot], k_win.at[:, slot(1 - odd)], n_send.at[2], n_recv.at[2], req=beyond
    )
    v_onward = remote(
        v_win.at[slot(1 - odd)], v_win.at[slot(odd)], n_send.at[3], n_recv.at[3], req=onward
    )
    k_beside_in = remote(
        k_win.at[:, own_slot], k_win.at[:, slot(1 - odd)], n_send.at[0], n_recv.at[0], req=beside
    )
    v_beside_in = remote(v_win.at[own_slot], v_win.at[slot(1 - odd)], n_send.at[1], n_recv.at[1], req=beside)
    k_beyond_in = remote(
        k_win.at[:, own_slot], k_win.at[:, slot(odd)], n_send.at[2], n_recv.at[2], req=beyond
    )
    v_onward_in = remote(
        v_win.at[own_slot], v_win.at[slot(odd)], n_send.at[3], n_recv.at[3], req=beyond
    )

    parts = [pl.ds(r * half, half) for r in range(2)]

    def o_copy(r):
        def make(d, peer, owner):
            return remote(
                o_send.at[peer, parts[r]],
                att_in.at[parts[r], lanes_of(owner)],
                o_ssem.at[r, d],
                o_rsem.at[r, d],
                req=peer,
            )

        return make

    def l_copy(r):
        def make(d, peer, owner):
            return remote(
                l_send.at[peer, r], l_in.at[owner, r], l_ssem.at[r, d], l_rsem.at[r, d], req=peer
            )

        return make

    def outgoing(make):
        return [make(d, lax.rem(me + d, n_req), me) for d in range(1, n_req)]

    def incoming(make):
        return [
            make(d, lax.rem(me + d, n_req), lax.rem(me + n_req - d, n_req)) for d in range(1, n_req)
        ]

    def kc_copy(d, peer, owner):
        return cache_copy(k_cache, 0, kc_send, kc_recv, d, peer, owner)

    def vc_copy(d, peer, owner):
        return cache_copy(v_cache, D, vc_send, vc_recv, d, peer, owner)

    for copy in outgoing(kc_copy) + outgoing(vc_copy):
        copy.start()
    own_copies = [
        pltpu.make_async_copy(
            cache_hbm.at[:, :, pl.ds(pl.multiple_of(first + me * LANES, LANES), LANES)],
            buf.at[:, pl.ds(pl.multiple_of(me * piece, piece), piece), :],
            own_sem.at[i],
        )
        for i, (buf, first) in enumerate([(k_cache, 0), (v_cache, D)])
    ]
    for copy in own_copies:
        copy.start()

    loads[0].wait()
    wide = tok[...].astype(jnp.float32)
    scale = lax.rsqrt(jnp.mean(wide * wide, axis=-1, keepdims=True) + epsilon)
    normed[...] = (wide * scale * attn_gain[...]).astype(jnp.bfloat16)

    tile = 512
    for part in range(3):
        loads[1 + part].wait()

        @pl.loop(0, D // tile)
        def _(t, part=part):
            cols = pl.ds(pl.multiple_of(t * tile, tile), tile)
            made = jnp.dot(
                normed[...], w_attn[part, :, cols], preferred_element_type=jnp.float32
            ).astype(jnp.bfloat16)
            if part == 0:
                stage[:, cols] = made
            elif part == 1:
                k_win[cols, own_slot] = made.T
            else:
                v_win[own_slot, cols] = made

        if part == 0:
            for copy in outgoing(q_copy):
                copy.start()
            for load in loads[4:]:
                load.start()
        elif part == 1:
            k_beside.start()

            @pl.when(has_beyond)
            def _():
                k_beyond.start()
        else:
            v_beside.start()
    q_all[rows_of(me), :] = stage[:, lanes_of(me)]

    @pl.when(jnp.logical_not(has_beyond))
    def _():
        k_win[:, slot(odd)] = jnp.zeros((D, rows), jnp.bfloat16)
        v_win[slot(odd), :] = jnp.zeros((rows, D), jnp.bfloat16)

    ends = []
    total = 0
    n_requests = lengths.shape[1]
    for j in range(n_requests):
        total = total + lengths[0, j]
        ends.append(total)
    def stacked(r, head):
        return pl.ds((2 * r + head) * half, half)

    row_iota = lax.broadcasted_iota(jnp.int32, (rows, LANES), 0)
    lane_iota = lax.broadcasted_iota(jnp.int32, (rows, LANES), 1)
    @pl.loop(0, n_req)
    def _(b):
        ids = row_iota + b * rows
        start = jnp.zeros_like(ids)
        prefix = jnp.full(ids.shape, prefix_map[0, 0], jnp.int32)
        for j in range(n_requests):
            past = ids >= ends[j]
            start = start + jnp.where(past, lengths[0, j], 0)
            if j + 1 < n_requests:
                prefix = jnp.where(past, prefix_map[0, j + 1], prefix)
        row_prefix[b] = prefix
        distance = LANES + ids - start - lane_iota
        for head in range(2):
            terms = chain(distance, rel_bias, 2 * me + head, 0)
            for r in range(2):
                tail_bias[b, stacked(r, head), :] = terms[r * half : (r + 1) * half]

    def request_of(ids):
        number = jnp.where(ids < 0, -1, 0)
        for end in ends:
            number = number + jnp.where(ids >= end, 1, 0)
        return number

    own_number = request_of(row_iota + me * rows)
    key_numbers = [
        request_of(lax.broadcasted_iota(jnp.int32, (8, LANES), 1) + (me + part - 1) * rows)[:1]
        for part in range(3)
    ]

    @pl.loop(0, n_req)
    def _(pair):
        for part in range(3):
            same = key_numbers[part] == own_number
            ahead = lane_iota + (part - 1) * rows - row_iota
            distance = jnp.abs(ahead)
            for head in range(2):
                if part == 0:
                    both = chain(distance, rel_bias, 2 * pair + head, 0)
                elif part == 2:
                    both = chain(distance, rel_bias, 2 * pair + head, 16)
                else:
                    both = jnp.where(
                        ahead > 0,
                        chain(distance, rel_bias, 2 * pair + head, 16),
                        chain(distance, rel_bias, 2 * pair + head, 0),
                    )
                both = jnp.where(same, both, masked_score)
                for r in range(2):
                    near_bias[pair, stacked(r, head), pl.ds(part * LANES, LANES)] = both[
                        r * half : (r + 1) * half
                    ]

    loads[5].wait()

    @pl.loop(0, w_in.shape[0] // tile)
    def _(t):
        cols = pl.ds(pl.multiple_of(t * tile, tile), tile)
        w_up[:, cols] = w_in[cols, :].T

    first_head = lane_iota < DK

    def query_heads(q):
        nothing = jnp.zeros_like(q)
        first = first_head[:half]
        return jnp.concatenate(
            [jnp.where(first, q, nothing), jnp.where(first, nothing, q)], axis=0
        )

    def one_row(stack):
        return jnp.where(first_head[:half], stack[:half], stack[half:]).astype(jnp.bfloat16)

    v_beside_in.wait_recv()

    @pl.when(has_onward)
    def _():
        v_onward.start()

    for copy in own_copies:
        copy.wait()
    for copy in incoming(kc_copy):
        copy.wait_recv()
    for which in range(PREF_GRP):
        k_cross[pl.ds(which * LANES, LANES), :] = k_cache[which].T
    for make in (q_copy, vc_copy):
        for copy in incoming(make):
            copy.wait_recv()

    far_bias = jnp.concatenate(
        [jnp.full((half, 1), rel_bias[2 * me + head, 15], jnp.float32) for head in range(2)], axis=0
    )
    far_keys = PLEN - LANES

    def far_scores(b, r):
        here = pl.ds(r * rows, rows)
        qh = query_heads(q_all[pl.ds(pl.multiple_of(b * rows + r * half, half), half), :])
        choice = row_prefix[b, parts[r], :]
        zero_first = jnp.concatenate([choice, choice], axis=0) == 0
        nothing = jnp.zeros_like(qh)
        q2 = jnp.concatenate(
            [jnp.where(zero_first, qh, nothing), jnp.where(zero_first, nothing, qh)], axis=1
        )
        scores = jnp.dot(q2, k_cross[...], preferred_element_type=jnp.float32)
        scores = jnp.concatenate(
            [scores[:, :far_keys] + far_bias, scores[:, far_keys:] + tail_bias[b, here, :]], axis=1
        )
        return zero_first, scores

    def far_terms(scores):
        top = jnp.max(scores, axis=1, keepdims=True)
        terms = jnp.exp(scores - top)
        return top, jnp.sum(terms, axis=1, keepdims=True), terms.astype(jnp.bfloat16)

    def far(blocks, r):
        values = jnp.concatenate([v_cache[0], v_cache[1]], axis=1)
        scored = [far_scores(b, r) for b in blocks]
        termed = [far_terms(scores) for _, scores in scored]
        accs = [jnp.dot(t[2], values, preferred_element_type=jnp.float32) for t in termed]
        results = []
        for (zero_first, _), (top, total, _), acc in zip(scored, termed, accs):
            chosen = jnp.where(zero_first, acc[:, :LANES], acc[:, LANES:]) / total
            logs = jnp.broadcast_to(top + jnp.log(total), (rows, LANES)).T
            results.append((one_row(chosen), logs[:8]))
        return results

    far_step = 4
    for r in range(2):
        for begin in range(1, n_req + 1, far_step):
            turns = range(begin, begin + far_step)
            blocks = [lax.rem(me + d, n_req) for d in turns]
            for d, b, (result, logs) in zip(turns, blocks, far(blocks, r)):
                if d < n_req:
                    o_send[b, parts[r], :] = result
                    l_send[b, r] = logs
                else:
                    att_in[parts[r], lanes_of(me)] = result
                    l_in[me, r] = logs
            for d, b in zip(turns, blocks):
                if d < n_req:
                    o_copy(r)(d, b, me).start()
                    l_copy(r)(d, b, me).start()

    k_beside_in.wait_recv()

    @pl.when(has_beyond)
    def _():
        k_beyond_in.wait_recv()
        v_onward_in.wait_recv()

    def near(pairs):
        lanes = [lanes_of(pair) for pair in pairs]
        scores = [
            jnp.dot(
                jnp.concatenate([query_heads(stage[parts[r], at]) for r in range(2)], axis=0),
                k_win[at, :],
                preferred_element_type=jnp.float32,
            )
            + near_bias[pair]
            for pair, at in zip(pairs, lanes)
        ]
        tops = [jnp.max(x, axis=1, keepdims=True) for x in scores]
        terms = [jnp.exp(x - t) for x, t in zip(scores, tops)]
        accs = [
            jnp.dot(x.astype(jnp.bfloat16), v_win[:, at], preferred_element_type=jnp.float32)
            for x, at in zip(terms, lanes)
        ]
        for pair, top, x, acc in zip(pairs, tops, terms, accs):
            row_max[pair] = jnp.broadcast_to(top, (2 * rows, LANES))
            row_sum[pair] = jnp.broadcast_to(jnp.sum(x, axis=1, keepdims=True), (2 * rows, LANES))
            row_acc[pair] = acc

    near_step = 2

    @pl.loop(0, n_req // near_step)
    def _(step):
        near([step * near_step + i for i in range(near_step)])

    def merge(pair, r):
        here = pl.ds(r * rows, rows)
        at = pl.ds(pair * LANES, LANES)
        logs = jnp.broadcast_to(l_in[pair, r, :1, :], (rows, LANES)).T
        there = att_in[parts[r], at].astype(jnp.float32)
        there = jnp.concatenate([there, there], axis=0)
        top = jnp.maximum(logs, row_max[pair, here, :])
        scale_one = jnp.exp(logs - top)
        scale_two = jnp.exp(row_max[pair, here, :] - top)
        whole = there * scale_one + row_acc[pair, here, :] * scale_two
        att[parts[r], at] = one_row(whole / (scale_one + row_sum[pair, here, :] * scale_two))

    mine = [
        remote(n_two.at[0, parts[r]], n_two.at[1, parts[r]], f_send.at[10 + r], f_recv.at[10 + r], grp=mate)
        for r in range(2)
    ]
    cross = [
        remote(n_two.at[0, parts[r]], n_two.at[2, parts[r]], f_send.at[1 + r], f_recv.at[1 + r], grp=across)
        for r in range(2)
    ]
    relay = [
        remote(n_two.at[2, parts[r]], n_two.at[3, parts[r]], f_send.at[3 + r], f_recv.at[3 + r], grp=mate)
        for r in range(2)
    ]
    back = remote(fast_out, fast_in, f_send.at[5], f_recv.at[5], grp=mate)
    swap = [
        remote(chip_out.at[r], chip_in.at[r], f_send.at[6 + r], f_recv.at[6 + r], grp=mate) for r in range(2)
    ]
    home = [
        remote(far_out.at[r], far_in.at[r], f_send.at[8 + r], f_recv.at[8 + r], grp=across) for r in range(2)
    ]

    loads[4].wait()
    for r in range(2):
        for copy in incoming(o_copy(r)) + incoming(l_copy(r)):
            copy.wait_recv()
        for pair in range(n_req):
            merge(pair, r)

        @pl.loop(0, D // tile)
        def _(t, r=r):
            cols = pl.ds(pl.multiple_of(t * tile, tile), tile)
            h_one[parts[r], cols] = (
                tok[parts[r], cols].astype(jnp.float32)
                + jnp.dot(
                    att[parts[r], :], w_attn[3, :, cols], preferred_element_type=jnp.float32
                )
            ).astype(jnp.bfloat16)

        wide = h_one[parts[r], :].astype(jnp.float32)
        scale = lax.rsqrt(jnp.mean(wide * wide, axis=-1, keepdims=True) + epsilon)
        n_two[0, parts[r], :] = (wide * scale * mlp_gain[...]).astype(jnp.bfloat16)
        cross[r].start()
        mine[r].start()

    loads[6].wait()

    def up(rows_in):
        @pl.loop(0, w_in.shape[0] // tile)
        def _(t):
            cols = pl.ds(pl.multiple_of(t * tile, tile), tile)
            units[:, cols] = jnp.maximum(
                jnp.dot(rows_in, w_up[:, cols], preferred_element_type=jnp.float32), 0.0
            ).astype(jnp.bfloat16)

    def down(out):
        @pl.loop(0, D // tile)
        def _(t):
            cols = pl.ds(pl.multiple_of(t * tile, tile), tile)
            out[:, cols] = jnp.dot(
                units[...], w_out[:, cols], preferred_element_type=jnp.float32
            ).astype(out.dtype)

    def far_rows(r):
        return jnp.concatenate([n_two[2, parts[r]], n_two[3, parts[r]]], axis=0)

    def send_home(r):
        swap[r].wait_recv()
        far_out[r] = (part_far[r, pl.ds(0, half), :] + chip_in[r].astype(jnp.float32)).astype(jnp.bfloat16)
        home[r].start()

    def finish_far(r):
        down(part_far.at[r])
        chip_out[r] = part_far[r, pl.ds(half, half), :].astype(jnp.bfloat16)
        swap[r].start()

    up(n_two[0])
    cross[0].wait_recv()
    relay[0].start()
    down(part_own)
    for copy in mine:
        copy.wait_recv()
    up(n_two[1])
    down(fast_out)
    back.start()
    cross[1].wait_recv()
    relay[1].start()
    relay[0].wait_recv()
    up(far_rows(0))
    finish_far(0)
    relay[1].wait_recv()
    up(far_rows(1))
    send_home(0)
    finish_far(1)
    back.wait_recv()
    part_own[...] = (
        part_own[...] + h_one[...].astype(jnp.float32) + fast_in[...].astype(jnp.float32)
    )
    send_home(1)
    for r in range(2):
        home[r].wait_recv()
        out_ref[parts[r], :] = (
            part_own[parts[r], :] + far_in[r].astype(jnp.float32)
        ).astype(jnp.bfloat16)

    k_beside.wait_send()
    v_beside.wait_send()

    @pl.when(has_beyond)
    def _():
        k_beyond.wait_send()

    @pl.when(has_onward)
    def _():
        v_onward.wait_send()

    for make in (kc_copy, vc_copy, q_copy, o_copy(0), o_copy(1), l_copy(0), l_copy(1)):
        for copy in outgoing(make):
            copy.wait_send()
    for copy in [back] + mine + cross + relay + swap + home:
        copy.wait_send()


def fused(
    tokens,
    attn_gain,
    w_query,
    w_key,
    w_value,
    w_attn_out,
    rel_bias,
    prefix_cache,
    lengths,
    prefix_map,
    mlp_gain,
    w_in,
    w_out,
):
    n_req = lax.axis_size("req")
    rows = tokens.shape[0]
    group = n_req * rows
    hbm = pl.BlockSpec(memory_space=pl.ANY)
    vmem = pl.BlockSpec(memory_space=pltpu.VMEM)
    smem = pl.BlockSpec(memory_space=pltpu.SMEM)
    half = rows // 2
    bf16, f32 = jnp.bfloat16, jnp.float32
    sems = pltpu.SemaphoreType.DMA
    return pl.pallas_call(
        functools.partial(layer_kernel, n_req),
        out_shape=jax.ShapeDtypeStruct((rows, D), bf16),
        in_specs=[hbm, vmem, hbm, hbm, hbm, hbm, smem, hbm, smem, smem, vmem, hbm, hbm],
        out_specs=vmem,
        scratch_shapes=[
            pltpu.VMEM((rows, D), bf16),
            pltpu.VMEM((4, D, D), bf16),
            pltpu.VMEM(w_in.shape, bf16),
            pltpu.VMEM(w_out.shape, bf16),
            pltpu.VMEM((rows, D), bf16),
            pltpu.VMEM((rows, D), bf16),
            pltpu.VMEM((PREF_GRP, PLEN, LANES), bf16),
            pltpu.VMEM((PREF_GRP, PLEN, LANES), bf16),
            pltpu.VMEM((group, LANES), bf16),
            pltpu.VMEM((D, 3 * rows), bf16),
            pltpu.VMEM((3 * rows, D), bf16),
            pltpu.VMEM((PREF_GRP * LANES, PLEN), bf16),
            pltpu.VMEM(w_in.shape[::-1], bf16),
            pltpu.VMEM((n_req, 2 * rows, LANES), f32),
            pltpu.VMEM((n_req, 2 * rows, 3 * LANES), f32),
            pltpu.VMEM((n_req, rows, LANES), jnp.int32),
            pltpu.VMEM((n_req, 2 * rows, LANES), f32),
            pltpu.VMEM((n_req, 2 * rows, LANES), f32),
            pltpu.VMEM((n_req, 2 * rows, LANES), f32),
            pltpu.VMEM((n_req, rows, LANES), bf16),
            pltpu.VMEM((n_req, 2, 8, LANES), f32),
            pltpu.VMEM((rows, D), bf16),
            pltpu.VMEM((n_req, 2, 8, LANES), f32),
            pltpu.VMEM((rows, D), bf16),
            pltpu.VMEM((rows, D), bf16),
            pltpu.VMEM((4, rows, D), bf16),
            pltpu.VMEM((rows, w_in.shape[0]), bf16),
            pltpu.VMEM((rows, D), f32),
            pltpu.VMEM((2, rows, D), f32),
            pltpu.VMEM((rows, D), bf16),
            pltpu.VMEM((rows, D), bf16),
            pltpu.VMEM((2, half, D), bf16),
            pltpu.VMEM((2, half, D), bf16),
            pltpu.VMEM((2, half, D), bf16),
            pltpu.VMEM((2, half, D), bf16),
            sems((7,)),
            sems((2,)),
        ]
        + [sems((n_req,)) for _ in range(6)]
        + [sems((4,)), sems((4,))]
        + [sems((2, n_req)) for _ in range(4)]
        + [sems((12,)), sems((12,))],
        compiler_params=pltpu.CompilerParams(
            collective_id=0, has_side_effects=True, vmem_limit_bytes=63 * 1024 * 1024
        ),
    )(
        tokens,
        attn_gain.reshape(1, D),
        w_query,
        w_key,
        w_value,
        w_attn_out,
        rel_bias.T,
        prefix_cache,
        lengths,
        prefix_map,
        mlp_gain.reshape(1, D),
        w_in,
        w_out,
    )


def pairs_fit(mesh):
    return mesh.shape["req"] * LANES == D and mesh.shape["grp"] == 4


def solution(mesh):
    return jax.shard_map(
        fused if pairs_fit(mesh) else body,
        mesh=mesh,
        in_specs=(
            P(("grp", "req"), None),
            P(),
            P(),
            P(),
            P(),
            P(),
            P(),
            P("grp", "req", None),
            P("grp", None),
            P("grp", None),
            P(),
            P("grp", None),
            P("grp", None),
        ),
        out_specs=P(("grp", "req"), None),
        check_vma=False,
    )
```

```python
import functools

import jax
import jax.numpy as jnp
from jax import lax
from jax.experimental import pallas as pl
from jax.experimental.pallas import tpu as pltpu
from jax.sharding import PartitionSpec as P

D = 1024
H = 16
DK = 64
PLEN = 512
PREF_GRP = 2
LANES = 128
MESH = pl.DeviceIdType.MESH


epsilon = 1e-06
far_marks = (12, 16, 23, 32, 46, 64, 91)
masked_score = -1e30


def padded(value, sides, width):
    for axis, dim in sides:
        count, length = (lax.axis_size(axis), value.shape[dim])
        up = [(i, (i + 1) % count) for i in range(count - 1)]
        down = [(j, i) for i, j in up]
        last = lax.slice_in_dim(value, length - width, length, axis=dim)
        leading = lax.slice_in_dim(value, 0, width, axis=dim)
        before = lax.ppermute(last, axis, up)
        after = lax.ppermute(leading, axis, down)
        value = jnp.concatenate([before, value, after], axis=dim)
    return value


def bucket_of(relative):
    distance = jnp.abs(relative)
    far_bucket = 8 + sum([(distance >= threshold).astype(jnp.int32) for threshold in far_marks])
    bucket = jnp.where(distance < 8, distance, far_bucket)
    return bucket + jnp.where(relative > 0, 16, 0)


def bias_lookup(relative, rel_bias):
    buckets = bucket_of(relative)
    marks = jnp.arange(rel_bias.shape[0], dtype=jnp.int32)
    one_hot = (buckets[:, :, None] == marks[None, None, :]).astype(jnp.float32)
    return jnp.einsum(
        "qkb,bh->hqk",
        one_hot,
        rel_bias,
        precision=lax.Precision.HIGHEST,
        preferred_element_type=jnp.float32,
    )


def norm_rows(values_in, gain):
    widened = values_in.astype(jnp.float32)
    scale = lax.rsqrt(jnp.mean(widened * widened, axis=-1, keepdims=True) + epsilon)
    return (widened * scale * gain).astype(jnp.bfloat16)


def layout(lengths_row, prefix_row, row_ids):
    req_ends = jnp.cumsum(lengths_row)
    req_starts = req_ends - lengths_row
    member = (
        (row_ids[:, None] >= req_starts[None, :]) & (row_ids[:, None] < req_ends[None, :])
    ).astype(jnp.int32)
    numbers = jnp.arange(lengths_row.shape[0], dtype=jnp.int32)
    req_index = jnp.sum(member * numbers[None, :], axis=1) + jnp.sum(member, axis=1) - 1
    offset = row_ids - jnp.sum(member * req_starts[None, :], axis=1)
    chosen = jnp.sum(member * prefix_row[None, :], axis=1)
    return (req_index, offset, chosen)


def softmax_part(scores, value_rows, allowed):
    scores = jnp.where(allowed[None], scores, masked_score)
    row_max = jnp.max(scores, axis=2)
    exp_terms = jnp.where(allowed[None], jnp.exp(scores - row_max[:, :, None]), 0.0)
    row_sum = jnp.sum(exp_terms, axis=2)
    weighted = jnp.einsum(
        "hqk,khd->hqd",
        exp_terms.astype(jnp.bfloat16),
        value_rows,
        preferred_element_type=jnp.float32,
    )
    return (row_max, row_sum, weighted)


def combine(first_part, second_part):
    row_max = jnp.maximum(first_part[0], second_part[0])
    scale_one = jnp.exp(first_part[0] - row_max)
    scale_two = jnp.exp(second_part[0] - row_max)
    row_sum = first_part[1] * scale_one + second_part[1] * scale_two
    weighted = first_part[2] * scale_one[:, :, None] + second_part[2] * scale_two[:, :, None]
    return (row_max, row_sum, weighted)


def feed_forward(rows_in, in_part, out_part):
    units = lax.dot_general(
        rows_in, in_part, (((1,), (1,)), ((), ())), preferred_element_type=jnp.float32
    )
    units = jnp.maximum(units, 0.0).astype(jnp.bfloat16)
    return jnp.dot(units, out_part, preferred_element_type=jnp.float32)


def body(
    tokens,
    attn_gain,
    w_query,
    w_key,
    w_value,
    w_attn_out,
    rel_bias,
    prefix_cache,
    lengths,
    prefix_map,
    mlp_gain,
    w_in,
    w_out,
):
    rows_here = tokens.shape[0]
    device_pos = lax.axis_index("req")
    group_lengths = lengths[0]
    group_map = prefix_map[0]
    normed = norm_rows(tokens, attn_gain)
    query = (
        jnp.dot(normed, w_query, preferred_element_type=jnp.float32)
        .astype(jnp.bfloat16)
        .reshape(rows_here, H, DK)
    )
    key_value = jnp.concatenate(
        [
            jnp.dot(normed, w_key, preferred_element_type=jnp.float32).astype(jnp.bfloat16),
            jnp.dot(normed, w_value, preferred_element_type=jnp.float32).astype(jnp.bfloat16),
        ],
        axis=1,
    )
    query_ids = device_pos * rows_here + jnp.arange(rows_here, dtype=jnp.int32)
    query_req, query_offset, query_prefix = layout(group_lengths, group_map, query_ids)
    all_positions = jnp.arange(PLEN, dtype=jnp.int32)
    prefix_bias = bias_lookup(all_positions[None, :] - PLEN - query_offset[:, None], rel_bias)
    empty_state = (
        jnp.full((H, rows_here), masked_score, jnp.float32),
        jnp.zeros((H, rows_here), jnp.float32),
        jnp.zeros((H, rows_here, DK), jnp.float32),
    )
    running = empty_state
    shard_kv = lax.all_gather(prefix_cache, "req", axis=1, tiled=True)
    prefix_ids = jnp.arange(PREF_GRP, dtype=jnp.int32)
    slices = shard_kv.shape[0]
    piece_len = shard_kv.shape[1]
    step_len = max(min(piece_len, 512 // slices), 1)
    for begin in range(0, piece_len, step_len):
        width = min(step_len, piece_len - begin)
        block = shard_kv[:, begin : begin + width]
        key_rows = block[:, :, :D].reshape(slices, width, H, DK)
        value_rows = block[:, :, D:].reshape(-1, H, DK)
        rel_terms = lax.dynamic_slice_in_dim(prefix_bias, begin, width, 2)
        prefix_scores = jnp.einsum(
            "qhd,swhd->hqsw", query, key_rows, preferred_element_type=jnp.float32
        )
        prefix_scores = (prefix_scores + rel_terms[:, :, None, :]).reshape(
            H, rows_here, slices * width
        )
        allowed = jnp.repeat(query_prefix[:, None] == prefix_ids[None, :], width, axis=1)
        running = combine(running, softmax_part(prefix_scores, value_rows, allowed))
    state = running
    window = padded(key_value, (("req", 0),), rows_here)
    window_ids = device_pos * rows_here - rows_here + jnp.arange(3 * rows_here, dtype=jnp.int32)
    window_req = layout(group_lengths, group_map, window_ids)[0]
    for part_idx in range(3):
        part_rows = window[part_idx * rows_here : (part_idx + 1) * rows_here]
        part_ids = window_ids[part_idx * rows_here : (part_idx + 1) * rows_here]
        part_req = window_req[part_idx * rows_here : (part_idx + 1) * rows_here]
        suffix_terms = bias_lookup(part_ids[None, :] - query_ids[:, None], rel_bias)
        suffix_allowed = part_req[None, :] == query_req[:, None]
        scores = (
            jnp.einsum(
                "qhd,khd->hqk",
                query,
                part_rows[:, :D].reshape(-1, H, DK),
                preferred_element_type=jnp.float32,
            )
            + suffix_terms
        )
        suffix_state = softmax_part(scores, part_rows[:, D:].reshape(-1, H, DK), suffix_allowed)
        state = combine(state, suffix_state)
    attended = (
        (state[2] / state[1][:, :, None])
        .transpose(1, 0, 2)
        .reshape(rows_here, D)
        .astype(jnp.bfloat16)
    )
    hidden_one = (
        tokens.astype(jnp.float32)
        + jnp.dot(attended, w_attn_out, preferred_element_type=jnp.float32)
    ).astype(jnp.bfloat16)
    normed_two = norm_rows(hidden_one, mlp_gain)
    gathered = lax.all_gather(normed_two, "grp", axis=0, tiled=True)
    mlp_total = lax.psum_scatter(
        feed_forward(gathered, w_in, w_out).astype(jnp.bfloat16),
        "grp",
        scatter_dimension=0,
        tiled=True,
    ).astype(jnp.float32)
    return (hidden_one.astype(jnp.float32) + mlp_total).astype(jnp.bfloat16)


def bucket_steps():
    return tuple((i, i) for i in range(1, 9)) + tuple((t, 9 + i) for i, t in enumerate(far_marks))


def chain(distance, table, head, first):
    value = jnp.full(distance.shape, table[head, first], jnp.float32)
    for threshold, number in bucket_steps():
        value = jnp.where(distance >= threshold, table[head, first + number], value)
    return value


def layer_kernel(
    n_req,
    tokens_hbm,
    attn_gain,
    wq_hbm,
    wk_hbm,
    wv_hbm,
    wo_hbm,
    rel_bias,
    cache_hbm,
    lengths,
    prefix_map,
    mlp_gain,
    win_hbm,
    wout_hbm,
    out_ref,
    tok,
    w_attn,
    w_in,
    w_out,
    normed,
    stage,
    k_cache,
    v_cache,
    q_all,
    k_side,
    k_all,
    v_all,
    k_cross,
    w_up,
    tail_bias,
    near_bias,
    key_req,
    row_facts,
    row_code,
    row_max,
    row_sum,
    row_acc,
    o_send,
    att,
    h_one,
    n_two,
    units,
    part_own,
    part_far,
    fast_out,
    fast_in,
    chip_out,
    chip_in,
    far_out,
    far_in,
    load_sem,
    own_sem,
    kc_send,
    kc_recv,
    vc_send,
    vc_recv,
    q_send,
    q_recv,
    k_send,
    k_recv,
    v_send,
    v_recv,
    o_ssem,
    o_rsem,
    f_send,
    f_recv,
):
    me = lax.axis_index("req")
    grp = lax.axis_index("grp")
    side = lax.rem(grp, 2)
    plane = lax.div(grp, 2)
    mate = plane * 2 + (1 - side)
    across = (1 - plane) * 2 + side
    rows = tokens_hbm.shape[0]
    piece = cache_hbm.shape[1]
    half = rows // 2

    def remote(src, dst, ssem, rsem, **where):
        return pltpu.make_async_remote_copy(
            src_ref=src, dst_ref=dst, send_sem=ssem, recv_sem=rsem, device_id=where, device_id_type=MESH
        )

    def lanes_of(index):
        return pl.ds(pl.multiple_of(index * LANES, LANES), LANES)

    def rows_of(index):
        return pl.ds(pl.multiple_of(index * rows, rows), rows)

    loads = [
        pltpu.make_async_copy(src, dst, load_sem.at[i])
        for i, (src, dst) in enumerate(
            [
                (tokens_hbm, tok),
                (wq_hbm, w_attn.at[0]),
                (wk_hbm, w_attn.at[1]),
                (wv_hbm, w_attn.at[2]),
                (wo_hbm, w_attn.at[3]),
                (win_hbm, w_in),
                (wout_hbm, w_out),
            ]
        )
    ]
    for load in loads[:4]:
        load.start()

    barrier = pltpu.get_barrier_semaphore()
    for d in range(1, n_req):
        pl.semaphore_signal(
            barrier, inc=1, device_id={"req": lax.rem(me + d, n_req)}, device_id_type=MESH
        )
    for other in (mate, across):
        pl.semaphore_signal(barrier, inc=1, device_id={"grp": other}, device_id_type=MESH)
    pl.semaphore_wait(barrier, n_req + 1)

    def cache_copy(buf, first, sends, recvs, d, peer, owner):
        return remote(
            cache_hbm.at[:, :, pl.ds(pl.multiple_of(first + peer * LANES, LANES), LANES)],
            buf.at[:, pl.ds(pl.multiple_of(owner * piece, piece), piece), :],
            sends.at[d],
            recvs.at[d],
            req=peer,
        )

    def q_copy(d, peer, owner):
        return remote(
            stage.at[0, :, lanes_of(peer)], q_all.at[rows_of(owner), :], q_send.at[d], q_recv.at[d], req=peer
        )

    def k_copy(d, peer, owner):
        return remote(
            k_side.at[lanes_of(peer), :], k_all.at[:, lanes_of(owner + 1)], k_send.at[d], k_recv.at[d], req=peer
        )

    def v_copy(d, peer, owner):
        return remote(
            stage.at[1, :, lanes_of(peer)], v_all.at[rows_of(owner + 1), :], v_send.at[d], v_recv.at[d], req=peer
        )

    parts = [pl.ds(r * half, half) for r in range(2)]

    def o_copy(r):
        def make(d, peer, owner):
            return remote(
                o_send.at[peer, parts[r]],
                att.at[parts[r], lanes_of(owner)],
                o_ssem.at[r, d],
                o_rsem.at[r, d],
                req=peer,
            )

        return make

    def outgoing(make):
        return [make(d, lax.rem(me + d, n_req), me) for d in range(1, n_req)]

    def incoming(make):
        return [
            make(d, lax.rem(me + d, n_req), lax.rem(me + n_req - d, n_req)) for d in range(1, n_req)
        ]

    def kc_copy(d, peer, owner):
        return cache_copy(k_cache, 0, kc_send, kc_recv, d, peer, owner)

    def vc_copy(d, peer, owner):
        return cache_copy(v_cache, D, vc_send, vc_recv, d, peer, owner)

    for copy in outgoing(kc_copy) + outgoing(vc_copy):
        copy.start()
    own_copies = [
        pltpu.make_async_copy(
            cache_hbm.at[:, :, pl.ds(pl.multiple_of(first + me * LANES, LANES), LANES)],
            buf.at[:, pl.ds(pl.multiple_of(me * piece, piece), piece), :],
            own_sem.at[i],
        )
        for i, (buf, first) in enumerate([(k_cache, 0), (v_cache, D)])
    ]
    for copy in own_copies:
        copy.start()

    loads[0].wait()
    wide = tok[...].astype(jnp.float32)
    scale = lax.rsqrt(jnp.mean(wide * wide, axis=-1, keepdims=True) + epsilon)
    normed[...] = (wide * scale * attn_gain[...]).astype(jnp.bfloat16)

    tile = 512
    makers = (q_copy, k_copy, v_copy)
    for part in range(3):
        loads[1 + part].wait()

        @pl.loop(0, D // tile)
        def _(t, part=part):
            cols = pl.ds(pl.multiple_of(t * tile, tile), tile)
            made = jnp.dot(
                normed[...], w_attn[part, :, cols], preferred_element_type=jnp.float32
            ).astype(jnp.bfloat16)
            if part == 1:
                k_side[cols, :] = made.T
            else:
                stage[part // 2, :, cols] = made

        for copy in outgoing(makers[part]):
            copy.start()
        if part == 0:
            for load in loads[4:]:
                load.start()
    q_all[rows_of(me), :] = stage[0, :, lanes_of(me)]
    k_all[:, lanes_of(me + 1)] = k_side[lanes_of(me), :]
    v_all[rows_of(me + 1), :] = stage[1, :, lanes_of(me)]
    zeros = jnp.zeros((rows, LANES), jnp.bfloat16)
    for outer in (0, n_req + 1):
        k_all[:, pl.ds(outer * rows, rows)] = zeros
        v_all[pl.ds(outer * rows, rows), :] = zeros

    ends = []
    total = 0
    n_requests = lengths.shape[1]
    for j in range(n_requests):
        total = total + lengths[0, j]
        ends.append(total)
    key_ids = lax.broadcasted_iota(jnp.int32, key_req.shape, 1) - rows
    key_number = jnp.where(key_ids < 0, -1, 0)
    for end in ends:
        key_number = key_number + jnp.where(key_ids >= end, 1, 0)
    key_req[...] = key_number

    def stacked(r, head):
        return pl.ds((2 * r + head) * half, half)

    row_iota = lax.broadcasted_iota(jnp.int32, (rows, LANES), 0)
    lane_iota = lax.broadcasted_iota(jnp.int32, (rows, LANES), 1)
    ids = lax.broadcasted_iota(jnp.int32, row_facts.shape, 0) * rows + lax.broadcasted_iota(
        jnp.int32, row_facts.shape, 1
    )
    number = jnp.zeros_like(ids)
    start = jnp.zeros_like(ids)
    prefix = jnp.full(ids.shape, prefix_map[0, 0], jnp.int32)
    for j in range(n_requests):
        past = ids >= ends[j]
        number = number + jnp.where(past, 1, 0)
        start = start + jnp.where(past, lengths[0, j], 0)
        if j + 1 < n_requests:
            prefix = jnp.where(past, prefix_map[0, j + 1], prefix)
    row_facts[...] = ((start * 2 + prefix) * 1024 + number).astype(jnp.float32)

    def bias_of(distance, head, first):
        return chain(distance, rel_bias, 2 * me + head, first) - rel_bias[2 * me + head, 15]

    @pl.loop(0, n_req)
    def _(b):
        code = jnp.broadcast_to(row_facts[pl.ds(b, 1), :], (rows, LANES)).T.astype(jnp.int32)
        row_code[b] = code
        distance = LANES + row_iota + b * rows - (code >> 11) - lane_iota
        for head in range(2):
            terms = bias_of(distance, head, 0)
            for r in range(2):
                tail_bias[b, stacked(r, head), :] = terms[r * half : (r + 1) * half]

    first_head = lane_iota < DK

    def query_heads(b, r):
        q = q_all[pl.ds(pl.multiple_of(b * rows + r * half, half), half), :]
        nothing = jnp.zeros_like(q)
        first = first_head[:half]
        return jnp.concatenate(
            [jnp.where(first, q, nothing), jnp.where(first, nothing, q)], axis=0
        )

    for copy in own_copies:
        copy.wait()
    for copy in incoming(kc_copy):
        copy.wait_recv()
    for which in range(PREF_GRP):
        k_cross[pl.ds(which * LANES, LANES), :] = k_cache[which].T
    for make in (q_copy, vc_copy):
        for copy in incoming(make):
            copy.wait_recv()

    far_keys = PLEN - LANES

    def far_scores(b):
        qh = jnp.concatenate([query_heads(b, 0), query_heads(b, 1)], axis=0)
        choice = row_code[b] & 1024
        zero_first = (
            jnp.concatenate([choice[:half], choice[:half], choice[half:], choice[half:]], axis=0) == 0
        )
        nothing = jnp.zeros_like(qh)
        q2 = jnp.concatenate(
            [jnp.where(zero_first, qh, nothing), jnp.where(zero_first, nothing, qh)], axis=1
        )
        scores = jnp.dot(q2, k_cross[...], preferred_element_type=jnp.float32)
        scores = jnp.concatenate(
            [scores[:, :far_keys], scores[:, far_keys:] + tail_bias[b]], axis=1
        )
        return zero_first, scores

    def far_terms(scores):
        top = jnp.max(scores, axis=1, keepdims=True)
        terms = jnp.exp(scores - top)
        return top, jnp.sum(terms, axis=1, keepdims=True), terms.astype(jnp.bfloat16)

    far_step = 2

    @pl.loop(0, n_req // far_step)
    def _(step):
        blocks = [step * far_step + i for i in range(far_step)]
        values = jnp.concatenate([v_cache[0], v_cache[1]], axis=1)
        scored = [far_scores(b) for b in blocks]
        termed = [far_terms(scores) for _, scores in scored]
        accs = [jnp.dot(t[2], values, preferred_element_type=jnp.float32) for t in termed]
        for b, (zero_first, _), (top, total, _), acc in zip(blocks, scored, termed, accs):
            row_max[b] = jnp.broadcast_to(top, (2 * rows, LANES))
            row_sum[b] = jnp.broadcast_to(total, (2 * rows, LANES))
            row_acc[b] = jnp.where(zero_first, acc[:, :LANES], acc[:, LANES:])

    for head in range(2):
        for part in range(3):
            ahead = lane_iota + (part - 1) * rows - row_iota
            distance = jnp.abs(ahead)
            if part == 0:
                both = bias_of(distance, head, 0)
            elif part == 2:
                both = bias_of(distance, head, 16)
            else:
                both = jnp.where(ahead > 0, bias_of(distance, head, 16), bias_of(distance, head, 0))
            for r in range(2):
                near_bias[0, stacked(r, head), pl.ds(part * LANES, LANES)] = both[r * half : (r + 1) * half]

    @pl.loop(0, n_req)
    def _(step):
        b = n_req - 1 - step
        number = row_code[b] & 1023
        for part in range(3):
            other = key_req[pl.ds(0, 1), pl.ds(pl.multiple_of(b * rows + part * LANES, LANES), LANES)]
            same = other == number
            cols = pl.ds(part * LANES, LANES)
            for r in range(2):
                same_half = same[r * half : (r + 1) * half]
                for head in range(2):
                    near_bias[b, stacked(r, head), cols] = jnp.where(
                        same_half, near_bias[0, stacked(r, head), cols], masked_score
                    )

    for make in (k_copy, v_copy):
        for copy in incoming(make):
            copy.wait_recv()

    def near(blocks, r):
        here = pl.ds(r * rows, rows)
        windows = [pl.ds(pl.multiple_of(b * rows, rows), 3 * rows) for b in blocks]
        scores = [
            jnp.dot(query_heads(b, r), k_all[:, w], preferred_element_type=jnp.float32)
            + near_bias[b, here, :]
            for b, w in zip(blocks, windows)
        ]
        olds = [row_max[b, here, :] for b in blocks]
        tops = [jnp.maximum(o, jnp.max(x, axis=1, keepdims=True)) for o, x in zip(olds, scores)]
        terms = [jnp.exp(x - jnp.concatenate([t, t, t], axis=1)) for x, t in zip(scores, tops)]
        shrinks = [jnp.exp(o - t) for o, t in zip(olds, tops)]
        sums = [
            row_sum[b, here, :] * z + jnp.sum(x, axis=1, keepdims=True)
            for b, z, x in zip(blocks, shrinks, terms)
        ]
        accs = [
            row_acc[b, here, :] * z
            + jnp.dot(x.astype(jnp.bfloat16), v_all[w, :], preferred_element_type=jnp.float32)
            for b, z, x, w in zip(blocks, shrinks, terms, windows)
        ]
        results = [a / x for a, x in zip(accs, sums)]
        return [jnp.where(first_head[:half], x[:half], x[half:]).astype(jnp.bfloat16) for x in results]

    near_step = 4
    for r in range(2):
        for begin in range(1, n_req + 1, near_step):
            turns = range(begin, begin + near_step)
            blocks = [lax.rem(me + d, n_req) for d in turns]
            for d, b, result in zip(turns, blocks, near(blocks, r)):
                if d < n_req:
                    o_send[b, parts[r], :] = result
                else:
                    att[parts[r], lanes_of(me)] = result
            for d, b in zip(turns, blocks):
                if d < n_req:
                    o_copy(r)(d, b, me).start()

    mine = [
        remote(n_two.at[0, parts[r]], n_two.at[1, parts[r]], f_send.at[10 + r], f_recv.at[10 + r], grp=mate)
        for r in range(2)
    ]
    cross = [
        remote(n_two.at[0, parts[r]], n_two.at[2, parts[r]], f_send.at[1 + r], f_recv.at[1 + r], grp=across)
        for r in range(2)
    ]
    relay = [
        remote(n_two.at[2, parts[r]], n_two.at[3, parts[r]], f_send.at[3 + r], f_recv.at[3 + r], grp=mate)
        for r in range(2)
    ]
    back = remote(fast_out, fast_in, f_send.at[5], f_recv.at[5], grp=mate)
    swap = [
        remote(chip_out.at[r], chip_in.at[r], f_send.at[6 + r], f_recv.at[6 + r], grp=mate) for r in range(2)
    ]
    home = [
        remote(far_out.at[r], far_in.at[r], f_send.at[8 + r], f_recv.at[8 + r], grp=across) for r in range(2)
    ]

    loads[5].wait()

    @pl.loop(0, w_in.shape[0] // tile)
    def _(t):
        cols = pl.ds(pl.multiple_of(t * tile, tile), tile)
        w_up[:, cols] = w_in[cols, :].T

    loads[4].wait()
    for r in range(2):
        for copy in incoming(o_copy(r)):
            copy.wait_recv()

        @pl.loop(0, D // tile)
        def _(t, r=r):
            cols = pl.ds(pl.multiple_of(t * tile, tile), tile)
            h_one[parts[r], cols] = (
                tok[parts[r], cols].astype(jnp.float32)
                + jnp.dot(
                    att[parts[r], :], w_attn[3, :, cols], preferred_element_type=jnp.float32
                )
            ).astype(jnp.bfloat16)

        wide = h_one[parts[r], :].astype(jnp.float32)
        scale = lax.rsqrt(jnp.mean(wide * wide, axis=-1, keepdims=True) + epsilon)
        n_two[0, parts[r], :] = (wide * scale * mlp_gain[...]).astype(jnp.bfloat16)
        cross[r].start()
        mine[r].start()

    loads[6].wait()

    def up(rows_in):
        @pl.loop(0, w_in.shape[0] // tile)
        def _(t):
            cols = pl.ds(pl.multiple_of(t * tile, tile), tile)
            units[:, cols] = jnp.maximum(
                jnp.dot(rows_in, w_up[:, cols], preferred_element_type=jnp.float32), 0.0
            ).astype(jnp.bfloat16)

    def down(out):
        @pl.loop(0, D // tile)
        def _(t):
            cols = pl.ds(pl.multiple_of(t * tile, tile), tile)
            out[:, cols] = jnp.dot(
                units[...], w_out[:, cols], preferred_element_type=jnp.float32
            ).astype(out.dtype)

    def far_rows(r):
        return jnp.concatenate([n_two[2, parts[r]], n_two[3, parts[r]]], axis=0)

    def send_home(r):
        swap[r].wait_recv()
        far_out[r] = (part_far[r, pl.ds(0, half), :] + chip_in[r].astype(jnp.float32)).astype(jnp.bfloat16)
        home[r].start()

    def finish_far(r):
        down(part_far.at[r])
        chip_out[r] = part_far[r, pl.ds(half, half), :].astype(jnp.bfloat16)
        swap[r].start()

    up(n_two[0])
    cross[0].wait_recv()
    relay[0].start()
    down(part_own)
    for copy in mine:
        copy.wait_recv()
    up(n_two[1])
    down(fast_out)
    back.start()
    cross[1].wait_recv()
    relay[1].start()
    relay[0].wait_recv()
    up(far_rows(0))
    finish_far(0)
    relay[1].wait_recv()
    up(far_rows(1))
    send_home(0)
    finish_far(1)
    back.wait_recv()
    part_own[...] = (
        part_own[...] + h_one[...].astype(jnp.float32) + fast_in[...].astype(jnp.float32)
    )
    send_home(1)
    for r in range(2):
        home[r].wait_recv()
        out_ref[parts[r], :] = (
            part_own[parts[r], :] + far_in[r].astype(jnp.float32)
        ).astype(jnp.bfloat16)

    for make in (kc_copy, vc_copy, q_copy, k_copy, v_copy, o_copy(0), o_copy(1)):
        for copy in outgoing(make):
            copy.wait_send()
    for copy in [back] + mine + cross + relay + swap + home:
        copy.wait_send()


def fused(
    tokens,
    attn_gain,
    w_query,
    w_key,
    w_value,
    w_attn_out,
    rel_bias,
    prefix_cache,
    lengths,
    prefix_map,
    mlp_gain,
    w_in,
    w_out,
):
    n_req = lax.axis_size("req")
    rows = tokens.shape[0]
    group = n_req * rows
    hbm = pl.BlockSpec(memory_space=pl.ANY)
    vmem = pl.BlockSpec(memory_space=pltpu.VMEM)
    smem = pl.BlockSpec(memory_space=pltpu.SMEM)
    half = rows // 2
    bf16, f32 = jnp.bfloat16, jnp.float32
    sems = pltpu.SemaphoreType.DMA
    return pl.pallas_call(
        functools.partial(layer_kernel, n_req),
        out_shape=jax.ShapeDtypeStruct((rows, D), bf16),
        in_specs=[hbm, vmem, hbm, hbm, hbm, hbm, smem, hbm, smem, smem, vmem, hbm, hbm],
        out_specs=vmem,
        scratch_shapes=[
            pltpu.VMEM((rows, D), bf16),
            pltpu.VMEM((4, D, D), bf16),
            pltpu.VMEM(w_in.shape, bf16),
            pltpu.VMEM(w_out.shape, bf16),
            pltpu.VMEM((rows, D), bf16),
            pltpu.VMEM((2, rows, D), bf16),
            pltpu.VMEM((PREF_GRP, PLEN, LANES), bf16),
            pltpu.VMEM((PREF_GRP, PLEN, LANES), bf16),
            pltpu.VMEM((group, LANES), bf16),
            pltpu.VMEM((D, rows), bf16),
            pltpu.VMEM((LANES, group + 2 * rows), bf16),
            pltpu.VMEM((group + 2 * rows, LANES), bf16),
            pltpu.VMEM((PREF_GRP * LANES, PLEN), bf16),
            pltpu.VMEM(w_in.shape[::-1], bf16),
            pltpu.VMEM((n_req, 2 * rows, LANES), f32),
            pltpu.VMEM((n_req, 2 * rows, 3 * LANES), f32),
            pltpu.VMEM((8, group + 2 * rows), jnp.int32),
            pltpu.VMEM((n_req, LANES), f32),
            pltpu.VMEM((n_req, rows, LANES), jnp.int32),
            pltpu.VMEM((n_req, 2 * rows, LANES), f32),
            pltpu.VMEM((n_req, 2 * rows, LANES), f32),
            pltpu.VMEM((n_req, 2 * rows, LANES), f32),
            pltpu.VMEM((n_req, rows, LANES), bf16),
            pltpu.VMEM((rows, D), bf16),
            pltpu.VMEM((rows, D), bf16),
            pltpu.VMEM((4, rows, D), bf16),
            pltpu.VMEM((rows, w_in.shape[0]), bf16),
            pltpu.VMEM((rows, D), f32),
            pltpu.VMEM((2, rows, D), f32),
            pltpu.VMEM((rows, D), bf16),
            pltpu.VMEM((rows, D), bf16),
            pltpu.VMEM((2, half, D), bf16),
            pltpu.VMEM((2, half, D), bf16),
            pltpu.VMEM((2, half, D), bf16),
            pltpu.VMEM((2, half, D), bf16),
            sems((7,)),
            sems((2,)),
        ]
        + [sems((n_req,)) for _ in range(10)]
        + [sems((2, n_req)) for _ in range(2)]
        + [sems((12,)), sems((12,))],
        compiler_params=pltpu.CompilerParams(
            collective_id=0, has_side_effects=True, vmem_limit_bytes=63 * 1024 * 1024
        ),
    )(
        tokens,
        attn_gain.reshape(1, D),
        w_query,
        w_key,
        w_value,
        w_attn_out,
        rel_bias.T,
        prefix_cache,
        lengths,
        prefix_map,
        mlp_gain.reshape(1, D),
        w_in,
        w_out,
    )


def pairs_fit(mesh):
    return mesh.shape["req"] * LANES == D and mesh.shape["grp"] == 4


def solution(mesh):
    return jax.shard_map(
        fused if pairs_fit(mesh) else body,
        mesh=mesh,
        in_specs=(
            P(("grp", "req"), None),
            P(),
            P(),
            P(),
            P(),
            P(),
            P(),
            P("grp", "req", None),
            P("grp", None),
            P("grp", None),
            P(),
            P("grp", None),
            P("grp", None),
        ),
        out_specs=P(("grp", "req"), None),
        check_vma=False,
    )
```

```python
import functools

import jax
import jax.numpy as jnp
from jax import lax
from jax.experimental import pallas as pl
from jax.experimental.pallas import tpu as pltpu
from jax.sharding import PartitionSpec as P

D = 1024
H = 16
DK = 64
PLEN = 512
PREF_GRP = 2
LANES = 128
MESH = pl.DeviceIdType.MESH


epsilon = 1e-06
far_marks = (12, 16, 23, 32, 46, 64, 91)
masked_score = -1e30


def padded(value, sides, width):
    for axis, dim in sides:
        count, length = (lax.axis_size(axis), value.shape[dim])
        up = [(i, (i + 1) % count) for i in range(count - 1)]
        down = [(j, i) for i, j in up]
        last = lax.slice_in_dim(value, length - width, length, axis=dim)
        leading = lax.slice_in_dim(value, 0, width, axis=dim)
        before = lax.ppermute(last, axis, up)
        after = lax.ppermute(leading, axis, down)
        value = jnp.concatenate([before, value, after], axis=dim)
    return value


def bucket_of(relative):
    distance = jnp.abs(relative)
    far_bucket = 8 + sum([(distance >= threshold).astype(jnp.int32) for threshold in far_marks])
    bucket = jnp.where(distance < 8, distance, far_bucket)
    return bucket + jnp.where(relative > 0, 16, 0)


def bias_lookup(relative, rel_bias):
    buckets = bucket_of(relative)
    marks = jnp.arange(rel_bias.shape[0], dtype=jnp.int32)
    one_hot = (buckets[:, :, None] == marks[None, None, :]).astype(jnp.float32)
    return jnp.einsum(
        "qkb,bh->hqk",
        one_hot,
        rel_bias,
        precision=lax.Precision.HIGHEST,
        preferred_element_type=jnp.float32,
    )


def norm_rows(values_in, gain):
    widened = values_in.astype(jnp.float32)
    scale = lax.rsqrt(jnp.mean(widened * widened, axis=-1, keepdims=True) + epsilon)
    return (widened * scale * gain).astype(jnp.bfloat16)


def layout(lengths_row, prefix_row, row_ids):
    req_ends = jnp.cumsum(lengths_row)
    req_starts = req_ends - lengths_row
    member = (
        (row_ids[:, None] >= req_starts[None, :]) & (row_ids[:, None] < req_ends[None, :])
    ).astype(jnp.int32)
    numbers = jnp.arange(lengths_row.shape[0], dtype=jnp.int32)
    req_index = jnp.sum(member * numbers[None, :], axis=1) + jnp.sum(member, axis=1) - 1
    offset = row_ids - jnp.sum(member * req_starts[None, :], axis=1)
    chosen = jnp.sum(member * prefix_row[None, :], axis=1)
    return (req_index, offset, chosen)


def softmax_part(scores, value_rows, allowed):
    scores = jnp.where(allowed[None], scores, masked_score)
    row_max = jnp.max(scores, axis=2)
    exp_terms = jnp.where(allowed[None], jnp.exp(scores - row_max[:, :, None]), 0.0)
    row_sum = jnp.sum(exp_terms, axis=2)
    weighted = jnp.einsum(
        "hqk,khd->hqd",
        exp_terms.astype(jnp.bfloat16),
        value_rows,
        preferred_element_type=jnp.float32,
    )
    return (row_max, row_sum, weighted)


def combine(first_part, second_part):
    row_max = jnp.maximum(first_part[0], second_part[0])
    scale_one = jnp.exp(first_part[0] - row_max)
    scale_two = jnp.exp(second_part[0] - row_max)
    row_sum = first_part[1] * scale_one + second_part[1] * scale_two
    weighted = first_part[2] * scale_one[:, :, None] + second_part[2] * scale_two[:, :, None]
    return (row_max, row_sum, weighted)


def feed_forward(rows_in, in_part, out_part):
    units = lax.dot_general(
        rows_in, in_part, (((1,), (1,)), ((), ())), preferred_element_type=jnp.float32
    )
    units = jnp.maximum(units, 0.0).astype(jnp.bfloat16)
    return jnp.dot(units, out_part, preferred_element_type=jnp.float32)


def body(
    tokens,
    attn_gain,
    w_query,
    w_key,
    w_value,
    w_attn_out,
    rel_bias,
    prefix_cache,
    lengths,
    prefix_map,
    mlp_gain,
    w_in,
    w_out,
):
    rows_here = tokens.shape[0]
    device_pos = lax.axis_index("req")
    group_lengths = lengths[0]
    group_map = prefix_map[0]
    normed = norm_rows(tokens, attn_gain)
    query = (
        jnp.dot(normed, w_query, preferred_element_type=jnp.float32)
        .astype(jnp.bfloat16)
        .reshape(rows_here, H, DK)
    )
    key_value = jnp.concatenate(
        [
            jnp.dot(normed, w_key, preferred_element_type=jnp.float32).astype(jnp.bfloat16),
            jnp.dot(normed, w_value, preferred_element_type=jnp.float32).astype(jnp.bfloat16),
        ],
        axis=1,
    )
    query_ids = device_pos * rows_here + jnp.arange(rows_here, dtype=jnp.int32)
    query_req, query_offset, query_prefix = layout(group_lengths, group_map, query_ids)
    all_positions = jnp.arange(PLEN, dtype=jnp.int32)
    prefix_bias = bias_lookup(all_positions[None, :] - PLEN - query_offset[:, None], rel_bias)
    empty_state = (
        jnp.full((H, rows_here), masked_score, jnp.float32),
        jnp.zeros((H, rows_here), jnp.float32),
        jnp.zeros((H, rows_here, DK), jnp.float32),
    )
    running = empty_state
    shard_kv = lax.all_gather(prefix_cache, "req", axis=1, tiled=True)
    prefix_ids = jnp.arange(PREF_GRP, dtype=jnp.int32)
    slices = shard_kv.shape[0]
    piece_len = shard_kv.shape[1]
    step_len = max(min(piece_len, 512 // slices), 1)
    for begin in range(0, piece_len, step_len):
        width = min(step_len, piece_len - begin)
        block = shard_kv[:, begin : begin + width]
        key_rows = block[:, :, :D].reshape(slices, width, H, DK)
        value_rows = block[:, :, D:].reshape(-1, H, DK)
        rel_terms = lax.dynamic_slice_in_dim(prefix_bias, begin, width, 2)
        prefix_scores = jnp.einsum(
            "qhd,swhd->hqsw", query, key_rows, preferred_element_type=jnp.float32
        )
        prefix_scores = (prefix_scores + rel_terms[:, :, None, :]).reshape(
            H, rows_here, slices * width
        )
        allowed = jnp.repeat(query_prefix[:, None] == prefix_ids[None, :], width, axis=1)
        running = combine(running, softmax_part(prefix_scores, value_rows, allowed))
    state = running
    window = padded(key_value, (("req", 0),), rows_here)
    window_ids = device_pos * rows_here - rows_here + jnp.arange(3 * rows_here, dtype=jnp.int32)
    window_req = layout(group_lengths, group_map, window_ids)[0]
    for part_idx in range(3):
        part_rows = window[part_idx * rows_here : (part_idx + 1) * rows_here]
        part_ids = window_ids[part_idx * rows_here : (part_idx + 1) * rows_here]
        part_req = window_req[part_idx * rows_here : (part_idx + 1) * rows_here]
        suffix_terms = bias_lookup(part_ids[None, :] - query_ids[:, None], rel_bias)
        suffix_allowed = part_req[None, :] == query_req[:, None]
        scores = (
            jnp.einsum(
                "qhd,khd->hqk",
                query,
                part_rows[:, :D].reshape(-1, H, DK),
                preferred_element_type=jnp.float32,
            )
            + suffix_terms
        )
        suffix_state = softmax_part(scores, part_rows[:, D:].reshape(-1, H, DK), suffix_allowed)
        state = combine(state, suffix_state)
    attended = (
        (state[2] / state[1][:, :, None])
        .transpose(1, 0, 2)
        .reshape(rows_here, D)
        .astype(jnp.bfloat16)
    )
    hidden_one = (
        tokens.astype(jnp.float32)
        + jnp.dot(attended, w_attn_out, preferred_element_type=jnp.float32)
    ).astype(jnp.bfloat16)
    normed_two = norm_rows(hidden_one, mlp_gain)
    gathered = lax.all_gather(normed_two, "grp", axis=0, tiled=True)
    mlp_total = lax.psum_scatter(
        feed_forward(gathered, w_in, w_out).astype(jnp.bfloat16),
        "grp",
        scatter_dimension=0,
        tiled=True,
    ).astype(jnp.float32)
    return (hidden_one.astype(jnp.float32) + mlp_total).astype(jnp.bfloat16)


def bucket_steps():
    return tuple((i, i) for i in range(1, 9)) + tuple((t, 9 + i) for i, t in enumerate(far_marks))


def chain(distance, table, head, first):
    value = jnp.full(distance.shape, table[head, first], jnp.float32)
    for threshold, number in bucket_steps():
        value = jnp.where(distance >= threshold, table[head, first + number], value)
    return value


def layer_kernel(
    n_req,
    tokens_hbm,
    attn_gain,
    wq_hbm,
    wk_hbm,
    wv_hbm,
    wo_hbm,
    rel_bias,
    cache_hbm,
    lengths,
    prefix_map,
    mlp_gain,
    win_hbm,
    wout_hbm,
    out_ref,
    tok,
    w_attn,
    w_in,
    w_out,
    normed,
    stage,
    k_cache,
    v_cache,
    q_all,
    k_side,
    k_all,
    v_all,
    k_cross,
    w_up,
    tail_bias,
    near_bias,
    key_req,
    row_facts,
    row_code,
    row_max,
    row_sum,
    row_acc,
    o_send,
    att,
    h_one,
    n_two,
    units,
    part_own,
    part_far,
    fast_out,
    fast_in,
    chip_out,
    chip_in,
    far_out,
    far_in,
    load_sem,
    own_sem,
    kc_send,
    kc_recv,
    vc_send,
    vc_recv,
    q_send,
    q_recv,
    k_send,
    k_recv,
    v_send,
    v_recv,
    o_ssem,
    o_rsem,
    f_send,
    f_recv,
):
    me = lax.axis_index("req")
    grp = lax.axis_index("grp")
    side = lax.rem(grp, 2)
    plane = lax.div(grp, 2)
    mate = plane * 2 + (1 - side)
    across = (1 - plane) * 2 + side
    rows = tokens_hbm.shape[0]
    piece = cache_hbm.shape[1]
    half = rows // 2

    def flipped(d):
        other, bit = 0, 1
        while bit < n_req:
            digit = lax.rem(lax.div(me, bit), 2)
            other = other + bit * (1 - digit if d & bit else digit)
            bit = 2 * bit
        return other

    far_first = list(range(n_req // 2, n_req))
    turn_order = [far_first[0]]
    for near_turn, far_turn in zip(range(1, n_req // 2), far_first[1:]):
        turn_order += [near_turn, far_turn]

    def remote(src, dst, ssem, rsem, **where):
        return pltpu.make_async_remote_copy(
            src_ref=src, dst_ref=dst, send_sem=ssem, recv_sem=rsem, device_id=where, device_id_type=MESH
        )

    def lanes_of(index):
        return pl.ds(pl.multiple_of(index * LANES, LANES), LANES)

    def rows_of(index):
        return pl.ds(pl.multiple_of(index * rows, rows), rows)

    loads = [
        pltpu.make_async_copy(src, dst, load_sem.at[i])
        for i, (src, dst) in enumerate(
            [
                (tokens_hbm, tok),
                (wq_hbm, w_attn.at[0]),
                (wk_hbm, w_attn.at[1]),
                (wv_hbm, w_attn.at[2]),
                (wo_hbm, w_attn.at[3]),
                (win_hbm, w_in),
                (wout_hbm, w_out),
            ]
        )
    ]
    for load in loads[:4]:
        load.start()

    barrier = pltpu.get_barrier_semaphore()
    for d in range(1, n_req):
        pl.semaphore_signal(
            barrier, inc=1, device_id={"req": flipped(d)}, device_id_type=MESH
        )
    for other in (mate, across):
        pl.semaphore_signal(barrier, inc=1, device_id={"grp": other}, device_id_type=MESH)
    pl.semaphore_wait(barrier, n_req + 1)

    def cache_copy(buf, first, sends, recvs, d, peer, owner):
        return remote(
            cache_hbm.at[:, :, pl.ds(pl.multiple_of(first + peer * LANES, LANES), LANES)],
            buf.at[:, pl.ds(pl.multiple_of(owner * piece, piece), piece), :],
            sends.at[d],
            recvs.at[d],
            req=peer,
        )

    def q_copy(d, peer, owner):
        return remote(
            stage.at[0, :, lanes_of(peer)], q_all.at[rows_of(owner), :], q_send.at[d], q_recv.at[d], req=peer
        )

    def k_copy(d, peer, owner):
        return remote(
            k_side.at[lanes_of(peer), :], k_all.at[:, lanes_of(owner + 1)], k_send.at[d], k_recv.at[d], req=peer
        )

    def v_copy(d, peer, owner):
        return remote(
            stage.at[1, :, lanes_of(peer)], v_all.at[rows_of(owner + 1), :], v_send.at[d], v_recv.at[d], req=peer
        )

    parts = [pl.ds(r * half, half) for r in range(2)]

    def o_copy(r):
        def make(d, peer, owner):
            return remote(
                o_send.at[peer, parts[r]],
                att.at[parts[r], lanes_of(owner)],
                o_ssem.at[r, d],
                o_rsem.at[r, d],
                req=peer,
            )

        return make

    def outgoing(make):
        return [make(d, flipped(d), me) for d in turn_order]

    def incoming(make):
        return [make(d, flipped(d), flipped(d)) for d in turn_order]

    def kc_copy(d, peer, owner):
        return cache_copy(k_cache, 0, kc_send, kc_recv, d, peer, owner)

    def vc_copy(d, peer, owner):
        return cache_copy(v_cache, D, vc_send, vc_recv, d, peer, owner)

    for copy in outgoing(kc_copy) + outgoing(vc_copy):
        copy.start()
    own_copies = [
        pltpu.make_async_copy(
            cache_hbm.at[:, :, pl.ds(pl.multiple_of(first + me * LANES, LANES), LANES)],
            buf.at[:, pl.ds(pl.multiple_of(me * piece, piece), piece), :],
            own_sem.at[i],
        )
        for i, (buf, first) in enumerate([(k_cache, 0), (v_cache, D)])
    ]
    for copy in own_copies:
        copy.start()

    loads[0].wait()
    wide = tok[...].astype(jnp.float32)
    scale = lax.rsqrt(jnp.mean(wide * wide, axis=-1, keepdims=True) + epsilon)
    normed[...] = (wide * scale * attn_gain[...]).astype(jnp.bfloat16)

    tile = 512
    makers = (q_copy, k_copy, v_copy)
    for part in range(3):
        loads[1 + part].wait()

        @pl.loop(0, D // tile)
        def _(t, part=part):
            cols = pl.ds(pl.multiple_of(t * tile, tile), tile)
            made = jnp.dot(
                normed[...], w_attn[part, :, cols], preferred_element_type=jnp.float32
            ).astype(jnp.bfloat16)
            if part == 1:
                k_side[cols, :] = made.T
            else:
                stage[part // 2, :, cols] = made

        for copy in outgoing(makers[part]):
            copy.start()
        if part == 0:
            for load in loads[4:]:
                load.start()
    q_all[rows_of(me), :] = stage[0, :, lanes_of(me)]
    k_all[:, lanes_of(me + 1)] = k_side[lanes_of(me), :]
    v_all[rows_of(me + 1), :] = stage[1, :, lanes_of(me)]
    zeros = jnp.zeros((rows, LANES), jnp.bfloat16)
    for outer in (0, n_req + 1):
        k_all[:, pl.ds(outer * rows, rows)] = zeros
        v_all[pl.ds(outer * rows, rows), :] = zeros

    ends = []
    total = 0
    n_requests = lengths.shape[1]
    for j in range(n_requests):
        total = total + lengths[0, j]
        ends.append(total)
    key_ids = lax.broadcasted_iota(jnp.int32, key_req.shape, 1) - rows
    key_number = jnp.where(key_ids < 0, -1, 0)
    for end in ends:
        key_number = key_number + jnp.where(key_ids >= end, 1, 0)
    key_req[...] = key_number

    def stacked(r, head):
        return pl.ds((2 * r + head) * half, half)

    row_iota = lax.broadcasted_iota(jnp.int32, (rows, LANES), 0)
    lane_iota = lax.broadcasted_iota(jnp.int32, (rows, LANES), 1)
    ids = lax.broadcasted_iota(jnp.int32, row_facts.shape, 0) * rows + lax.broadcasted_iota(
        jnp.int32, row_facts.shape, 1
    )
    number = jnp.zeros_like(ids)
    start = jnp.zeros_like(ids)
    prefix = jnp.full(ids.shape, prefix_map[0, 0], jnp.int32)
    for j in range(n_requests):
        past = ids >= ends[j]
        number = number + jnp.where(past, 1, 0)
        start = start + jnp.where(past, lengths[0, j], 0)
        if j + 1 < n_requests:
            prefix = jnp.where(past, prefix_map[0, j + 1], prefix)
    row_facts[...] = ((start * 2 + prefix) * 1024 + number).astype(jnp.float32)

    def bias_of(distance, head, first):
        return chain(distance, rel_bias, 2 * me + head, first) - rel_bias[2 * me + head, 15]

    @pl.loop(0, n_req)
    def _(b):
        code = jnp.broadcast_to(row_facts[pl.ds(b, 1), :], (rows, LANES)).T.astype(jnp.int32)
        row_code[b] = code
        distance = LANES + row_iota + b * rows - (code >> 11) - lane_iota
        for head in range(2):
            terms = bias_of(distance, head, 0)
            for r in range(2):
                tail_bias[b, stacked(r, head), :] = terms[r * half : (r + 1) * half]

    first_head = lane_iota < DK

    def query_heads(b, r):
        q = q_all[pl.ds(pl.multiple_of(b * rows + r * half, half), half), :]
        nothing = jnp.zeros_like(q)
        first = first_head[:half]
        return jnp.concatenate(
            [jnp.where(first, q, nothing), jnp.where(first, nothing, q)], axis=0
        )

    for copy in own_copies:
        copy.wait()
    for copy in incoming(kc_copy):
        copy.wait_recv()
    for which in range(PREF_GRP):
        k_cross[pl.ds(which * LANES, LANES), :] = k_cache[which].T
    for make in (q_copy, vc_copy):
        for copy in incoming(make):
            copy.wait_recv()

    far_keys = PLEN - LANES

    def far_scores(b):
        qh = jnp.concatenate([query_heads(b, 0), query_heads(b, 1)], axis=0)
        choice = row_code[b] & 1024
        zero_first = (
            jnp.concatenate([choice[:half], choice[:half], choice[half:], choice[half:]], axis=0) == 0
        )
        nothing = jnp.zeros_like(qh)
        q2 = jnp.concatenate(
            [jnp.where(zero_first, qh, nothing), jnp.where(zero_first, nothing, qh)], axis=1
        )
        scores = jnp.dot(q2, k_cross[...], preferred_element_type=jnp.float32)
        scores = jnp.concatenate(
            [scores[:, :far_keys], scores[:, far_keys:] + tail_bias[b]], axis=1
        )
        return zero_first, scores

    def far_terms(scores):
        top = jnp.max(scores, axis=1, keepdims=True)
        terms = jnp.exp(scores - top)
        return top, jnp.sum(terms, axis=1, keepdims=True), terms.astype(jnp.bfloat16)

    far_step = 2

    @pl.loop(0, n_req // far_step)
    def _(step):
        blocks = [step * far_step + i for i in range(far_step)]
        values = jnp.concatenate([v_cache[0], v_cache[1]], axis=1)
        scored = [far_scores(b) for b in blocks]
        termed = [far_terms(scores) for _, scores in scored]
        accs = [jnp.dot(t[2], values, preferred_element_type=jnp.float32) for t in termed]
        for b, (zero_first, _), (top, total, _), acc in zip(blocks, scored, termed, accs):
            row_max[b] = jnp.broadcast_to(top, (2 * rows, LANES))
            row_sum[b] = jnp.broadcast_to(total, (2 * rows, LANES))
            row_acc[b] = jnp.where(zero_first, acc[:, :LANES], acc[:, LANES:])

    for head in range(2):
        for part in range(3):
            ahead = lane_iota + (part - 1) * rows - row_iota
            distance = jnp.abs(ahead)
            if part == 0:
                both = bias_of(distance, head, 0)
            elif part == 2:
                both = bias_of(distance, head, 16)
            else:
                both = jnp.where(ahead > 0, bias_of(distance, head, 16), bias_of(distance, head, 0))
            for r in range(2):
                near_bias[0, stacked(r, head), pl.ds(part * LANES, LANES)] = both[r * half : (r + 1) * half]

    @pl.loop(0, n_req)
    def _(step):
        b = n_req - 1 - step
        number = row_code[b] & 1023
        for part in range(3):
            other = key_req[pl.ds(0, 1), pl.ds(pl.multiple_of(b * rows + part * LANES, LANES), LANES)]
            same = other == number
            cols = pl.ds(part * LANES, LANES)
            for r in range(2):
                same_half = same[r * half : (r + 1) * half]
                for head in range(2):
                    near_bias[b, stacked(r, head), cols] = jnp.where(
                        same_half, near_bias[0, stacked(r, head), cols], masked_score
                    )

    for make in (k_copy, v_copy):
        for copy in incoming(make):
            copy.wait_recv()

    def near(blocks, r):
        here = pl.ds(r * rows, rows)
        windows = [pl.ds(pl.multiple_of(b * rows, rows), 3 * rows) for b in blocks]
        scores = [
            jnp.dot(query_heads(b, r), k_all[:, w], preferred_element_type=jnp.float32)
            + near_bias[b, here, :]
            for b, w in zip(blocks, windows)
        ]
        olds = [row_max[b, here, :] for b in blocks]
        tops = [jnp.maximum(o, jnp.max(x, axis=1, keepdims=True)) for o, x in zip(olds, scores)]
        terms = [jnp.exp(x - jnp.concatenate([t, t, t], axis=1)) for x, t in zip(scores, tops)]
        shrinks = [jnp.exp(o - t) for o, t in zip(olds, tops)]
        sums = [
            row_sum[b, here, :] * z + jnp.sum(x, axis=1, keepdims=True)
            for b, z, x in zip(blocks, shrinks, terms)
        ]
        accs = [
            row_acc[b, here, :] * z
            + jnp.dot(x.astype(jnp.bfloat16), v_all[w, :], preferred_element_type=jnp.float32)
            for b, z, x, w in zip(blocks, shrinks, terms, windows)
        ]
        results = [a / x for a, x in zip(accs, sums)]
        return [jnp.where(first_head[:half], x[:half], x[half:]).astype(jnp.bfloat16) for x in results]

    near_step = 4
    for r in range(2):
        for begin in range(0, n_req, near_step):
            turns = (turn_order + [0])[begin : begin + near_step]
            blocks = [flipped(d) for d in turns]
            for d, b, result in zip(turns, blocks, near(blocks, r)):
                if d > 0:
                    o_send[b, parts[r], :] = result
                else:
                    att[parts[r], lanes_of(me)] = result
            for d, b in zip(turns, blocks):
                if d > 0:
                    o_copy(r)(d, b, me).start()

    mine = [
        remote(n_two.at[0, parts[r]], n_two.at[1, parts[r]], f_send.at[10 + r], f_recv.at[10 + r], grp=mate)
        for r in range(2)
    ]
    cross = [
        remote(n_two.at[0, parts[r]], n_two.at[2, parts[r]], f_send.at[1 + r], f_recv.at[1 + r], grp=across)
        for r in range(2)
    ]
    relay = [
        remote(n_two.at[2, parts[r]], n_two.at[3, parts[r]], f_send.at[3 + r], f_recv.at[3 + r], grp=mate)
        for r in range(2)
    ]
    back = remote(fast_out, fast_in, f_send.at[5], f_recv.at[5], grp=mate)
    swap = [
        remote(chip_out.at[r], chip_in.at[r], f_send.at[6 + r], f_recv.at[6 + r], grp=mate) for r in range(2)
    ]
    home = [
        remote(far_out.at[r], far_in.at[r], f_send.at[8 + r], f_recv.at[8 + r], grp=across) for r in range(2)
    ]

    loads[5].wait()

    @pl.loop(0, w_in.shape[0] // tile)
    def _(t):
        cols = pl.ds(pl.multiple_of(t * tile, tile), tile)
        w_up[:, cols] = w_in[cols, :].T

    loads[4].wait()
    for r in range(2):
        for copy in incoming(o_copy(r)):
            copy.wait_recv()

        @pl.loop(0, D // tile)
        def _(t, r=r):
            cols = pl.ds(pl.multiple_of(t * tile, tile), tile)
            h_one[parts[r], cols] = (
                tok[parts[r], cols].astype(jnp.float32)
                + jnp.dot(
                    att[parts[r], :], w_attn[3, :, cols], preferred_element_type=jnp.float32
                )
            ).astype(jnp.bfloat16)

        wide = h_one[parts[r], :].astype(jnp.float32)
        scale = lax.rsqrt(jnp.mean(wide * wide, axis=-1, keepdims=True) + epsilon)
        n_two[0, parts[r], :] = (wide * scale * mlp_gain[...]).astype(jnp.bfloat16)
        cross[r].start()
        mine[r].start()

    loads[6].wait()

    def up(rows_in):
        @pl.loop(0, w_in.shape[0] // tile)
        def _(t):
            cols = pl.ds(pl.multiple_of(t * tile, tile), tile)
            units[:, cols] = jnp.maximum(
                jnp.dot(rows_in, w_up[:, cols], preferred_element_type=jnp.float32), 0.0
            ).astype(jnp.bfloat16)

    def down(out):
        @pl.loop(0, D // tile)
        def _(t):
            cols = pl.ds(pl.multiple_of(t * tile, tile), tile)
            out[:, cols] = jnp.dot(
                units[...], w_out[:, cols], preferred_element_type=jnp.float32
            ).astype(out.dtype)

    def far_rows(r):
        return jnp.concatenate([n_two[2, parts[r]], n_two[3, parts[r]]], axis=0)

    def send_home(r):
        swap[r].wait_recv()
        far_out[r] = (part_far[r, pl.ds(0, half), :] + chip_in[r].astype(jnp.float32)).astype(jnp.bfloat16)
        home[r].start()

    def finish_far(r):
        down(part_far.at[r])
        chip_out[r] = part_far[r, pl.ds(half, half), :].astype(jnp.bfloat16)
        swap[r].start()

    up(n_two[0])
    cross[0].wait_recv()
    relay[0].start()
    down(part_own)
    for copy in mine:
        copy.wait_recv()
    up(n_two[1])
    down(fast_out)
    back.start()
    cross[1].wait_recv()
    relay[1].start()
    relay[0].wait_recv()
    up(far_rows(0))
    finish_far(0)
    relay[1].wait_recv()
    up(far_rows(1))
    send_home(0)
    finish_far(1)
    back.wait_recv()
    part_own[...] = (
        part_own[...] + h_one[...].astype(jnp.float32) + fast_in[...].astype(jnp.float32)
    )
    send_home(1)
    for r in range(2):
        home[r].wait_recv()
        out_ref[parts[r], :] = (
            part_own[parts[r], :] + far_in[r].astype(jnp.float32)
        ).astype(jnp.bfloat16)

    for make in (kc_copy, vc_copy, q_copy, k_copy, v_copy, o_copy(0), o_copy(1)):
        for copy in outgoing(make):
            copy.wait_send()
    for copy in [back] + mine + cross + relay + swap + home:
        copy.wait_send()


def fused(
    tokens,
    attn_gain,
    w_query,
    w_key,
    w_value,
    w_attn_out,
    rel_bias,
    prefix_cache,
    lengths,
    prefix_map,
    mlp_gain,
    w_in,
    w_out,
):
    n_req = lax.axis_size("req")
    rows = tokens.shape[0]
    group = n_req * rows
    hbm = pl.BlockSpec(memory_space=pl.ANY)
    vmem = pl.BlockSpec(memory_space=pltpu.VMEM)
    smem = pl.BlockSpec(memory_space=pltpu.SMEM)
    half = rows // 2
    bf16, f32 = jnp.bfloat16, jnp.float32
    sems = pltpu.SemaphoreType.DMA
    return pl.pallas_call(
        functools.partial(layer_kernel, n_req),
        out_shape=jax.ShapeDtypeStruct((rows, D), bf16),
        in_specs=[hbm, vmem, hbm, hbm, hbm, hbm, smem, hbm, smem, smem, vmem, hbm, hbm],
        out_specs=vmem,
        scratch_shapes=[
            pltpu.VMEM((rows, D), bf16),
            pltpu.VMEM((4, D, D), bf16),
            pltpu.VMEM(w_in.shape, bf16),
            pltpu.VMEM(w_out.shape, bf16),
            pltpu.VMEM((rows, D), bf16),
            pltpu.VMEM((2, rows, D), bf16),
            pltpu.VMEM((PREF_GRP, PLEN, LANES), bf16),
            pltpu.VMEM((PREF_GRP, PLEN, LANES), bf16),
            pltpu.VMEM((group, LANES), bf16),
            pltpu.VMEM((D, rows), bf16),
            pltpu.VMEM((LANES, group + 2 * rows), bf16),
            pltpu.VMEM((group + 2 * rows, LANES), bf16),
            pltpu.VMEM((PREF_GRP * LANES, PLEN), bf16),
            pltpu.VMEM(w_in.shape[::-1], bf16),
            pltpu.VMEM((n_req, 2 * rows, LANES), f32),
            pltpu.VMEM((n_req, 2 * rows, 3 * LANES), f32),
            pltpu.VMEM((8, group + 2 * rows), jnp.int32),
            pltpu.VMEM((n_req, LANES), f32),
            pltpu.VMEM((n_req, rows, LANES), jnp.int32),
            pltpu.VMEM((n_req, 2 * rows, LANES), f32),
            pltpu.VMEM((n_req, 2 * rows, LANES), f32),
            pltpu.VMEM((n_req, 2 * rows, LANES), f32),
            pltpu.VMEM((n_req, rows, LANES), bf16),
            pltpu.VMEM((rows, D), bf16),
            pltpu.VMEM((rows, D), bf16),
            pltpu.VMEM((4, rows, D), bf16),
            pltpu.VMEM((rows, w_in.shape[0]), bf16),
            pltpu.VMEM((rows, D), f32),
            pltpu.VMEM((2, rows, D), f32),
            pltpu.VMEM((rows, D), bf16),
            pltpu.VMEM((rows, D), bf16),
            pltpu.VMEM((2, half, D), bf16),
            pltpu.VMEM((2, half, D), bf16),
            pltpu.VMEM((2, half, D), bf16),
            pltpu.VMEM((2, half, D), bf16),
            sems((7,)),
            sems((2,)),
        ]
        + [sems((n_req,)) for _ in range(10)]
        + [sems((2, n_req)) for _ in range(2)]
        + [sems((12,)), sems((12,))],
        compiler_params=pltpu.CompilerParams(
            collective_id=0, has_side_effects=True, vmem_limit_bytes=63 * 1024 * 1024
        ),
    )(
        tokens,
        attn_gain.reshape(1, D),
        w_query,
        w_key,
        w_value,
        w_attn_out,
        rel_bias.T,
        prefix_cache,
        lengths,
        prefix_map,
        mlp_gain.reshape(1, D),
        w_in,
        w_out,
    )


def pairs_fit(mesh):
    return mesh.shape["req"] == D // LANES and mesh.shape["grp"] == 4


def solution(mesh):
    return jax.shard_map(
        fused if pairs_fit(mesh) else body,
        mesh=mesh,
        in_specs=(
            P(("grp", "req"), None),
            P(),
            P(),
            P(),
            P(),
            P(),
            P(),
            P("grp", "req", None),
            P("grp", None),
            P("grp", None),
            P(),
            P("grp", None),
            P("grp", None),
        ),
        out_specs=P(("grp", "req"), None),
        check_vma=False,
    )
```

```python
import functools

import jax
import jax.numpy as jnp
from jax import lax
from jax.experimental import pallas as pl
from jax.experimental.pallas import tpu as pltpu
from jax.sharding import PartitionSpec as P

D = 1024
H = 16
DK = 64
PLEN = 512
PREF_GRP = 2
LANES = 128
MESH = pl.DeviceIdType.MESH


epsilon = 1e-06
far_marks = (12, 16, 23, 32, 46, 64, 91)
masked_score = -1e30


def padded(value, sides, width):
    for axis, dim in sides:
        count, length = (lax.axis_size(axis), value.shape[dim])
        up = [(i, (i + 1) % count) for i in range(count - 1)]
        down = [(j, i) for i, j in up]
        last = lax.slice_in_dim(value, length - width, length, axis=dim)
        leading = lax.slice_in_dim(value, 0, width, axis=dim)
        before = lax.ppermute(last, axis, up)
        after = lax.ppermute(leading, axis, down)
        value = jnp.concatenate([before, value, after], axis=dim)
    return value


def bucket_of(relative):
    distance = jnp.abs(relative)
    far_bucket = 8 + sum([(distance >= threshold).astype(jnp.int32) for threshold in far_marks])
    bucket = jnp.where(distance < 8, distance, far_bucket)
    return bucket + jnp.where(relative > 0, 16, 0)


def bias_lookup(relative, rel_bias):
    buckets = bucket_of(relative)
    marks = jnp.arange(rel_bias.shape[0], dtype=jnp.int32)
    one_hot = (buckets[:, :, None] == marks[None, None, :]).astype(jnp.float32)
    return jnp.einsum(
        "qkb,bh->hqk",
        one_hot,
        rel_bias,
        precision=lax.Precision.HIGHEST,
        preferred_element_type=jnp.float32,
    )


def norm_rows(values_in, gain):
    widened = values_in.astype(jnp.float32)
    scale = lax.rsqrt(jnp.mean(widened * widened, axis=-1, keepdims=True) + epsilon)
    return (widened * scale * gain).astype(jnp.bfloat16)


def layout(lengths_row, prefix_row, row_ids):
    req_ends = jnp.cumsum(lengths_row)
    req_starts = req_ends - lengths_row
    member = (
        (row_ids[:, None] >= req_starts[None, :]) & (row_ids[:, None] < req_ends[None, :])
    ).astype(jnp.int32)
    numbers = jnp.arange(lengths_row.shape[0], dtype=jnp.int32)
    req_index = jnp.sum(member * numbers[None, :], axis=1) + jnp.sum(member, axis=1) - 1
    offset = row_ids - jnp.sum(member * req_starts[None, :], axis=1)
    chosen = jnp.sum(member * prefix_row[None, :], axis=1)
    return (req_index, offset, chosen)


def softmax_part(scores, value_rows, allowed):
    scores = jnp.where(allowed[None], scores, masked_score)
    row_max = jnp.max(scores, axis=2)
    exp_terms = jnp.where(allowed[None], jnp.exp(scores - row_max[:, :, None]), 0.0)
    row_sum = jnp.sum(exp_terms, axis=2)
    weighted = jnp.einsum(
        "hqk,khd->hqd",
        exp_terms.astype(jnp.bfloat16),
        value_rows,
        preferred_element_type=jnp.float32,
    )
    return (row_max, row_sum, weighted)


def combine(first_part, second_part):
    row_max = jnp.maximum(first_part[0], second_part[0])
    scale_one = jnp.exp(first_part[0] - row_max)
    scale_two = jnp.exp(second_part[0] - row_max)
    row_sum = first_part[1] * scale_one + second_part[1] * scale_two
    weighted = first_part[2] * scale_one[:, :, None] + second_part[2] * scale_two[:, :, None]
    return (row_max, row_sum, weighted)


def feed_forward(rows_in, in_part, out_part):
    units = lax.dot_general(
        rows_in, in_part, (((1,), (1,)), ((), ())), preferred_element_type=jnp.float32
    )
    units = jnp.maximum(units, 0.0).astype(jnp.bfloat16)
    return jnp.dot(units, out_part, preferred_element_type=jnp.float32)


def body(
    tokens,
    attn_gain,
    w_query,
    w_key,
    w_value,
    w_attn_out,
    rel_bias,
    prefix_cache,
    lengths,
    prefix_map,
    mlp_gain,
    w_in,
    w_out,
):
    rows_here = tokens.shape[0]
    device_pos = lax.axis_index("req")
    group_lengths = lengths[0]
    group_map = prefix_map[0]
    normed = norm_rows(tokens, attn_gain)
    query = (
        jnp.dot(normed, w_query, preferred_element_type=jnp.float32)
        .astype(jnp.bfloat16)
        .reshape(rows_here, H, DK)
    )
    key_value = jnp.concatenate(
        [
            jnp.dot(normed, w_key, preferred_element_type=jnp.float32).astype(jnp.bfloat16),
            jnp.dot(normed, w_value, preferred_element_type=jnp.float32).astype(jnp.bfloat16),
        ],
        axis=1,
    )
    query_ids = device_pos * rows_here + jnp.arange(rows_here, dtype=jnp.int32)
    query_req, query_offset, query_prefix = layout(group_lengths, group_map, query_ids)
    all_positions = jnp.arange(PLEN, dtype=jnp.int32)
    prefix_bias = bias_lookup(all_positions[None, :] - PLEN - query_offset[:, None], rel_bias)
    empty_state = (
        jnp.full((H, rows_here), masked_score, jnp.float32),
        jnp.zeros((H, rows_here), jnp.float32),
        jnp.zeros((H, rows_here, DK), jnp.float32),
    )
    running = empty_state
    shard_kv = lax.all_gather(prefix_cache, "req", axis=1, tiled=True)
    prefix_ids = jnp.arange(PREF_GRP, dtype=jnp.int32)
    slices = shard_kv.shape[0]
    piece_len = shard_kv.shape[1]
    step_len = max(min(piece_len, 512 // slices), 1)
    for begin in range(0, piece_len, step_len):
        width = min(step_len, piece_len - begin)
        block = shard_kv[:, begin : begin + width]
        key_rows = block[:, :, :D].reshape(slices, width, H, DK)
        value_rows = block[:, :, D:].reshape(-1, H, DK)
        rel_terms = lax.dynamic_slice_in_dim(prefix_bias, begin, width, 2)
        prefix_scores = jnp.einsum(
            "qhd,swhd->hqsw", query, key_rows, preferred_element_type=jnp.float32
        )
        prefix_scores = (prefix_scores + rel_terms[:, :, None, :]).reshape(
            H, rows_here, slices * width
        )
        allowed = jnp.repeat(query_prefix[:, None] == prefix_ids[None, :], width, axis=1)
        running = combine(running, softmax_part(prefix_scores, value_rows, allowed))
    state = running
    window = padded(key_value, (("req", 0),), rows_here)
    window_ids = device_pos * rows_here - rows_here + jnp.arange(3 * rows_here, dtype=jnp.int32)
    window_req = layout(group_lengths, group_map, window_ids)[0]
    for part_idx in range(3):
        part_rows = window[part_idx * rows_here : (part_idx + 1) * rows_here]
        part_ids = window_ids[part_idx * rows_here : (part_idx + 1) * rows_here]
        part_req = window_req[part_idx * rows_here : (part_idx + 1) * rows_here]
        suffix_terms = bias_lookup(part_ids[None, :] - query_ids[:, None], rel_bias)
        suffix_allowed = part_req[None, :] == query_req[:, None]
        scores = (
            jnp.einsum(
                "qhd,khd->hqk",
                query,
                part_rows[:, :D].reshape(-1, H, DK),
                preferred_element_type=jnp.float32,
            )
            + suffix_terms
        )
        suffix_state = softmax_part(scores, part_rows[:, D:].reshape(-1, H, DK), suffix_allowed)
        state = combine(state, suffix_state)
    attended = (
        (state[2] / state[1][:, :, None])
        .transpose(1, 0, 2)
        .reshape(rows_here, D)
        .astype(jnp.bfloat16)
    )
    hidden_one = (
        tokens.astype(jnp.float32)
        + jnp.dot(attended, w_attn_out, preferred_element_type=jnp.float32)
    ).astype(jnp.bfloat16)
    normed_two = norm_rows(hidden_one, mlp_gain)
    gathered = lax.all_gather(normed_two, "grp", axis=0, tiled=True)
    mlp_total = lax.psum_scatter(
        feed_forward(gathered, w_in, w_out).astype(jnp.bfloat16),
        "grp",
        scatter_dimension=0,
        tiled=True,
    ).astype(jnp.float32)
    return (hidden_one.astype(jnp.float32) + mlp_total).astype(jnp.bfloat16)


def bucket_steps():
    return tuple((i, i) for i in range(1, 9)) + tuple((t, 9 + i) for i, t in enumerate(far_marks))


def chain(distance, table, head, first):
    value = jnp.full(distance.shape, table[head, first], jnp.float32)
    for threshold, number in bucket_steps():
        value = jnp.where(distance >= threshold, table[head, first + number], value)
    return value


def layer_kernel(
    n_req,
    tokens_hbm,
    attn_gain,
    wq_hbm,
    wk_hbm,
    wv_hbm,
    wo_hbm,
    rel_bias,
    cache_hbm,
    lengths,
    prefix_map,
    mlp_gain,
    win_hbm,
    wout_hbm,
    out_ref,
    tok,
    w_attn,
    w_in,
    w_out,
    normed,
    stage,
    k_cache,
    v_cache,
    q_all,
    k_side,
    k_all,
    v_all,
    k_cross,
    w_up,
    tail_bias,
    near_bias,
    key_req,
    row_facts,
    row_code,
    row_max,
    row_sum,
    row_acc,
    o_send,
    att,
    h_one,
    n_two,
    units,
    part_own,
    part_far,
    fast_out,
    fast_in,
    chip_out,
    chip_in,
    far_out,
    far_in,
    load_sem,
    own_sem,
    kc_send,
    kc_recv,
    vc_send,
    vc_recv,
    q_send,
    q_recv,
    k_send,
    k_recv,
    v_send,
    v_recv,
    o_ssem,
    o_rsem,
    f_send,
    f_recv,
):
    me = lax.axis_index("req")
    grp = lax.axis_index("grp")
    side = lax.rem(grp, 2)
    plane = lax.div(grp, 2)
    mate = plane * 2 + (1 - side)
    across = (1 - plane) * 2 + side
    rows = tokens_hbm.shape[0]
    piece = cache_hbm.shape[1]
    half = rows // 2

    def remote(src, dst, ssem, rsem, **where):
        return pltpu.make_async_remote_copy(
            src_ref=src, dst_ref=dst, send_sem=ssem, recv_sem=rsem, device_id=where, device_id_type=MESH
        )

    def lanes_of(index):
        return pl.ds(pl.multiple_of(index * LANES, LANES), LANES)

    def rows_of(index):
        return pl.ds(pl.multiple_of(index * rows, rows), rows)

    loads = [
        pltpu.make_async_copy(src, dst, load_sem.at[i])
        for i, (src, dst) in enumerate(
            [
                (tokens_hbm, tok),
                (wq_hbm, w_attn.at[0]),
                (wk_hbm, w_attn.at[1]),
                (wv_hbm, w_attn.at[2]),
                (wo_hbm, w_attn.at[3]),
                (win_hbm, w_in),
                (wout_hbm, w_out),
            ]
        )
    ]
    for load in loads[:4]:
        load.start()

    barrier = pltpu.get_barrier_semaphore()
    for d in range(1, n_req):
        pl.semaphore_signal(
            barrier, inc=1, device_id={"req": lax.rem(me + d, n_req)}, device_id_type=MESH
        )
    for other in (mate, across):
        pl.semaphore_signal(barrier, inc=1, device_id={"grp": other}, device_id_type=MESH)
    pl.semaphore_wait(barrier, n_req + 1)

    def cache_copy(buf, first, sends, recvs, d, peer, owner):
        return remote(
            cache_hbm.at[:, :, pl.ds(pl.multiple_of(first + peer * LANES, LANES), LANES)],
            buf.at[:, pl.ds(pl.multiple_of(owner * piece, piece), piece), :],
            sends.at[d],
            recvs.at[d],
            req=peer,
        )

    def q_copy(d, peer, owner):
        return remote(
            stage.at[0, :, lanes_of(peer)], q_all.at[rows_of(owner), :], q_send.at[d], q_recv.at[d], req=peer
        )

    def k_copy(d, peer, owner):
        return remote(
            k_side.at[lanes_of(peer), :], k_all.at[:, lanes_of(owner + 1)], k_send.at[d], k_recv.at[d], req=peer
        )

    def v_copy(d, peer, owner):
        return remote(
            stage.at[1, :, lanes_of(peer)], v_all.at[rows_of(owner + 1), :], v_send.at[d], v_recv.at[d], req=peer
        )

    parts = [pl.ds(r * half, half) for r in range(2)]

    def o_copy(r):
        def make(d, peer, owner):
            return remote(
                o_send.at[peer, parts[r]],
                att.at[parts[r], lanes_of(owner)],
                o_ssem.at[r, d],
                o_rsem.at[r, d],
                req=peer,
            )

        return make

    def outgoing(make):
        return [make(d, lax.rem(me + d, n_req), me) for d in range(1, n_req)]

    def incoming(make):
        return [
            make(d, lax.rem(me + d, n_req), lax.rem(me + n_req - d, n_req)) for d in range(1, n_req)
        ]

    def kc_copy(d, peer, owner):
        return cache_copy(k_cache, 0, kc_send, kc_recv, d, peer, owner)

    def vc_copy(d, peer, owner):
        return cache_copy(v_cache, D, vc_send, vc_recv, d, peer, owner)

    for copy in outgoing(kc_copy) + outgoing(vc_copy):
        copy.start()
    own_copies = [
        pltpu.make_async_copy(
            cache_hbm.at[:, :, pl.ds(pl.multiple_of(first + me * LANES, LANES), LANES)],
            buf.at[:, pl.ds(pl.multiple_of(me * piece, piece), piece), :],
            own_sem.at[i],
        )
        for i, (buf, first) in enumerate([(k_cache, 0), (v_cache, D)])
    ]
    for copy in own_copies:
        copy.start()

    loads[0].wait()
    wide = tok[...].astype(jnp.float32)
    scale = lax.rsqrt(jnp.mean(wide * wide, axis=-1, keepdims=True) + epsilon)
    normed[...] = (wide * scale * attn_gain[...]).astype(jnp.bfloat16)

    tile = 1024
    turn_tile = 512
    makers = (q_copy, k_copy, v_copy)
    for part in range(3):
        loads[1 + part].wait()

        @pl.loop(0, D // tile)
        def _(t, part=part):
            cols = pl.ds(pl.multiple_of(t * tile, tile), tile)
            made = jnp.dot(
                normed[...], w_attn[part, :, cols], preferred_element_type=jnp.float32
            ).astype(jnp.bfloat16)
            if part == 1:
                k_side[cols, :] = made.T
            else:
                stage[part // 2, :, cols] = made

        for copy in outgoing(makers[part]):
            copy.start()
        if part == 0:
            for load in loads[4:]:
                load.start()
    q_all[rows_of(me), :] = stage[0, :, lanes_of(me)]
    k_all[:, lanes_of(me + 1)] = k_side[lanes_of(me), :]
    v_all[rows_of(me + 1), :] = stage[1, :, lanes_of(me)]
    zeros = jnp.zeros((rows, LANES), jnp.bfloat16)
    for outer in (0, n_req + 1):
        k_all[:, pl.ds(outer * rows, rows)] = zeros
        v_all[pl.ds(outer * rows, rows), :] = zeros

    ends = []
    total = 0
    n_requests = lengths.shape[1]
    for j in range(n_requests):
        total = total + lengths[0, j]
        ends.append(total)
    key_ids = lax.broadcasted_iota(jnp.int32, key_req.shape, 1) - rows
    key_number = jnp.where(key_ids < 0, -1, 0)
    for end in ends:
        key_number = key_number + jnp.where(key_ids >= end, 1, 0)
    key_req[...] = key_number

    def stacked(r, head):
        return pl.ds((2 * r + head) * half, half)

    row_iota = lax.broadcasted_iota(jnp.int32, (rows, LANES), 0)
    lane_iota = lax.broadcasted_iota(jnp.int32, (rows, LANES), 1)
    ids = lax.broadcasted_iota(jnp.int32, row_facts.shape, 0) * rows + lax.broadcasted_iota(
        jnp.int32, row_facts.shape, 1
    )
    number = jnp.zeros_like(ids)
    start = jnp.zeros_like(ids)
    prefix = jnp.full(ids.shape, prefix_map[0, 0], jnp.int32)
    for j in range(n_requests):
        past = ids >= ends[j]
        number = number + jnp.where(past, 1, 0)
        start = start + jnp.where(past, lengths[0, j], 0)
        if j + 1 < n_requests:
            prefix = jnp.where(past, prefix_map[0, j + 1], prefix)
    row_facts[...] = ((start * 2 + prefix) * 1024 + number).astype(jnp.float32)

    def bias_of(distance, head, first):
        return chain(distance, rel_bias, 2 * me + head, first) - rel_bias[2 * me + head, 15]

    @pl.loop(0, n_req)
    def _(b):
        code = jnp.broadcast_to(row_facts[pl.ds(b, 1), :], (rows, LANES)).T.astype(jnp.int32)
        row_code[b] = code
        distance = LANES + row_iota + b * rows - (code >> 11) - lane_iota
        for head in range(2):
            terms = bias_of(distance, head, 0)
            for r in range(2):
                tail_bias[b, stacked(r, head), :] = terms[r * half : (r + 1) * half]

    first_head = lane_iota < DK

    def query_heads(b, r):
        q = q_all[pl.ds(pl.multiple_of(b * rows + r * half, half), half), :]
        nothing = jnp.zeros_like(q)
        first = first_head[:half]
        return jnp.concatenate(
            [jnp.where(first, q, nothing), jnp.where(first, nothing, q)], axis=0
        )

    for copy in own_copies:
        copy.wait()
    for copy in incoming(kc_copy):
        copy.wait_recv()
    for which in range(PREF_GRP):
        k_cross[pl.ds(which * LANES, LANES), :] = k_cache[which].T
    for make in (q_copy, vc_copy):
        for copy in incoming(make):
            copy.wait_recv()

    far_keys = PLEN - LANES

    def far_scores(b):
        qh = jnp.concatenate([query_heads(b, 0), query_heads(b, 1)], axis=0)
        choice = row_code[b] & 1024
        zero_first = (
            jnp.concatenate([choice[:half], choice[:half], choice[half:], choice[half:]], axis=0) == 0
        )
        nothing = jnp.zeros_like(qh)
        q2 = jnp.concatenate(
            [jnp.where(zero_first, qh, nothing), jnp.where(zero_first, nothing, qh)], axis=1
        )
        scores = jnp.dot(q2, k_cross[...], preferred_element_type=jnp.float32)
        scores = jnp.concatenate(
            [scores[:, :far_keys], scores[:, far_keys:] + tail_bias[b]], axis=1
        )
        return zero_first, scores

    def far_terms(scores):
        top = jnp.max(scores, axis=1, keepdims=True)
        terms = jnp.exp(scores - top)
        return top, jnp.sum(terms, axis=1, keepdims=True), terms.astype(jnp.bfloat16)

    far_step = 2

    @pl.loop(0, n_req // far_step)
    def _(step):
        blocks = [step * far_step + i for i in range(far_step)]
        values = jnp.concatenate([v_cache[0], v_cache[1]], axis=1)
        scored = [far_scores(b) for b in blocks]
        termed = [far_terms(scores) for _, scores in scored]
        accs = [jnp.dot(t[2], values, preferred_element_type=jnp.float32) for t in termed]
        for b, (zero_first, _), (top, total, _), acc in zip(blocks, scored, termed, accs):
            row_max[b] = jnp.broadcast_to(top, (2 * rows, LANES))
            row_sum[b] = jnp.broadcast_to(total, (2 * rows, LANES))
            row_acc[b] = jnp.where(zero_first, acc[:, :LANES], acc[:, LANES:])

    for head in range(2):
        for part in range(3):
            ahead = lane_iota + (part - 1) * rows - row_iota
            distance = jnp.abs(ahead)
            if part == 0:
                both = bias_of(distance, head, 0)
            elif part == 2:
                both = bias_of(distance, head, 16)
            else:
                both = jnp.where(ahead > 0, bias_of(distance, head, 16), bias_of(distance, head, 0))
            for r in range(2):
                near_bias[0, stacked(r, head), pl.ds(part * LANES, LANES)] = both[r * half : (r + 1) * half]

    @pl.loop(0, n_req)
    def _(step):
        b = n_req - 1 - step
        number = row_code[b] & 1023
        for part in range(3):
            other = key_req[pl.ds(0, 1), pl.ds(pl.multiple_of(b * rows + part * LANES, LANES), LANES)]
            same = other == number
            cols = pl.ds(part * LANES, LANES)
            for r in range(2):
                same_half = same[r * half : (r + 1) * half]
                for head in range(2):
                    near_bias[b, stacked(r, head), cols] = jnp.where(
                        same_half, near_bias[0, stacked(r, head), cols], masked_score
                    )

    for make in (k_copy, v_copy):
        for copy in incoming(make):
            copy.wait_recv()

    def near(blocks, r):
        here = pl.ds(r * rows, rows)
        windows = [pl.ds(pl.multiple_of(b * rows, rows), 3 * rows) for b in blocks]
        scores = [
            jnp.dot(query_heads(b, r), k_all[:, w], preferred_element_type=jnp.float32)
            + near_bias[b, here, :]
            for b, w in zip(blocks, windows)
        ]
        olds = [row_max[b, here, :] for b in blocks]
        tops = [jnp.maximum(o, jnp.max(x, axis=1, keepdims=True)) for o, x in zip(olds, scores)]
        terms = [jnp.exp(x - jnp.concatenate([t, t, t], axis=1)) for x, t in zip(scores, tops)]
        shrinks = [jnp.exp(o - t) for o, t in zip(olds, tops)]
        sums = [
            row_sum[b, here, :] * z + jnp.sum(x, axis=1, keepdims=True)
            for b, z, x in zip(blocks, shrinks, terms)
        ]
        accs = [
            row_acc[b, here, :] * z
            + jnp.dot(x.astype(jnp.bfloat16), v_all[w, :], preferred_element_type=jnp.float32)
            for b, z, x, w in zip(blocks, shrinks, terms, windows)
        ]
        results = [a / x for a, x in zip(accs, sums)]
        return [jnp.where(first_head[:half], x[:half], x[half:]).astype(jnp.bfloat16) for x in results]

    near_step = 4
    for r in range(2):
        for begin in range(1, n_req + 1, near_step):
            turns = range(begin, begin + near_step)
            blocks = [lax.rem(me + d, n_req) for d in turns]
            for d, b, result in zip(turns, blocks, near(blocks, r)):
                if d < n_req:
                    o_send[b, parts[r], :] = result
                else:
                    att[parts[r], lanes_of(me)] = result
            for d, b in zip(turns, blocks):
                if d < n_req:
                    o_copy(r)(d, b, me).start()

    mine = [
        remote(n_two.at[0, parts[r]], n_two.at[1, parts[r]], f_send.at[10 + r], f_recv.at[10 + r], grp=mate)
        for r in range(2)
    ]
    cross = [
        remote(n_two.at[0, parts[r]], n_two.at[2, parts[r]], f_send.at[1 + r], f_recv.at[1 + r], grp=across)
        for r in range(2)
    ]
    relay = [
        remote(n_two.at[2, parts[r]], n_two.at[3, parts[r]], f_send.at[3 + r], f_recv.at[3 + r], grp=mate)
        for r in range(2)
    ]
    back = remote(fast_out, fast_in, f_send.at[5], f_recv.at[5], grp=mate)
    swap = [
        remote(chip_out.at[r], chip_in.at[r], f_send.at[6 + r], f_recv.at[6 + r], grp=mate) for r in range(2)
    ]
    home = [
        remote(far_out.at[r], far_in.at[r], f_send.at[8 + r], f_recv.at[8 + r], grp=across) for r in range(2)
    ]

    loads[5].wait()

    @pl.loop(0, w_in.shape[0] // turn_tile)
    def _(t):
        cols = pl.ds(pl.multiple_of(t * turn_tile, turn_tile), turn_tile)
        w_up[:, cols] = w_in[cols, :].T

    loads[4].wait()
    for r in range(2):
        for copy in incoming(o_copy(r)):
            copy.wait_recv()

        @pl.loop(0, D // tile)
        def _(t, r=r):
            cols = pl.ds(pl.multiple_of(t * tile, tile), tile)
            h_one[parts[r], cols] = (
                tok[parts[r], cols].astype(jnp.float32)
                + jnp.dot(
                    att[parts[r], :], w_attn[3, :, cols], preferred_element_type=jnp.float32
                )
            ).astype(jnp.bfloat16)

        wide = h_one[parts[r], :].astype(jnp.float32)
        scale = lax.rsqrt(jnp.mean(wide * wide, axis=-1, keepdims=True) + epsilon)
        n_two[0, parts[r], :] = (wide * scale * mlp_gain[...]).astype(jnp.bfloat16)
        cross[r].start()
        mine[r].start()

    loads[6].wait()

    def up(rows_in):
        @pl.loop(0, w_in.shape[0] // tile)
        def _(t):
            cols = pl.ds(pl.multiple_of(t * tile, tile), tile)
            units[:, cols] = jnp.maximum(
                jnp.dot(rows_in, w_up[:, cols], preferred_element_type=jnp.float32), 0.0
            ).astype(jnp.bfloat16)

    def down(out):
        @pl.loop(0, D // tile)
        def _(t):
            cols = pl.ds(pl.multiple_of(t * tile, tile), tile)
            out[:, cols] = jnp.dot(
                units[...], w_out[:, cols], preferred_element_type=jnp.float32
            ).astype(out.dtype)

    def far_rows(r):
        return jnp.concatenate([n_two[2, parts[r]], n_two[3, parts[r]]], axis=0)

    def send_home(r):
        swap[r].wait_recv()
        far_out[r] = (part_far[r, pl.ds(0, half), :] + chip_in[r].astype(jnp.float32)).astype(jnp.bfloat16)
        home[r].start()

    def finish_far(r):
        down(part_far.at[r])
        chip_out[r] = part_far[r, pl.ds(half, half), :].astype(jnp.bfloat16)
        swap[r].start()

    up(n_two[0])
    cross[0].wait_recv()
    relay[0].start()
    down(part_own)
    for copy in mine:
        copy.wait_recv()
    up(n_two[1])
    down(fast_out)
    back.start()
    cross[1].wait_recv()
    relay[1].start()
    relay[0].wait_recv()
    up(far_rows(0))
    finish_far(0)
    relay[1].wait_recv()
    up(far_rows(1))
    send_home(0)
    finish_far(1)
    back.wait_recv()
    part_own[...] = (
        part_own[...] + h_one[...].astype(jnp.float32) + fast_in[...].astype(jnp.float32)
    )
    send_home(1)
    for r in range(2):
        home[r].wait_recv()
        out_ref[parts[r], :] = (
            part_own[parts[r], :] + far_in[r].astype(jnp.float32)
        ).astype(jnp.bfloat16)

    for make in (kc_copy, vc_copy, q_copy, k_copy, v_copy, o_copy(0), o_copy(1)):
        for copy in outgoing(make):
            copy.wait_send()
    for copy in [back] + mine + cross + relay + swap + home:
        copy.wait_send()


def fused(
    tokens,
    attn_gain,
    w_query,
    w_key,
    w_value,
    w_attn_out,
    rel_bias,
    prefix_cache,
    lengths,
    prefix_map,
    mlp_gain,
    w_in,
    w_out,
):
    n_req = lax.axis_size("req")
    rows = tokens.shape[0]
    group = n_req * rows
    hbm = pl.BlockSpec(memory_space=pl.ANY)
    vmem = pl.BlockSpec(memory_space=pltpu.VMEM)
    smem = pl.BlockSpec(memory_space=pltpu.SMEM)
    half = rows // 2
    bf16, f32 = jnp.bfloat16, jnp.float32
    sems = pltpu.SemaphoreType.DMA
    return pl.pallas_call(
        functools.partial(layer_kernel, n_req),
        out_shape=jax.ShapeDtypeStruct((rows, D), bf16),
        in_specs=[hbm, vmem, hbm, hbm, hbm, hbm, smem, hbm, smem, smem, vmem, hbm, hbm],
        out_specs=vmem,
        scratch_shapes=[
            pltpu.VMEM((rows, D), bf16),
            pltpu.VMEM((4, D, D), bf16),
            pltpu.VMEM(w_in.shape, bf16),
            pltpu.VMEM(w_out.shape, bf16),
            pltpu.VMEM((rows, D), bf16),
            pltpu.VMEM((2, rows, D), bf16),
            pltpu.VMEM((PREF_GRP, PLEN, LANES), bf16),
            pltpu.VMEM((PREF_GRP, PLEN, LANES), bf16),
            pltpu.VMEM((group, LANES), bf16),
            pltpu.VMEM((D, rows), bf16),
            pltpu.VMEM((LANES, group + 2 * rows), bf16),
            pltpu.VMEM((group + 2 * rows, LANES), bf16),
            pltpu.VMEM((PREF_GRP * LANES, PLEN), bf16),
            pltpu.VMEM(w_in.shape[::-1], bf16),
            pltpu.VMEM((n_req, 2 * rows, LANES), f32),
            pltpu.VMEM((n_req, 2 * rows, 3 * LANES), f32),
            pltpu.VMEM((8, group + 2 * rows), jnp.int32),
            pltpu.VMEM((n_req, LANES), f32),
            pltpu.VMEM((n_req, rows, LANES), jnp.int32),
            pltpu.VMEM((n_req, 2 * rows, LANES), f32),
            pltpu.VMEM((n_req, 2 * rows, LANES), f32),
            pltpu.VMEM((n_req, 2 * rows, LANES), f32),
            pltpu.VMEM((n_req, rows, LANES), bf16),
            pltpu.VMEM((rows, D), bf16),
            pltpu.VMEM((rows, D), bf16),
            pltpu.VMEM((4, rows, D), bf16),
            pltpu.VMEM((rows, w_in.shape[0]), bf16),
            pltpu.VMEM((rows, D), f32),
            pltpu.VMEM((2, rows, D), f32),
            pltpu.VMEM((rows, D), bf16),
            pltpu.VMEM((rows, D), bf16),
            pltpu.VMEM((2, half, D), bf16),
            pltpu.VMEM((2, half, D), bf16),
            pltpu.VMEM((2, half, D), bf16),
            pltpu.VMEM((2, half, D), bf16),
            sems((7,)),
            sems((2,)),
        ]
        + [sems((n_req,)) for _ in range(10)]
        + [sems((2, n_req)) for _ in range(2)]
        + [sems((12,)), sems((12,))],
        compiler_params=pltpu.CompilerParams(
            collective_id=0, has_side_effects=True, vmem_limit_bytes=63 * 1024 * 1024
        ),
    )(
        tokens,
        attn_gain.reshape(1, D),
        w_query,
        w_key,
        w_value,
        w_attn_out,
        rel_bias.T,
        prefix_cache,
        lengths,
        prefix_map,
        mlp_gain.reshape(1, D),
        w_in,
        w_out,
    )


def pairs_fit(mesh):
    return mesh.shape["req"] * LANES == D and mesh.shape["grp"] == 4


def solution(mesh):
    return jax.shard_map(
        fused if pairs_fit(mesh) else body,
        mesh=mesh,
        in_specs=(
            P(("grp", "req"), None),
            P(),
            P(),
            P(),
            P(),
            P(),
            P(),
            P("grp", "req", None),
            P("grp", None),
            P("grp", None),
            P(),
            P("grp", None),
            P("grp", None),
        ),
        out_specs=P(("grp", "req"), None),
        check_vma=False,
    )
```
